32 devices in a mesh: cuts: 4 (over y, x), blk: 8 (over z, core).
Axes of the slice: x: 2, y: 2, z: 4, core: 2. Of those that a mesh axis runs over, the one named last changes fastest.
Arguments:
- gap_load: float32 [4, 16, 2, 256, 128], P('cuts', 'blk'), may hold values from -24 to 24
- offsets: int32 [4, 16, 2], P('cuts', 'blk'), may hold values from -1 to 255, as said below
- corner_map: int32 [4, 16, 4], P('cuts', 'blk'), may hold values from -1 to 63, as said below
- flexibility: float32 [4, 16, 1024, 1024], P('cuts', 'blk'), may hold values from -0.5 to 4.5, as said below
- coupling: float32 [4, 16, 12, 1024], P('cuts', 'blk'), may hold values from -1.25 to 1.25
- corner_rows: float32 [4, 16, 12, 192], P('cuts', 'blk'), may hold values from -0.1 to 1.1, as said below
Outputs:
- multipliers: float32 [4, 16, 2, 256, 128], P('cuts', 'blk')
- residual: float32 [4, 16, 2, 256, 128], P('cuts', 'blk')
The draws below stay inside these ranges and needn't reach their ends.
Inputs may be any that keep to these rules, and one draw needn't show every extreme that they name: `offsets`: on an interface owned by a subdomain, the neighbour's dof k matches the owner's dof (k + offset) mod 256; -1 marks an interface without multipliers: the tunnel's far end, or one that touches an excavated subdomain. `corner_map`: entries k = 0, 1, 2, 3 are the corners at near-left, near-right, far-left, far-right. Entry 2 of subdomain (r, c) is never -1, and every node is entry 2 of exactly one subdomain; the same node is entry 3 of (r, (c - 1) mod 16) and, for r + 1 < 4, entries 0 of (r + 1, c) and 1 of (r + 1, (c - 1) mod 16), and no other entry. -1 marks a clamped corner at the tunnel's near end. `flexibility`: each block is symmetric positive definite. `corner_rows`: row 3 k + j of a subdomain is row 3 m + j of one symmetric positive definite matrix of order 3 * 64, with m = corner_map entry k; zero rows where that entry is -1.
All inputs are finite; a program needn't handle non-finite values.
Results may differ from the reference program's by a relative error of at most 0.00021.
Values sent between devices are 32-bit elements; how exact they have to be, the bound alone decides.
No kernel may reach another device: no remote copies, remote signals or barrier semaphores. Data moves between devices by JAX's collectives and lax.ppermute only.
A program may use at most 64 MiB of HBM per device.

```python
import math
import jax
import jax.numpy as jnp
from jax import lax

FD = 256
NI = 1024
NRHS = 128
ITERS = 3
CYCLES = 4
NCIRC = 16
NCORN = 64


def corner_numbers(key):
    ordering = jax.random.permutation(jax.random.fold_in(key, 11), NCORN).astype(jnp.int32)
    nodes = jnp.concatenate([jnp.full((1, NCIRC), -1, jnp.int32), ordering.reshape(CYCLES, NCIRC)], axis=0)
    nearer = nodes[:-1]
    farther = nodes[1:]
    return jnp.stack([nearer, jnp.roll(nearer, -1, axis=1), farther, jnp.roll(farther, -1, axis=1)], axis=-1).astype(jnp.int32)


def symmetric_part(key, order_size):
    spread = 0.45 / math.sqrt(order_size)
    uniform_draw = jax.random.uniform(key, (order_size, order_size), jnp.float32, -spread, spread)
    return (uniform_draw + uniform_draw.T) * 0.7071067811865476


def draw_corner_map(key, part):
    return corner_numbers(key)


def draw_corner_rows(key, part):
    numbers = corner_numbers(key)
    dof_count = 3 * NCORN
    matrix = jnp.eye(dof_count, dtype=jnp.float32) + symmetric_part(jax.random.fold_in(key, 12), dof_count)
    spread = 3 * jnp.maximum(numbers, 0)[..., None] + jnp.arange(3, dtype=jnp.int32)
    spread = spread.reshape(CYCLES, NCIRC, 12)
    picked = matrix[spread]
    keep = jnp.repeat(numbers >= 0, 3, axis=-1)[..., None]
    return jnp.where(keep, picked, 0.0).astype(jnp.float32)


def draw_flexibility(key, part):

    def one_block(sub_key):
        base = jnp.eye(NI, dtype=jnp.float32) + symmetric_part(jax.random.fold_in(sub_key, 1), NI)
        scales = jnp.exp(jax.random.uniform(jax.random.fold_in(sub_key, 2), (NI,), jnp.float32, math.log(0.7), math.log(1.4)))
        return scales[:, None] * base * scales[None, :]
    sub_keys = jax.random.split(key, CYCLES * NCIRC)
    return lax.map(one_block, sub_keys).reshape(CYCLES, NCIRC, NI, NI)


def draw_offsets(key, part):
    cycle_index = jnp.arange(CYCLES)[:, None]
    excavated = (jax.random.randint(jax.random.fold_in(key, 21), (CYCLES, NCIRC), 0, 8) == 0) & (cycle_index > 0)
    excavated_next = jnp.concatenate([excavated[1:], jnp.ones((1, NCIRC), jnp.bool_)], axis=0)
    far_open = ~excavated & ~excavated_next
    right_open = ~excavated & ~jnp.roll(excavated, -1, axis=1)
    values = jax.random.permutation(jax.random.fold_in(key, 22), 2 * CYCLES * NCIRC) % FD
    values = values.astype(jnp.int32).reshape(CYCLES, NCIRC, 2)
    values = values.at[0, 0, 1].set(FD - 1)
    return jnp.where(jnp.stack([far_open, right_open], axis=-1), values, -1).astype(jnp.int32)


def draw_gap_load(key, part):
    shape = (CYCLES, NCIRC, 2, FD, NRHS)
    cycle_pos = jnp.arange(CYCLES, dtype=jnp.float32) / CYCLES
    circ_pos = jnp.arange(NCIRC, dtype=jnp.float32) / NCIRC
    factor = 1.0 + cycle_pos[:, None] + circ_pos[None, :]
    base = jnp.clip(jax.random.normal(key, shape, jnp.float32), -6.0, 6.0)
    return base * factor[:, :, None, None, None]


def steps_of(own_key, extent, cuts, low, largest):
    def one(axis_at, blocks):
        draws = jax.random.uniform(jax.random.fold_in(jax.random.fold_in(own_key, 6), axis_at), (blocks,), jnp.float32, low / len(cuts), largest / len(cuts))
        return jnp.repeat(jnp.exp(draws), extent[axis_at] // blocks).reshape((-1,) + (1,) * (len(extent) - axis_at - 1))

    gain = one(*cuts[0])
    for cut in cuts[1:]:
        gain = gain * one(*cut)
    return gain


def noise(stream_key, extent, deviation, limit, cuts=(), kind=jnp.bfloat16):
    array = deviation * jax.random.normal(stream_key, extent, jnp.float32)
    if cuts:
        array = array * steps_of(stream_key, extent, cuts, -0.22, 0.18)
    return jnp.clip(array, -limit, limit).astype(kind)


def setup_inputs(seed: int = 0) -> dict:
    streams_of = jax.random.split(jax.random.key(seed), 7)
    gap_load = draw_gap_load(jax.random.fold_in(streams_of[6], 71), 0)
    offsets = draw_offsets(jax.random.fold_in(streams_of[6], 71), 0)
    corner_map = draw_corner_map(jax.random.fold_in(streams_of[6], 71), 0)
    flexibility = draw_flexibility(jax.random.fold_in(streams_of[6], 71), 0)
    coupling = noise(streams_of[4], (CYCLES, NCIRC, 12, NI), 0.08, 1.25, ((0, 4), (1, 8)), jnp.float32)
    corner_rows = draw_corner_rows(jax.random.fold_in(streams_of[6], 71), 0)
    return dict(gap_load=gap_load, offsets=offsets, corner_map=corner_map, flexibility=flexibility, coupling=coupling, corner_rows=corner_rows)


HIGH = lax.Precision.HIGHEST


def rotate(values, amounts, orient):
    face_size = values.shape[-2]
    indices = (jnp.arange(face_size, dtype=jnp.int32) + orient * amounts[..., None]) % face_size
    return jnp.take_along_axis(values, indices[..., None].astype(jnp.int32), axis=-2)


def corner_indices(corner_map, dof_count):
    spread = 3 * corner_map[..., None] + jnp.arange(3, dtype=jnp.int32)
    spread = jnp.where(corner_map[..., None] >= 0, spread, dof_count)
    return spread.reshape(corner_map.shape[0], corner_map.shape[1], 12).astype(jnp.int32)


def operator(direction, offsets, flexibility, coupling, corner_rows, corner_dofs):
    cycle_count, circ_count, _, face_size, load_count = direction.shape
    sent_far = -rotate(direction[:, :, 0], offsets[:, :, 0], 1)
    sent_right = -rotate(direction[:, :, 1], offsets[:, :, 1], 1)
    nearside = jnp.concatenate([jnp.zeros_like(sent_far[:1]), sent_far[:-1]], axis=0)
    leftside = jnp.roll(sent_right, 1, axis=1)
    loads = jnp.stack([nearside, direction[:, :, 0], leftside, direction[:, :, 1]], axis=2)
    loads = loads.reshape(cycle_count, circ_count, 4 * face_size, load_count)
    corner_terms = jnp.einsum("rcki,rcin->rckn", coupling, loads, precision=HIGH)
    coarse = jnp.zeros((corner_rows.shape[-1], load_count), jnp.float32)
    coarse = coarse.at[corner_dofs.reshape(-1)].add(corner_terms.reshape(-1, load_count), mode="drop")
    corner_values = jnp.einsum("rckm,mn->rckn", corner_rows, coarse, precision=HIGH)
    moved = jnp.einsum("rcij,rcjn->rcin", flexibility, loads, precision=HIGH)
    moved = moved + jnp.einsum("rcki,rckn->rcin", coupling, corner_values, precision=HIGH)
    moved = moved.reshape(cycle_count, circ_count, 4, face_size, load_count)
    far_near = jnp.concatenate([moved[1:, :, 0], jnp.zeros_like(moved[:1, :, 0])], axis=0)
    right_left = jnp.roll(moved[:, :, 2], -1, axis=1)
    jump_far = moved[:, :, 1] - rotate(far_near, offsets[:, :, 0], -1)
    jump_right = moved[:, :, 3] - rotate(right_left, offsets[:, :, 1], -1)
    active = (offsets >= 0).astype(jnp.float32)[..., None, None]
    return jnp.stack([jump_far, jump_right], axis=2) * active


def inner_sum(first, second):
    return jnp.sum(first * second, axis=(0, 1, 2, 3))


def reference(gap_load, offsets, corner_map, flexibility, coupling, corner_rows):
    active = (offsets >= 0).astype(jnp.float32)[..., None, None]
    corner_dofs = corner_indices(corner_map, corner_rows.shape[-1])
    residual = gap_load * active
    direction = residual
    multipliers = jnp.zeros_like(residual)
    norm_now = inner_sum(residual, residual)
    for iteration in range(ITERS):
        mapped = operator(direction, offsets, flexibility, coupling, corner_rows, corner_dofs)
        step_size = norm_now / inner_sum(direction, mapped)
        multipliers = multipliers + step_size * direction
        residual = residual - step_size * mapped
        norm_next = inner_sum(residual, residual)
        direction = residual + (norm_next / norm_now) * direction
        norm_now = norm_next
    return multipliers, residual
```

```python
import functools

import jax
import jax.numpy as jnp
from jax import lax
from jax.experimental import pallas as pl
from jax.experimental.pallas import tpu as pltpu
from jax.sharding import PartitionSpec as P

ITERS = 3
NEAR, FAR, LEFT, RIGHT = range(4)
VMEM = pl.BlockSpec(memory_space=pltpu.VMEM)
SMEM = pl.BlockSpec(memory_space=pltpu.SMEM)
ANY = pl.BlockSpec(memory_space=pl.ANY)
F32, BF16 = jnp.float32, jnp.bfloat16


def shifted(value, axis, steps, wrap):
    count = lax.axis_size(axis)
    if wrap:
        pairs = [(source, (source + steps) % count) for source in range(count)]
    else:
        pairs = [(source, source + steps) for source in range(count) if 0 <= source + steps < count]
    return lax.ppermute(value, axis, pairs)


def summed(value, axis):
    others = [shifted(value, axis, k, True) for k in range(1, lax.axis_size(axis))]
    return functools.reduce(jnp.add, others, value)


def collected(value, axis):
    count, stride = lax.axis_size(axis), 1
    parts = [value]
    while stride < count:
        radix = next((r for r in range(8, 1, -1) if (count // stride) % r == 0), count // stride)
        value = parts[0] if len(parts) == 1 else jnp.concatenate(parts, axis=0)
        parts = [value] + [shifted(value, axis, k * stride, True) for k in range(1, radix)]
        stride *= radix
    return parts


def halves(value):
    high = value.astype(BF16)
    return high, (value - high.astype(F32)).astype(BF16)


def kept_halves(value):
    high = lax.reduce_precision(value, 8, 7)
    return high.astype(BF16), (value - high).astype(BF16)


def dot(first, second):
    return lax.dot_general(first, second, (((1,), (0,)), ((), ())), preferred_element_type=F32)


def rotated(buffer, value, start):
    size = value.shape[0]
    buffer[0:size] = value
    buffer[size:] = value
    return buffer[pl.ds(start, size)]


def prepare_kernel(offsets, gap, residual, to_far, to_right, inner, buffer):
    count, _, size, _ = gap.shape
    for s in range(count):
        for face in range(2):
            shift = offsets[s, face]
            value = gap[s, face] * (shift >= 0).astype(F32)
            residual[s, face] = value
            turned = -rotated(buffer.at[s, face], value, jnp.maximum(shift, 0))
            if face == 0:
                to_far[s] = turned
            elif s == count - 1:
                to_right[...] = turned
            else:
                inner[s] = turned
    inner[count - 1] = jnp.zeros(inner.shape[1:], F32)


def split_kernel(block, high, low):
    high[...], low[...] = halves(block[...])


def apply_flexibility(loads, a_high, a_low, coupling, height, outs, scratch, rr_rows):
    near, far, sides, to_left, to_right, terms = outs
    split = scratch["split"]
    count, size = len(loads), loads[0][0].shape[0]
    for s in range(count):
        for face in range(4):
            high, low = halves(loads[s][face])
            split[s, face * size:(face + 1) * size, 0:128] = high
            split[s, face * size:(face + 1) * size, 128:256] = low
    terms[...] = jnp.zeros_like(terms)
    total = jnp.zeros((1, 128), F32)
    width = coupling.shape[1] // 2
    for s in range(count):
        both = dot(coupling[s], split[s])
        mine = both[0:width, 0:128] + both[0:width, 128:256] + both[width:, 0:128]
        terms[s * height:s * height + width] += mine
    for s in range(count):
        for face in range(4):
            scratch["wait"](s * 4 + face)
            rows = slice(face * size, (face + 1) * size)
            product = dot(a_high[s, rows], split[s])
            product = product[:, 0:128] + product[:, 128:256]
            product = product + dot(a_low[s, rows], split[s, :, 0:128])
            total = total + jnp.sum(product * loads[s][face], axis=0, keepdims=True)
            if face == NEAR:
                near[s] = product
            elif face == FAR:
                far[s] = product
            else:
                sides[s, face - 2] = product
                if face == LEFT and s == 0:
                    to_left[...] = product
                if face == RIGHT and s == count - 1:
                    to_right[...] = product
    squares = jnp.zeros((1, 128), F32)
    for s in range(count):
        for face in (FAR, RIGHT):
            squares = squares + jnp.sum(loads[s][face] * loads[s][face], axis=0, keepdims=True)
    terms[rr_rows:rr_rows + 1] = squares
    terms[rr_rows + 1:rr_rows + 2] = total


def finish_operator(offsets, terms, matrix, spread, product, received, height, rr_rows, scratch, faces):
    k_high, k_low = matrix
    ct_own, ct_left, ct_right = spread
    near, far, sides = product
    from_near, from_far, from_left, from_right = received
    count, size = near.shape[0], near.shape[1]
    blocks = len(terms)
    stacked = scratch["stack"]
    norm = functools.reduce(jnp.add, [t[rr_rows:rr_rows + 1] for t in terms])
    energy = functools.reduce(jnp.add, [t[rr_rows + 1:rr_rows + 2] for t in terms])
    span = count * height
    for k in range(blocks):
        stacked[k * span:(k + 1) * span] = terms[k][0:span]
        stacked[k * span:k * span + height] = (
            terms[k][0:height] + terms[(k + 1) % blocks][span:span + height]
        )
    coarse = stacked[...]
    high, low = halves(coarse)
    both = dot(k_high[...], jnp.concatenate([high, low], axis=1))
    values = both[:, 0:128] + both[:, 128:256] + dot(k_low[...], high)
    energy = energy + jnp.sum(coarse * values, axis=0, keepdims=True)

    def column(q):
        block = (-(q // count)) % blocks
        at = block * span + (q % count) * height
        return values[at:at + height]

    def tripled(q):
        high, low = halves(jnp.concatenate([column(q), column(q + 1)], axis=0))
        return jnp.concatenate([high, high, low], axis=0)

    own = [[None] * 4 for _ in range(count)]
    other = [[None] * 4 for _ in range(count)]
    for s in range(count):
        added = dot(ct_own[s], tripled(s))
        parts = [added[i * size:(i + 1) * size] for i in range(6)]
        raw = [near[s], far[s], sides[s, 0], sides[s, 1]]
        own[s] = [raw[i] + parts[i] for i in range(4)]
        other[s][FAR] = from_far[s] + parts[4]
        if NEAR in faces:
            other[s][NEAR] = from_near[s] + parts[5]
    other[count - 1][RIGHT] = from_right[...] + dot(ct_right[...], tripled(count))
    if LEFT in faces:
        other[0][LEFT] = from_left[...] + dot(ct_left[...], tripled(-1))
    for s in range(count):
        if s + 1 < count:
            other[s][RIGHT] = own[s + 1][LEFT]
        if s > 0:
            other[s][LEFT] = own[s - 1][RIGHT]
    result = [[None] * 4 for _ in range(count)]
    for s in range(count):
        for face in faces:
            shift = offsets[s, face]
            safe = jnp.maximum(shift, 0)
            start = safe if face in (NEAR, LEFT) else size - safe
            turned = rotated(scratch["turn"].at[s, face], other[s][face], start)
            result[s][face] = (own[s][face] - turned) * (shift >= 0).astype(F32)
    return result, norm, energy


def copies_of(high, low, high_buffer, low_buffer, sems, size):
    count = high.shape[0]
    pairs = []
    for s in range(count):
        for face in range(4):
            rows = pl.ds(face * size, size)
            index = s * 4 + face
            pairs.append((
                pltpu.make_async_copy(high.at[s, rows], high_buffer.at[s, rows], sems.at[0, index]),
                pltpu.make_async_copy(low.at[s, rows], low_buffer.at[s, rows], sems.at[1, index]),
            ))
    for pair in pairs:
        for copy in pair:
            copy.start()

    def wait(index):
        for copy in pairs[index]:
            copy.wait()

    return wait


def first_kernel(height, rr_rows, residual, from_near, from_left, inner, a_high, a_low, coupling, *rest):
    outs, loads_out = rest[0:6], rest[6]
    high_buffer, low_buffer, sems, split = rest[7:]
    count, size = residual.shape[0], residual.shape[2]
    scratch = dict(split=split, wait=copies_of(a_high, a_low, high_buffer, low_buffer, sems, size))
    loads = []
    for s in range(count):
        left = from_left[...] if s == 0 else inner[s - 1]
        loads.append([from_near[s], residual[s, 0], left, residual[s, 1]])
        for face in range(4):
            loads_out[s, face] = loads[s][face]
    apply_flexibility(loads, high_buffer, low_buffer, coupling, height, outs, scratch, rr_rows)


def step_kernel(which, pieces, height, rr_rows, *refs):
    refs = list(refs)
    take = lambda number: [refs.pop(0) for _ in range(number)]
    last = which == ITERS - 1
    (offsets,) = take(1)
    terms = take(pieces)
    matrix, spread, product, received = take(2), take(3), take(3), take(4)
    (loads,) = take(1)
    map_before, ways, found, scalars = (take(4) if which > 0 else [None] * 4)
    if not last:
        a_high, a_low, coupling = take(3)
        outs = take(6)
        loads_out, map_out = take(2)
        ways_out, found_out = take(2) if which > 0 else (None, None)
        (scalars_out,) = take(1)
        stack, turn, high_buffer, low_buffer, sems, split = take(6)
        faces = (NEAR, FAR, LEFT, RIGHT)
    else:
        found_out, residual_out = take(2)
        stack, turn = take(2)
        faces = (FAR, RIGHT)
    count, size = loads.shape[0], loads.shape[2]
    scratch = dict(stack=stack, turn=turn)
    if not last:
        scratch["split"] = split
        scratch["wait"] = copies_of(a_high, a_low, high_buffer, low_buffer, sems, size)
    span = (count + 1) * height
    terms = [t[i:i + span] for t in terms for i in range(0, t.shape[0], span)]
    mapped, norm, energy = finish_operator(
        offsets, terms, matrix, spread, product, received, height, rr_rows, scratch, faces
    )
    if which > 0:
        ratio = norm / scalars[0:1]
        energy = energy - ratio * norm / scalars[1:2]
    step = norm / energy
    fresh = [[None] * 4 for _ in range(count)]
    for s in range(count):
        for face in faces:
            here = mapped[s][face]
            now = loads[s, face]
            if which > 0:
                here = here + ratio * map_before[s, face]
            fresh[s][face] = now - step * here
            if not last:
                map_out[s, face] = here
                loads_out[s, face] = fresh[s][face]
            if face in (FAR, RIGHT):
                i = 0 if face == FAR else 1
                if which == 0:
                    continue
                if which == 1:
                    before = ways[s, face]
                    start = scalars[1:2] * before
                else:
                    before = ways[s, i]
                    start = found[s, i]
                way = now + ratio * before
                found_out[s, i] = start + step * way
                if last:
                    residual_out[s, i] = fresh[s][face]
                else:
                    ways_out[s, i] = way
    if not last:
        scalars_out[...] = jnp.concatenate([norm, step, jnp.zeros((6, 128), F32)], axis=0)
        apply_flexibility(fresh, high_buffer, low_buffer, coupling, height, outs, scratch, rr_rows)


def placed(rows, at, height):
    pad = [(0, 0)] * (rows.ndim - 2) + [(height, height), (0, 0)]
    return lax.dynamic_slice_in_dim(jnp.pad(rows, pad), height - 3 * (at - 1), height, axis=rows.ndim - 2)


def by_columns(coupling):
    lead, length = coupling.shape[:-2], coupling.shape[-1]
    split = coupling.reshape(lead + (2, 2, 3, length))
    return jnp.swapaxes(split, -4, -3).reshape(lead + (2, 6, length))


def spread_out(faces, at, height):
    wide = placed(by_columns(faces), at, height)
    wide = wide.reshape(wide.shape[:-3] + (2 * height, wide.shape[-1]))
    high, low = kept_halves(jnp.swapaxes(wide, -1, -2))
    return jnp.concatenate([high, low, high], axis=-1)


def per_device(gap_load, offsets, corner_map, flexibility, coupling, corner_rows):
    _, count, _, size, loads_n = gap_load.shape
    dofs = corner_rows.shape[-1]
    cuts, blocks = lax.axis_size("cuts"), lax.axis_size("blk")
    at = lax.axis_index("cuts")
    rr_rows = 3 * cuts
    height = -(-(rr_rows + 2) // 8) * 8
    gap, offsets, corner_map, flexibility, coupling, corner_rows = (
        x[0] for x in (gap_load, offsets, corner_map, flexibility, coupling, corner_rows)
    )
    shape = lambda *dims: jax.ShapeDtypeStruct(dims, F32)
    face = shape(size, loads_n)
    faces = shape(count, size, loads_n)
    pair = shape(count, 2, size, loads_n)
    four = shape(count, 4, size, loads_n)

    residual, to_far, to_right, inner = pl.pallas_call(
        prepare_kernel,
        out_shape=(pair, faces, face, faces),
        in_specs=[SMEM, VMEM],
        out_specs=(VMEM,) * 4,
        scratch_shapes=[pltpu.VMEM((count, 2, 2 * size, loads_n), F32)],
        name="prepare",
    )(offsets, gap)
    from_near = shifted(to_far, "cuts", 1, False)
    from_left = shifted(to_right, "blk", 1, True)

    tile = size
    total = flexibility.shape[1]
    block = pl.BlockSpec((1, tile, total), lambda s, i: (s, i, 0))
    a_high, a_low = pl.pallas_call(
        split_kernel,
        grid=(count, total // tile),
        out_shape=(jax.ShapeDtypeStruct(flexibility.shape, BF16),) * 2,
        in_specs=[block],
        out_specs=(block, block),
        name="split",
    )(flexibility)

    cface = lambda f: coupling[:, :, f * size:(f + 1) * size]
    note = lambda amounts: jnp.broadcast_to((amounts + 1).astype(F32)[:, None, None], (amounts.shape[0], 4, size))
    c_far = jnp.concatenate([cface(FAR), note(offsets[:, 0])], axis=1)
    c_right = jnp.concatenate([cface(RIGHT)[-1:], note(offsets[-1:, 1])], axis=1)
    c_from_near = shifted(c_far, "cuts", 1, False)
    c_from_far = shifted(cface(NEAR), "cuts", -1, False)
    c_from_left = shifted(c_right, "blk", 1, True)
    c_from_right = shifted(cface(LEFT)[:1], "blk", -1, True)
    near_offsets = c_from_near[:, 12, 0].astype(jnp.int32) - 1
    first_left = c_from_left[:, 12, 0].astype(jnp.int32) - 1
    left_offsets = jnp.concatenate([first_left, offsets[:-1, 1]])
    all_offsets = jnp.stack([near_offsets, offsets[:, 0], left_offsets, offsets[:, 1]], axis=1)
    wide = placed(by_columns(coupling), at, height).reshape(count, 2 * height, total)
    c_rows = jnp.concatenate(kept_halves(wide), axis=1)
    own = spread_out(coupling, at, height)
    far_part = spread_out(c_from_far, at + 1, height)
    near_part = spread_out(c_from_near[:, :12], at - 1, height)
    ct_own = jnp.concatenate([own, far_part, near_part], axis=1)
    ct_left = spread_out(c_from_left[0, :12], at, height)
    ct_right = spread_out(c_from_right[0], at, height)

    slots = jnp.zeros((count, height, dofs), F32)
    slots = lax.dynamic_update_slice(slots, corner_rows[:, 6:9], (0, 3 * at, 0))
    numbers = (corner_map[:, 2] + 1).astype(F32)[:, None, None]
    slots = lax.dynamic_update_slice(slots, numbers, (0, rr_rows, at))
    pieces = collected(summed(slots.reshape(count * height, dofs), "cuts"), "blk")
    numbers = jnp.concatenate([
        piece.reshape(-1, height, dofs)[:, rr_rows, :cuts].astype(jnp.int32) - 1 for piece in pieces
    ], axis=0)
    chosen = 3 * numbers[..., None] + jnp.arange(3, dtype=jnp.int32)
    chosen = jnp.pad(chosen.reshape(-1, rr_rows), ((0, 0), (0, height - rr_rows)), constant_values=-1).reshape(-1)
    pick = (jnp.arange(dofs, dtype=jnp.int32)[:, None] == chosen[None, :]).astype(BF16)
    used = (jnp.arange(pieces[0].shape[0]) % height < rr_rows)[:, None]
    k_parts = [kept_halves(jnp.where(used, piece, 0.0)) for piece in pieces]
    k_high, k_low = (
        jnp.concatenate([jnp.dot(part[i], pick, preferred_element_type=F32).astype(BF16) for part in k_parts], axis=0)
        for i in range(2)
    )

    flops = 2 * count * total * total * loads_n * 3
    moved = 4 * flexibility.size
    cost = pl.CostEstimate(flops=flops, bytes_accessed=moved, transcendentals=0)
    params = pltpu.CompilerParams(vmem_limit_bytes=40 * 1024 * 1024)
    terms_shape = shape((count + 1) * height, loads_n)
    sends = (faces, faces, pair, face, face, terms_shape)
    a_buffers = [
        pltpu.VMEM(flexibility.shape, BF16),
        pltpu.VMEM(flexibility.shape, BF16),
        pltpu.SemaphoreType.DMA((2, 4 * count)),
        pltpu.VMEM((count, total, 2 * loads_n), BF16),
    ]
    f_buffers = [
        pltpu.VMEM((blocks * count * height, loads_n), F32),
        pltpu.VMEM((count, 4, 2 * size, loads_n), F32),
    ]
    *out, loads = pl.pallas_call(
        functools.partial(first_kernel, height, rr_rows),
        out_shape=sends + (four,),
        in_specs=[VMEM] * 4 + [ANY] * 2 + [VMEM],
        out_specs=(VMEM,) * 7,
        scratch_shapes=a_buffers,
        compiler_params=params,
        cost_estimate=cost,
        name="first",
    )(residual, from_near, from_left, inner, a_high, a_low, c_rows)

    state = []
    for which in range(ITERS):
        last = which == ITERS - 1
        near, far, sides, to_left, to_right, terms = out
        gathered = collected(summed(terms, "cuts"), "blk")
        r_far = shifted(near, "cuts", -1, False)
        r_right = shifted(to_left, "blk", -1, True)
        if last:
            r_near, r_left = far, to_right
        else:
            r_near = shifted(far, "cuts", 1, False)
            r_left = shifted(to_right, "blk", 1, True)
        args = [all_offsets, *gathered, k_high, k_low, ct_own, ct_left, ct_right, near, far, sides,
                r_near, r_far, r_left, r_right, loads, *state]
        specs = [SMEM] + [VMEM] * (len(args) - 1)
        if last:
            outs, scratch = (pair, pair), f_buffers
        else:
            args += [a_high, a_low, c_rows]
            specs += [ANY, ANY, VMEM]
            outs = sends + (four, four) + ((pair, pair) if which > 0 else ()) + (shape(8, loads_n),)
            scratch = f_buffers + a_buffers
        result = pl.pallas_call(
            functools.partial(step_kernel, which, len(gathered), height, rr_rows),
            out_shape=outs,
            in_specs=specs,
            out_specs=(VMEM,) * len(outs),
            scratch_shapes=scratch,
            compiler_params=params,
            cost_estimate=None if last else cost,
            name=f"step{which}",
        )(*args)
        if last:
            multipliers, residual = result
            break
        out = result[0:6]
        before, loads = loads, result[6]
        if which == 0:
            state = [result[7], before, before, result[8]]
        else:
            state = [result[7], result[8], result[9], result[10]]
    return multipliers[None], residual[None]


def solution(mesh):
    spec5, spec4, spec3 = (P("cuts", "blk", *[None] * k) for k in (3, 2, 1))
    return jax.shard_map(
        per_device,
        mesh=mesh,
        in_specs=(spec5, spec3, spec3, spec4, spec4, spec4),
        out_specs=(spec5, spec5),
        check_vma=False,
    )
```

```python
import functools

import jax
import jax.numpy as jnp
import numpy as np
from jax import lax
from jax.experimental import pallas as pl
from jax.experimental.pallas import tpu as pltpu
from jax.sharding import PartitionSpec as P

ITERS = 3
NEAR, FAR, LEFT, RIGHT = range(4)
VMEM = pl.BlockSpec(memory_space=pltpu.VMEM)
SMEM = pl.BlockSpec(memory_space=pltpu.SMEM)
ANY = pl.BlockSpec(memory_space=pl.ANY)
F32, BF16 = jnp.float32, jnp.bfloat16


def shifted(value, axis, steps, wrap):
    count = lax.axis_size(axis)
    if wrap:
        pairs = [(source, (source + steps) % count) for source in range(count)]
    else:
        pairs = [(source, source + steps) for source in range(count) if 0 <= source + steps < count]
    return lax.ppermute(value, axis, pairs)


def summed(value, axis):
    others = [shifted(value, axis, k, True) for k in range(1, lax.axis_size(axis))]
    return functools.reduce(jnp.add, others, value)


def chip_parts(value, axis):
    count, stride = lax.axis_size(axis) // 2, 1
    parts = [value]
    while stride < count:
        radix = next((r for r in range(8, 1, -1) if (count // stride) % r == 0), count // stride)
        value = parts[0] if len(parts) == 1 else jnp.concatenate(parts, axis=0)
        parts = [value] + [shifted(value, axis, 2 * k * stride, True) for k in range(1, radix)]
        stride *= radix
    return parts


def swapped(value, axis):
    return lax.ppermute(value, axis, [(source, source ^ 1) for source in range(lax.axis_size(axis))])


def halves(value):
    high = value.astype(BF16)
    return high, (value - high.astype(F32)).astype(BF16)


def kept_halves(value):
    high = lax.reduce_precision(value, 8, 7)
    return high.astype(BF16), (value - high).astype(BF16)


def dot(first, second):
    return lax.dot_general(first, second, (((1,), (0,)), ((), ())), preferred_element_type=F32)


def rotated(buffer, value, start):
    size = value.shape[0]
    buffer[0:size] = value
    buffer[size:] = value
    return buffer[pl.ds(start, size)]


def corner_kernel(cuts, height, at, corner_map, corner_rows, slots):
    count, _, dofs = corner_rows.shape
    lane = lax.broadcasted_iota(jnp.int32, (1, dofs), 1)
    slots[...] = jnp.zeros_like(slots)
    for s in range(count):
        for a in range(cuts):
            keep = (at[0] == a).astype(F32)
            slots[s * height + 3 * a:s * height + 3 * a + 3] = corner_rows[s, 6:9] * keep
        number = (corner_map[s, 2] + 1).astype(F32)
        slots[s * height + 3 * cuts:s * height + 3 * cuts + 1] = jnp.where(lane == at[0], number, 0.0)


def put_coupling(ref, size, face, amount):
    for i in range(size // 128):
        rows = size + 16 * i
        ref[rows:rows + 12] = face[:, i * 128:(i + 1) * 128]
        ref[rows + 12:rows + 16] = jnp.full((4, 128), amount, F32)


def got_coupling(ref, size):
    return jnp.concatenate([ref[size + 16 * i:size + 16 * i + 12] for i in range(size // 128)], axis=1)


def prepare_kernel(at, offsets, gap, coupling, rows_table, residual, to_far, to_right, inner, c_rows, buffer):
    count, _, size, _ = gap.shape
    for s in range(count):
        for face in range(2):
            shift = offsets[s, face]
            value = gap[s, face] * (shift >= 0).astype(F32)
            residual[s, face] = value
            turned = -rotated(buffer.at[s, face], value, jnp.maximum(shift, 0))
            amount = (shift + 1).astype(F32)
            if face == 0:
                to_far[s, 0:size] = turned
                put_coupling(to_far.at[s], size, coupling[s, :, FAR * size:(FAR + 1) * size], amount)
            elif s == count - 1:
                to_right[0:size] = turned
                put_coupling(to_right, size, coupling[s, :, RIGHT * size:(RIGHT + 1) * size], amount)
            else:
                inner[s] = turned
        c_rows[s] = dot(rows_table[at[0]], paired(coupling[s])).astype(BF16)
    inner[count - 1] = jnp.zeros(inner.shape[1:], F32)


def paired(face):
    high, low = halves(face)
    rest = jnp.zeros((4, face.shape[1]), F32)
    both = jnp.concatenate([high.astype(F32), rest, low.astype(F32), rest], axis=0)
    return both.astype(BF16)


def spread_kernel(at, coupling, from_near, from_far, from_left, from_right, table, ct_own, ct_left, ct_right):
    count, size = coupling.shape[0], coupling.shape[2] // 4

    def turned(face, cycle):
        product = lax.dot_general(
            paired(face), table[cycle + 1], (((0,), (0,)), ((), ())), preferred_element_type=F32
        )
        return product.astype(BF16)

    for s in range(count):
        ct_own[s, 0:4 * size] = turned(coupling[s], at[0])
        ct_own[s, 4 * size:5 * size] = turned(got_coupling(from_far.at[s], size), at[0] + 1)
        ct_own[s, 5 * size:6 * size] = turned(got_coupling(from_near.at[s], size), at[0] - 1)
    ct_left[...] = turned(got_coupling(from_left, size), at[0])
    ct_right[...] = turned(got_coupling(from_right, size), at[0])


def split_kernel(block, high, low):
    for s in range(block.shape[0]):
        for i in range(0, block.shape[1], 256):
            high[s, i:i + 256], low[s, i:i + 256] = halves(block[s, i:i + 256])


def sum_kernel(parts, *refs):
    refs[parts + (len(refs) - parts - 1) // 2][...] = functools.reduce(jnp.add, [r[...] for r in refs[:parts]])


def stack_kernel(parts, *refs):
    out = refs[parts + (len(refs) - parts - 1) // 2]
    size = refs[0].shape[0]
    for i in range(parts):
        out[i * size:(i + 1) * size] = refs[i][...]


def relay(kernel, parts, shape, through, name):
    specs = [VMEM] * len(parts) + [ANY] * len(through)
    return pl.pallas_call(
        functools.partial(kernel, len(parts)),
        out_shape=(shape, *[jax.ShapeDtypeStruct(x.shape, x.dtype) for x in through]),
        in_specs=specs,
        out_specs=(VMEM, *[ANY] * len(through)),
        input_output_aliases={len(parts) + i: 1 + i for i in range(len(through))},
        name=name,
    )(*parts, *through)


def apply_flexibility(loads, a_high, a_low, coupling, height, outs, scratch, rr_rows):
    near, far, sides, to_left, to_right, terms = outs
    split = scratch["split"]
    count, size = len(loads), loads[0][0].shape[0]
    for s in range(count):
        for face in range(4):
            high, low = halves(loads[s][face])
            split[s, face * size:(face + 1) * size, 0:128] = high
            split[s, face * size:(face + 1) * size, 128:256] = low
    terms[...] = jnp.zeros_like(terms)
    total = jnp.zeros((1, 128), F32)
    width = coupling.shape[1] // 2
    for s in range(count):
        both = dot(coupling[s], split[s])
        mine = both[0:width, 0:128] + both[0:width, 128:256] + both[width:, 0:128]
        terms[s * height:s * height + width] += mine
    for s in range(count):
        whole = dot(a_high[s], split[s])
        whole = whole[:, 0:128] + whole[:, 128:256] + dot(a_low[s], split[s, :, 0:128])
        for face in range(4):
            product = whole[face * size:(face + 1) * size]
            total = total + jnp.sum(product * loads[s][face], axis=0, keepdims=True)
            if face == NEAR:
                near[s, 0:size] = product
            elif face == FAR:
                far[s] = product
            else:
                sides[s, face - 2] = product
                if face == LEFT and s == 0:
                    to_left[0:size] = product
                if face == RIGHT and s == count - 1:
                    to_right[...] = product
    squares = jnp.zeros((1, 128), F32)
    for s in range(count):
        for face in (FAR, RIGHT):
            squares = squares + jnp.sum(loads[s][face] * loads[s][face], axis=0, keepdims=True)
    terms[rr_rows:rr_rows + 1] = squares
    terms[rr_rows + 1:rr_rows + 2] = total


def finish_operator(offsets, terms, matrix, spread, product, received, height, rr_rows, scratch, faces):
    k_high, k_low = matrix
    ct_own, ct_left, ct_right = spread
    near, far, sides = product
    from_near, from_far, from_left, from_right = received
    count, size = far.shape[0], far.shape[1]
    side, mine, theirs = terms
    odd = side[0] == 1
    stacked, table = scratch["stack"], scratch["values"]
    span = count * height
    chips = mine.shape[0] // (span + height)
    terms = []
    for k in range(chips):
        first, second = (x[k * (span + height):(k + 1) * (span + height)] for x in (mine, theirs))
        terms += [jnp.where(odd, second, first), jnp.where(odd, first, second)]
    norm = functools.reduce(jnp.add, [t[rr_rows:rr_rows + 1] for t in terms])
    energy = functools.reduce(jnp.add, [t[rr_rows + 1:rr_rows + 2] for t in terms])
    for k in range(2 * chips):
        behind = k - 1 if k % 2 else (k + 3) % (2 * chips)
        stacked[k * span:(k + 1) * span] = terms[k][0:span]
        stacked[k * span:k * span + height] = terms[k][0:height] + terms[behind][span:span + height]
    coarse = stacked[...]
    high, low = halves(coarse)
    both = dot(k_high[...], jnp.concatenate([high, low], axis=1))
    values = both[:, 0:128] + both[:, 128:256] + dot(k_low[...], high)
    energy = energy + jnp.sum(coarse * values, axis=0, keepdims=True)

    table[...] = values

    def column(q):
        along = side[0] + q // count
        block = (2 * (-(along // 2)) + along % 2) % (2 * chips)
        at = block * span + (q % count) * height
        return table[pl.ds(pl.multiple_of(at, 8), height)]

    def tripled(q):
        high, low = halves(jnp.concatenate([column(q), column(q + 1)], axis=0))
        return jnp.concatenate([high, high, low], axis=0)

    own = [[None] * 4 for _ in range(count)]
    other = [[None] * 4 for _ in range(count)]
    for s in range(count):
        added = dot(ct_own[s], tripled(s))
        parts = [added[i * size:(i + 1) * size] for i in range(6)]
        raw = [near[s, 0:size], far[s], sides[s, 0], sides[s, 1]]
        own[s] = [raw[i] + parts[i] for i in range(4)]
        other[s][FAR] = from_far[s, 0:size] + parts[4]
        if NEAR in faces:
            other[s][NEAR] = from_near[s] + parts[5]
    other[count - 1][RIGHT] = from_right[0:size] + dot(ct_right[...], tripled(count))
    if LEFT in faces:
        other[0][LEFT] = from_left[...] + dot(ct_left[...], tripled(-1))
    for s in range(count):
        if s + 1 < count:
            other[s][RIGHT] = own[s + 1][LEFT]
        if s > 0:
            other[s][LEFT] = own[s - 1][RIGHT]
    result = [[None] * 4 for _ in range(count)]
    for s in range(count):
        for face in faces:
            shift = offsets[s, face]
            safe = jnp.maximum(shift, 0)
            start = safe if face in (NEAR, LEFT) else size - safe
            turned = rotated(scratch["turn"].at[s, face], other[s][face], start)
            result[s][face] = (own[s][face] - turned) * (shift >= 0).astype(F32)
    return result, norm, energy


def first_kernel(height, rr_rows, residual, from_near, from_left, inner, coupling, a_high, a_low, c_rows, *rest):
    outs, loads_out, split = rest[0:6], rest[6], rest[7]
    near, to_left = outs[0], outs[3]
    count, size = residual.shape[0], residual.shape[2]
    loads = []
    for s in range(count):
        left = from_left[0:size] if s == 0 else inner[s - 1]
        loads.append([from_near[s, 0:size], residual[s, 0], left, residual[s, 1]])
        for face in range(4):
            loads_out[s, face] = loads[s][face]
        put_coupling(near.at[s], size, coupling[s, :, NEAR * size:(NEAR + 1) * size], 0.0)
    put_coupling(to_left, size, coupling[0, :, LEFT * size:(LEFT + 1) * size], 0.0)
    apply_flexibility(loads, a_high, a_low, c_rows, height, outs, dict(split=split), rr_rows)


def step_kernel(which, height, rr_rows, *refs):
    refs = list(refs)
    take = lambda number: [refs.pop(0) for _ in range(number)]
    last = which == ITERS - 1
    (offsets,) = take(1)
    terms = take(3)
    matrix, spread, product, received = take(2), take(3), take(3), take(4)
    (loads,) = take(1)
    map_before, ways, found, scalars = (take(4) if which > 0 else [None] * 4)
    if not last:
        a_high, a_low, coupling = take(3)
        outs = take(6)
        loads_out, map_out = take(2)
        ways_out, found_out = take(2) if which > 0 else (None, None)
        (scalars_out,) = take(1)
        stack, values, turn, split = take(4)
        faces = (NEAR, FAR, LEFT, RIGHT)
    else:
        found_out, residual_out = take(2)
        stack, values, turn = take(3)
        faces = (FAR, RIGHT)
    count, size = loads.shape[0], loads.shape[2]
    scratch = dict(stack=stack, values=values, turn=turn)
    if not last:
        scratch["split"] = split
    mapped, norm, energy = finish_operator(
        offsets, terms, matrix, spread, product, received, height, rr_rows, scratch, faces
    )
    if which > 0:
        ratio = norm / scalars[0:1]
        energy = energy - ratio * norm / scalars[1:2]
    step = norm / energy
    fresh = [[None] * 4 for _ in range(count)]
    for s in range(count):
        for face in faces:
            here = mapped[s][face]
            now = loads[s, face]
            if which > 0:
                here = here + ratio * map_before[s, face]
            fresh[s][face] = now - step * here
            if not last:
                map_out[s, face] = here
                loads_out[s, face] = fresh[s][face]
            if face in (FAR, RIGHT):
                i = 0 if face == FAR else 1
                if which == 0:
                    continue
                if which == 1:
                    before = ways[s, face]
                    start = scalars[1:2] * before
                else:
                    before = ways[s, i]
                    start = found[s, i]
                way = now + ratio * before
                found_out[s, i] = start + step * way
                if last:
                    residual_out[s, i] = fresh[s][face]
                else:
                    ways_out[s, i] = way
    if not last:
        scalars_out[...] = jnp.concatenate([norm, step, jnp.zeros((6, 128), F32)], axis=0)
        apply_flexibility(fresh, a_high, a_low, coupling, height, outs, scratch, rr_rows)


def corner_tables(cuts, height):
    places = np.zeros((cuts + 2, 12, 2 * height), np.float32)
    for at in range(-1, cuts + 1):
        for k in range(4):
            cycle = at - 1 + k // 2
            if 0 <= cycle < cuts:
                for j in range(3):
                    places[at + 1, 3 * k + j, (k % 2) * height + 3 * cycle + j] = 1
    wide = 2 * height
    table = np.zeros((cuts + 2, 32, 3 * wide), np.float32)
    rows = np.zeros((cuts, 2 * wide, 32), np.float32)
    table[:, 0:12, 0:wide] = table[:, 16:28, wide:2 * wide] = table[:, 0:12, 2 * wide:] = places
    rows[:, 0:wide, 0:12] = rows[:, wide:, 16:28] = np.swapaxes(places[1:-1], 1, 2)
    return jnp.asarray(table, BF16), jnp.asarray(rows, BF16)


def corner_matrix(slots, numbers_at, cuts, height, odd):
    dofs = slots.shape[1]
    parts = chip_parts(summed(slots, "cuts"), "blk")
    mine = jnp.concatenate(parts, axis=0)
    theirs = swapped(mine, "blk")
    mine, theirs = (x.reshape(-1, slots.shape[0], dofs) for x in (mine, theirs))
    rows = jnp.stack([jnp.where(odd, theirs, mine), jnp.where(odd, mine, theirs)], axis=1)
    rows = rows.reshape(-1, height, dofs)
    numbers = rows[:, numbers_at, :cuts].astype(jnp.int32) - 1
    chosen = 3 * numbers[..., None] + jnp.arange(3, dtype=jnp.int32)
    chosen = jnp.pad(chosen.reshape(-1, 3 * cuts), ((0, 0), (0, height - 3 * cuts)), constant_values=-1).reshape(-1)
    pick = (jnp.arange(dofs, dtype=jnp.int32)[:, None] == chosen[None, :]).astype(BF16)
    used = (jnp.arange(height) < numbers_at)[:, None]
    high, low = kept_halves(jnp.where(used, rows, 0.0).reshape(-1, dofs))
    return [jnp.dot(part, pick, preferred_element_type=F32).astype(BF16) for part in (high, low)]


def per_device(gap_load, offsets, corner_map, flexibility, coupling, corner_rows):
    _, count, _, size, loads_n = gap_load.shape
    dofs = corner_rows.shape[-1]
    cuts, blocks = lax.axis_size("cuts"), lax.axis_size("blk")
    at = lax.axis_index("cuts").reshape(1)
    side = (lax.axis_index("blk") % 2).reshape(1)
    rr_rows = 3 * cuts
    height = -(-(rr_rows + 2) // 8) * 8
    gap, offsets, corner_map, flexibility, coupling, corner_rows = (
        x[0] for x in (gap_load, offsets, corner_map, flexibility, coupling, corner_rows)
    )
    total = flexibility.shape[1]
    below = 16 * (size // 128)
    shape = lambda *dims, kind=F32: jax.ShapeDtypeStruct(dims, kind)
    face = shape(size, loads_n)
    faces = shape(count, size, loads_n)
    pair = shape(count, 2, size, loads_n)
    four = shape(count, 4, size, loads_n)
    long_face = shape(size + below, loads_n)
    long_faces = shape(count, size + below, loads_n)
    params = pltpu.CompilerParams(vmem_limit_bytes=40 * 1024 * 1024)
    table, rows_table = corner_tables(cuts, height)

    slots = pl.pallas_call(
        functools.partial(corner_kernel, cuts, height),
        out_shape=shape(count * height, dofs),
        in_specs=[SMEM, SMEM, VMEM],
        out_specs=VMEM,
        name="corner",
    )(at, corner_map, corner_rows)
    residual, to_far, to_right, inner, c_rows = pl.pallas_call(
        prepare_kernel,
        out_shape=(pair, long_faces, long_face, faces, shape(count, 4 * height, total, kind=BF16)),
        in_specs=[SMEM, SMEM] + [VMEM] * 3,
        out_specs=(VMEM,) * 5,
        scratch_shapes=[pltpu.VMEM((count, 2, 2 * size, loads_n), F32)],
        name="prepare",
    )(at, offsets, gap, coupling, rows_table)
    from_near = shifted(to_far, "cuts", 1, False)
    from_left = shifted(to_right, "blk", 1, True)
    k_high, k_low = corner_matrix(slots, rr_rows, cuts, height, side[0] == 1)
    a_high, a_low = pl.pallas_call(
        split_kernel,
        out_shape=(jax.ShapeDtypeStruct(flexibility.shape, BF16),) * 2,
        in_specs=[VMEM],
        out_specs=(VMEM, VMEM),
        compiler_params=params,
        cost_estimate=pl.CostEstimate(flops=0, bytes_accessed=8 * flexibility.size, transcendentals=0),
        name="split",
    )(flexibility)
    near_offsets = from_near[:, size + 12, 0]
    left_offsets = jnp.concatenate([from_left[size + 12:size + 13, 0], (offsets[:-1, 1] + 1).astype(F32)])
    all_offsets = jnp.stack([
        near_offsets.astype(jnp.int32) - 1, offsets[:, 0], left_offsets.astype(jnp.int32) - 1, offsets[:, 1]
    ], axis=1)

    flops = 2 * count * total * total * loads_n * 3
    cost = pl.CostEstimate(flops=flops, bytes_accessed=4 * flexibility.size, transcendentals=0)
    terms_shape = shape((count + 1) * height, loads_n)
    sends = (faces, faces, pair, face, face, terms_shape)
    first_sends = (long_faces, faces, pair, long_face, face, terms_shape)
    a_buffers = [pltpu.VMEM((count, total, 2 * loads_n), BF16)]
    f_buffers = [
        pltpu.VMEM((blocks * count * height, loads_n), F32),
        pltpu.VMEM((blocks * count * height, loads_n), F32),
        pltpu.VMEM((count, 4, 2 * size, loads_n), F32),
    ]
    *out, loads = pl.pallas_call(
        functools.partial(first_kernel, height, rr_rows),
        out_shape=first_sends + (four,),
        in_specs=[VMEM] * 8,
        out_specs=(VMEM,) * 7,
        scratch_shapes=a_buffers,
        compiler_params=params,
        cost_estimate=cost,
        name="first",
    )(residual, from_near, from_left, inner, coupling, a_high, a_low, c_rows)

    state = []
    for which in range(ITERS):
        last = which == ITERS - 1
        near, far, sides, to_left, to_right, terms = out
        pieces = [terms] + [shifted(terms, "cuts", k, True) for k in range(1, cuts)]
        terms, near = relay(sum_kernel, pieces, terms_shape, [near], f"sum{which}")
        r_far = shifted(near, "cuts", -1, False)
        pieces = chip_parts(terms, "blk")
        mine, far, to_left, to_right = relay(
            stack_kernel, pieces, shape(blocks // 2 * terms_shape.shape[0], loads_n), [far, to_left, to_right],
            f"stack{which}",
        )
        theirs = swapped(mine, "blk")
        r_right = shifted(to_left, "blk", -1, True)
        if last:
            r_near, r_left = far, to_right
        else:
            r_near = shifted(far, "cuts", 1, False)
            r_left = shifted(to_right, "blk", 1, True)
        if which == 0:
            ct_own, ct_left, ct_right = pl.pallas_call(
                spread_kernel,
                out_shape=(
                    shape(count, 6 * size, 6 * height, kind=BF16),
                    shape(size, 6 * height, kind=BF16),
                    shape(size, 6 * height, kind=BF16),
                ),
                in_specs=[SMEM] + [VMEM] * 6,
                out_specs=(VMEM,) * 3,
                name="spread",
            )(at, coupling, from_near, r_far, from_left, r_right, table)
        args = [all_offsets, side, mine, theirs, k_high, k_low, ct_own, ct_left, ct_right, near, far, sides,
                r_near, r_far, r_left, r_right, loads, *state]
        specs = [SMEM, SMEM] + [VMEM] * (len(args) - 2)
        if last:
            outs, scratch = (pair, pair), f_buffers
        else:
            args += [a_high, a_low, c_rows]
            specs += [VMEM] * 3
            outs = sends + (four, four) + ((pair, pair) if which > 0 else ()) + (shape(8, loads_n),)
            scratch = f_buffers + a_buffers
        result = pl.pallas_call(
            functools.partial(step_kernel, which, height, rr_rows),
            out_shape=outs,
            in_specs=specs,
            out_specs=(VMEM,) * len(outs),
            scratch_shapes=scratch,
            compiler_params=params,
            cost_estimate=None if last else cost,
            name=f"step{which}",
        )(*args)
        if last:
            multipliers, residual = result
            break
        out = result[0:6]
        before, loads = loads, result[6]
        if which == 0:
            state = [result[7], before, before, result[8]]
        else:
            state = [result[7], result[8], result[9], result[10]]
    return multipliers[None], residual[None]


def solution(mesh):
    spec5, spec4, spec3 = (P("cuts", "blk", *[None] * k) for k in (3, 2, 1))
    return jax.shard_map(
        per_device,
        mesh=mesh,
        in_specs=(spec5, spec3, spec3, spec4, spec4, spec4),
        out_specs=(spec5, spec5),
        check_vma=False,
    )
```

```python
import functools

import jax
import jax.numpy as jnp
import numpy as np
from jax import lax
from jax.experimental import pallas as pl
from jax.experimental.pallas import tpu as pltpu
from jax.sharding import PartitionSpec as P

ITERS = 3
NEAR, FAR, LEFT, RIGHT = range(4)
VMEM = pl.BlockSpec(memory_space=pltpu.VMEM)
SMEM = pl.BlockSpec(memory_space=pltpu.SMEM)
ANY = pl.BlockSpec(memory_space=pl.ANY)
F32, BF16 = jnp.float32, jnp.bfloat16


def shifted(value, axis, steps, wrap):
    count = lax.axis_size(axis)
    if wrap:
        pairs = [(source, (source + steps) % count) for source in range(count)]
    else:
        pairs = [(source, source + steps) for source in range(count) if 0 <= source + steps < count]
    return lax.ppermute(value, axis, pairs)


def summed(value, axis):
    others = [shifted(value, axis, k, True) for k in range(1, lax.axis_size(axis))]
    return functools.reduce(jnp.add, others, value)


def chip_parts(value, axis):
    count, stride = lax.axis_size(axis) // 2, 1
    parts = [value]
    while stride < count:
        radix = next((r for r in range(8, 1, -1) if (count // stride) % r == 0), count // stride)
        value = parts[0] if len(parts) == 1 else jnp.concatenate(parts, axis=0)
        parts = [value] + [shifted(value, axis, 2 * k * stride, True) for k in range(1, radix)]
        stride *= radix
    return parts


def swapped(value, axis):
    return lax.ppermute(value, axis, [(source, source ^ 1) for source in range(lax.axis_size(axis))])


def halves(value):
    high = value.astype(BF16)
    return high, (value - high.astype(F32)).astype(BF16)


def kept_halves(value):
    high = lax.reduce_precision(value, 8, 7)
    return high.astype(BF16), (value - high).astype(BF16)


def dot(first, second):
    return lax.dot_general(first, second, (((1,), (0,)), ((), ())), preferred_element_type=F32)


def rotated(buffer, value, start):
    size = value.shape[0]
    buffer[0:size] = value
    buffer[size:] = value
    return buffer[pl.ds(start, size)]


def corner_kernel(cuts, height, at, corner_map, corner_rows, slots):
    count, _, dofs = corner_rows.shape
    lane = lax.broadcasted_iota(jnp.int32, (1, dofs), 1)
    slots[...] = jnp.zeros_like(slots)
    for s in range(count):
        for a in range(cuts):
            keep = (at[0] == a).astype(F32)
            slots[s * height + 3 * a:s * height + 3 * a + 3] = corner_rows[s, 6:9] * keep
        number = (corner_map[s, 2] + 1).astype(F32)
        slots[s * height + 3 * cuts:s * height + 3 * cuts + 1] = jnp.where(lane == at[0], number, 0.0)


def put_coupling(ref, size, face, amount):
    for i in range(size // 128):
        rows = size + 16 * i
        ref[rows:rows + 12] = face[:, i * 128:(i + 1) * 128]
        ref[rows + 12:rows + 16] = jnp.full((4, 128), amount, F32)


def got_coupling(ref, size):
    return jnp.concatenate([ref[size + 16 * i:size + 16 * i + 12] for i in range(size // 128)], axis=1)


def prepare_kernel(at, offsets, gap, coupling, rows_table, residual, to_far, to_right, inner, c_rows, buffer):
    count, _, size, _ = gap.shape
    for s in range(count):
        for face in range(2):
            shift = offsets[s, face]
            value = gap[s, face] * (shift >= 0).astype(F32)
            residual[s, face] = value
            turned = -rotated(buffer.at[s, face], value, jnp.maximum(shift, 0))
            amount = (shift + 1).astype(F32)
            if face == 0:
                to_far[s, 0:size] = turned
                put_coupling(to_far.at[s], size, coupling[s, :, FAR * size:(FAR + 1) * size], amount)
            elif s == count - 1:
                to_right[0:size] = turned
                put_coupling(to_right, size, coupling[s, :, RIGHT * size:(RIGHT + 1) * size], amount)
            else:
                inner[s] = turned
        c_rows[s] = dot(rows_table[at[0]], paired(coupling[s])).astype(BF16)
    inner[count - 1] = jnp.zeros(inner.shape[1:], F32)


def paired(face):
    high, low = halves(face)
    rest = jnp.zeros((4, face.shape[1]), F32)
    both = jnp.concatenate([high.astype(F32), rest, low.astype(F32), rest], axis=0)
    return both.astype(BF16)


def spread_kernel(at, coupling, from_near, from_far, from_left, from_right, table, ct_own, ct_left, ct_right):
    count, size = coupling.shape[0], coupling.shape[2] // 4

    def turned(face, cycle):
        product = lax.dot_general(
            paired(face), table[cycle + 1], (((0,), (0,)), ((), ())), preferred_element_type=F32
        )
        return product.astype(BF16)

    for s in range(count):
        ct_own[s, 0:4 * size] = turned(coupling[s], at[0])
        ct_own[s, 4 * size:5 * size] = turned(got_coupling(from_far.at[s], size), at[0] + 1)
        ct_own[s, 5 * size:6 * size] = turned(got_coupling(from_near.at[s], size), at[0] - 1)
    ct_left[...] = turned(got_coupling(from_left, size), at[0])
    ct_right[...] = turned(got_coupling(from_right, size), at[0])


def split_kernel(block, high, low):
    for s in range(block.shape[0]):
        for i in range(0, block.shape[1], 256):
            high[s, i:i + 256], low[s, i:i + 256] = halves(block[s, i:i + 256])


def sum_kernel(parts, *refs):
    refs[parts + (len(refs) - parts - 1) // 2][...] = functools.reduce(jnp.add, [r[...] for r in refs[:parts]])


def stack_kernel(parts, *refs):
    out = refs[parts + (len(refs) - parts - 1) // 2]
    size = refs[0].shape[0]
    for i in range(parts):
        out[i * size:(i + 1) * size] = refs[i][...]


def room(*shapes):
    total = 0
    for x in shapes:
        dims = (1, 1, *x.shape)
        total += int(np.prod(dims[:-2])) * -(-dims[-2] // 16) * 16 * -(-dims[-1] // 128) * 128 * np.dtype(x.dtype).itemsize
    return pltpu.CompilerParams(vmem_limit_bytes=total + 2 * 1024 * 1024)


def relay(kernel, parts, shape, through, name):
    specs = [VMEM] * len(parts) + [ANY] * len(through)
    return pl.pallas_call(
        functools.partial(kernel, len(parts)),
        out_shape=(shape, *[jax.ShapeDtypeStruct(x.shape, x.dtype) for x in through]),
        in_specs=specs,
        out_specs=(VMEM, *[ANY] * len(through)),
        compiler_params=room(*parts, shape),
        input_output_aliases={len(parts) + i: 1 + i for i in range(len(through))},
        name=name,
    )(*parts, *through)


def apply_flexibility(loads, a_high, a_low, coupling, height, outs, scratch, rr_rows):
    near, far, sides, to_left, to_right, terms = outs
    split = scratch["split"]
    count, size = len(loads), loads[0][0].shape[0]
    for s in range(count):
        for face in range(4):
            high, low = halves(loads[s][face])
            split[s, face * size:(face + 1) * size, 0:128] = high
            split[s, face * size:(face + 1) * size, 128:256] = low
    terms[...] = jnp.zeros_like(terms)
    total = jnp.zeros((1, 128), F32)
    width = coupling.shape[1] // 2
    for s in range(count):
        both = dot(coupling[s], split[s])
        mine = both[0:width, 0:128] + both[0:width, 128:256] + both[width:, 0:128]
        terms[s * height:s * height + width] += mine
    for s in range(count):
        whole = dot(a_high[s], split[s])
        whole = whole[:, 0:128] + whole[:, 128:256] + dot(a_low[s], split[s, :, 0:128])
        for face in range(4):
            product = whole[face * size:(face + 1) * size]
            total = total + jnp.sum(product * loads[s][face], axis=0, keepdims=True)
            if face == NEAR:
                near[s, 0:size] = product
            elif face == FAR:
                far[s] = product
            else:
                sides[s, face - 2] = product
                if face == LEFT and s == 0:
                    to_left[0:size] = product
                if face == RIGHT and s == count - 1:
                    to_right[...] = product
    squares = jnp.zeros((1, 128), F32)
    for s in range(count):
        for face in (FAR, RIGHT):
            squares = squares + jnp.sum(loads[s][face] * loads[s][face], axis=0, keepdims=True)
    terms[rr_rows:rr_rows + 1] = squares
    terms[rr_rows + 1:rr_rows + 2] = total


def finish_operator(offsets, terms, matrix, spread, product, received, height, rr_rows, scratch, faces):
    k_high, k_low = matrix
    ct_own, ct_left, ct_right = spread
    near, far, sides = product
    from_near, from_far, from_left, from_right = received
    count, size = far.shape[0], far.shape[1]
    side, mine, theirs = terms
    odd = side[0] == 1
    stacked, table = scratch["stack"], scratch["values"]
    span = count * height
    chips = mine.shape[0] // (span + height)
    terms = []
    for k in range(chips):
        first, second = (x[k * (span + height):(k + 1) * (span + height)] for x in (mine, theirs))
        terms += [jnp.where(odd, second, first), jnp.where(odd, first, second)]
    norm = functools.reduce(jnp.add, [t[rr_rows:rr_rows + 1] for t in terms])
    energy = functools.reduce(jnp.add, [t[rr_rows + 1:rr_rows + 2] for t in terms])
    for k in range(2 * chips):
        behind = k - 1 if k % 2 else (k + 3) % (2 * chips)
        stacked[k * span:(k + 1) * span] = terms[k][0:span]
        stacked[k * span:k * span + height] = terms[k][0:height] + terms[behind][span:span + height]
    coarse = stacked[...]
    high, low = halves(coarse)
    both = dot(k_high[...], jnp.concatenate([high, low], axis=1))
    values = both[:, 0:128] + both[:, 128:256] + dot(k_low[...], high)
    energy = energy + jnp.sum(coarse * values, axis=0, keepdims=True)

    table[...] = values

    def column(q):
        along = side[0] + q // count
        block = (2 * (-(along // 2)) + along % 2) % (2 * chips)
        at = block * span + (q % count) * height
        return table[pl.ds(pl.multiple_of(at, 8), height)]

    def tripled(q):
        high, low = halves(jnp.concatenate([column(q), column(q + 1)], axis=0))
        return jnp.concatenate([high, high, low], axis=0)

    own = [[None] * 4 for _ in range(count)]
    other = [[None] * 4 for _ in range(count)]
    for s in range(count):
        added = dot(ct_own[s], tripled(s))
        parts = [added[i * size:(i + 1) * size] for i in range(6)]
        raw = [near[s, 0:size], far[s], sides[s, 0], sides[s, 1]]
        own[s] = [raw[i] + parts[i] for i in range(4)]
        other[s][FAR] = from_far[s, 0:size] + parts[4]
        if NEAR in faces:
            other[s][NEAR] = from_near[s] + parts[5]
    other[count - 1][RIGHT] = from_right[0:size] + dot(ct_right[...], tripled(count))
    if LEFT in faces:
        other[0][LEFT] = from_left[...] + dot(ct_left[...], tripled(-1))
    for s in range(count):
        if s + 1 < count:
            other[s][RIGHT] = own[s + 1][LEFT]
        if s > 0:
            other[s][LEFT] = own[s - 1][RIGHT]
    result = [[None] * 4 for _ in range(count)]
    for s in range(count):
        for face in faces:
            shift = offsets[s, face]
            safe = jnp.maximum(shift, 0)
            start = safe if face in (NEAR, LEFT) else size - safe
            turned = rotated(scratch["turn"].at[s, face], other[s][face], start)
            result[s][face] = (own[s][face] - turned) * (shift >= 0).astype(F32)
    return result, norm, energy


def first_kernel(height, rr_rows, residual, from_near, from_left, inner, coupling, a_high, a_low, c_rows, *rest):
    outs, loads_out, split = rest[0:6], rest[6], rest[7]
    near, to_left = outs[0], outs[3]
    count, size = residual.shape[0], residual.shape[2]
    loads = []
    for s in range(count):
        left = from_left[0:size] if s == 0 else inner[s - 1]
        loads.append([from_near[s, 0:size], residual[s, 0], left, residual[s, 1]])
        for face in range(4):
            loads_out[s, face] = loads[s][face]
        put_coupling(near.at[s], size, coupling[s, :, NEAR * size:(NEAR + 1) * size], 0.0)
    put_coupling(to_left, size, coupling[0, :, LEFT * size:(LEFT + 1) * size], 0.0)
    apply_flexibility(loads, a_high, a_low, c_rows, height, outs, dict(split=split), rr_rows)


def step_kernel(which, height, rr_rows, *refs):
    refs = list(refs)
    take = lambda number: [refs.pop(0) for _ in range(number)]
    last = which == ITERS - 1
    (offsets,) = take(1)
    terms = take(3)
    matrix, spread, product, received = take(2), take(3), take(3), take(4)
    (loads,) = take(1)
    map_before, ways, found, scalars = (take(4) if which > 0 else [None] * 4)
    if not last:
        a_high, a_low, coupling = take(3)
        outs = take(6)
        loads_out, map_out = take(2)
        ways_out, found_out = take(2) if which > 0 else (None, None)
        (scalars_out,) = take(1)
        stack, values, turn, split = take(4)
        faces = (NEAR, FAR, LEFT, RIGHT)
    else:
        found_out, residual_out = take(2)
        stack, values, turn = take(3)
        faces = (FAR, RIGHT)
    count, size = loads.shape[0], loads.shape[2]
    scratch = dict(stack=stack, values=values, turn=turn)
    if not last:
        scratch["split"] = split
    mapped, norm, energy = finish_operator(
        offsets, terms, matrix, spread, product, received, height, rr_rows, scratch, faces
    )
    if which > 0:
        ratio = norm / scalars[0:1]
        energy = energy - ratio * norm / scalars[1:2]
    step = norm / energy
    fresh = [[None] * 4 for _ in range(count)]
    for s in range(count):
        for face in faces:
            here = mapped[s][face]
            now = loads[s, face]
            if which > 0:
                here = here + ratio * map_before[s, face]
            fresh[s][face] = now - step * here
            if not last:
                map_out[s, face] = here
                loads_out[s, face] = fresh[s][face]
            if face in (FAR, RIGHT):
                i = 0 if face == FAR else 1
                if which == 0:
                    continue
                if which == 1:
                    before = ways[s, face]
                    start = scalars[1:2] * before
                else:
                    before = ways[s, i]
                    start = found[s, i]
                way = now + ratio * before
                found_out[s, i] = start + step * way
                if last:
                    residual_out[s, i] = fresh[s][face]
                else:
                    ways_out[s, i] = way
    if not last:
        scalars_out[...] = jnp.concatenate([norm, step, jnp.zeros((6, 128), F32)], axis=0)
        apply_flexibility(fresh, a_high, a_low, coupling, height, outs, scratch, rr_rows)


def corner_tables(cuts, height):
    places = np.zeros((cuts + 2, 12, 2 * height), np.float32)
    for at in range(-1, cuts + 1):
        for k in range(4):
            cycle = at - 1 + k // 2
            if 0 <= cycle < cuts:
                for j in range(3):
                    places[at + 1, 3 * k + j, (k % 2) * height + 3 * cycle + j] = 1
    wide = 2 * height
    table = np.zeros((cuts + 2, 32, 3 * wide), np.float32)
    rows = np.zeros((cuts, 2 * wide, 32), np.float32)
    table[:, 0:12, 0:wide] = table[:, 16:28, wide:2 * wide] = table[:, 0:12, 2 * wide:] = places
    rows[:, 0:wide, 0:12] = rows[:, wide:, 16:28] = np.swapaxes(places[1:-1], 1, 2)
    return jnp.asarray(table, BF16), jnp.asarray(rows, BF16)


def corner_matrix(slots, numbers_at, cuts, height, odd):
    dofs = slots.shape[1]
    parts = chip_parts(summed(slots, "cuts"), "blk")
    mine = jnp.concatenate(parts, axis=0)
    theirs = swapped(mine, "blk")
    mine, theirs = (x.reshape(-1, slots.shape[0], dofs) for x in (mine, theirs))
    rows = jnp.stack([jnp.where(odd, theirs, mine), jnp.where(odd, mine, theirs)], axis=1)
    rows = rows.reshape(-1, height, dofs)
    numbers = rows[:, numbers_at, :cuts].astype(jnp.int32) - 1
    chosen = 3 * numbers[..., None] + jnp.arange(3, dtype=jnp.int32)
    chosen = jnp.pad(chosen.reshape(-1, 3 * cuts), ((0, 0), (0, height - 3 * cuts)), constant_values=-1).reshape(-1)
    pick = (jnp.arange(dofs, dtype=jnp.int32)[:, None] == chosen[None, :]).astype(BF16)
    used = (jnp.arange(height) < numbers_at)[:, None]
    high, low = kept_halves(jnp.where(used, rows, 0.0).reshape(-1, dofs))
    return [jnp.dot(part, pick, preferred_element_type=F32).astype(BF16) for part in (high, low)]


def per_device(gap_load, offsets, corner_map, flexibility, coupling, corner_rows):
    _, count, _, size, loads_n = gap_load.shape
    dofs = corner_rows.shape[-1]
    cuts, blocks = lax.axis_size("cuts"), lax.axis_size("blk")
    at = lax.axis_index("cuts").reshape(1)
    side = (lax.axis_index("blk") % 2).reshape(1)
    rr_rows = 3 * cuts
    height = -(-(rr_rows + 2) // 8) * 8
    gap, offsets, corner_map, flexibility, coupling, corner_rows = (
        x[0] for x in (gap_load, offsets, corner_map, flexibility, coupling, corner_rows)
    )
    total = flexibility.shape[1]
    below = 16 * (size // 128)
    shape = lambda *dims, kind=F32: jax.ShapeDtypeStruct(dims, kind)
    face = shape(size, loads_n)
    faces = shape(count, size, loads_n)
    pair = shape(count, 2, size, loads_n)
    four = shape(count, 4, size, loads_n)
    long_face = shape(size + below, loads_n)
    long_faces = shape(count, size + below, loads_n)
    table, rows_table = corner_tables(cuts, height)

    slots = pl.pallas_call(
        functools.partial(corner_kernel, cuts, height),
        out_shape=shape(count * height, dofs),
        in_specs=[SMEM, SMEM, VMEM],
        out_specs=VMEM,
        compiler_params=room(corner_rows, shape(count * height, dofs)),
        name="corner",
    )(at, corner_map, corner_rows)
    residual, to_far, to_right, inner, c_rows = pl.pallas_call(
        prepare_kernel,
        out_shape=(pair, long_faces, long_face, faces, shape(count, 4 * height, total, kind=BF16)),
        in_specs=[SMEM, SMEM] + [VMEM] * 3,
        out_specs=(VMEM,) * 5,
        scratch_shapes=[pltpu.VMEM((count, 2, 2 * size, loads_n), F32)],
        compiler_params=room(gap, coupling, rows_table, pair, pair, pair, long_faces, long_faces, faces, coupling),
        name="prepare",
    )(at, offsets, gap, coupling, rows_table)
    from_near = shifted(to_far, "cuts", 1, False)
    from_left = shifted(to_right, "blk", 1, True)
    k_high, k_low = corner_matrix(slots, rr_rows, cuts, height, side[0] == 1)
    a_high, a_low = pl.pallas_call(
        split_kernel,
        out_shape=(jax.ShapeDtypeStruct(flexibility.shape, BF16),) * 2,
        in_specs=[VMEM],
        out_specs=(VMEM, VMEM),
        compiler_params=room(flexibility, flexibility),
        cost_estimate=pl.CostEstimate(flops=0, bytes_accessed=8 * flexibility.size, transcendentals=0),
        name="split",
    )(flexibility)
    near_offsets = from_near[:, size + 12, 0]
    left_offsets = jnp.concatenate([from_left[size + 12:size + 13, 0], (offsets[:-1, 1] + 1).astype(F32)])
    all_offsets = jnp.stack([
        near_offsets.astype(jnp.int32) - 1, offsets[:, 0], left_offsets.astype(jnp.int32) - 1, offsets[:, 1]
    ], axis=1)

    flops = 2 * count * total * total * loads_n * 3
    cost = pl.CostEstimate(flops=flops, bytes_accessed=4 * flexibility.size, transcendentals=0)
    terms_shape = shape((count + 1) * height, loads_n)
    sends = (faces, faces, pair, face, face, terms_shape)
    first_sends = (long_faces, faces, pair, long_face, face, terms_shape)
    a_buffers = [pltpu.VMEM((count, total, 2 * loads_n), BF16)]
    f_buffers = [
        pltpu.VMEM((blocks * count * height, loads_n), F32),
        pltpu.VMEM((blocks * count * height, loads_n), F32),
        pltpu.VMEM((count, 4, 2 * size, loads_n), F32),
    ]
    first_args = (residual, from_near, from_left, inner, coupling, a_high, a_low, c_rows)
    *out, loads = pl.pallas_call(
        functools.partial(first_kernel, height, rr_rows),
        out_shape=first_sends + (four,),
        in_specs=[VMEM] * 8,
        out_specs=(VMEM,) * 7,
        scratch_shapes=a_buffers,
        compiler_params=room(*first_args, *first_sends, four, *a_buffers),
        cost_estimate=cost,
        name="first",
    )(*first_args)

    state = []
    for which in range(ITERS):
        last = which == ITERS - 1
        near, far, sides, to_left, to_right, terms = out
        pieces = [terms] + [shifted(terms, "cuts", k, True) for k in range(1, cuts)]
        terms, near = relay(sum_kernel, pieces, terms_shape, [near], f"sum{which}")
        r_far = shifted(near, "cuts", -1, False)
        pieces = chip_parts(terms, "blk")
        mine, far, to_left, to_right = relay(
            stack_kernel, pieces, shape(blocks // 2 * terms_shape.shape[0], loads_n), [far, to_left, to_right],
            f"stack{which}",
        )
        theirs = swapped(mine, "blk")
        r_right = shifted(to_left, "blk", -1, True)
        if last:
            r_near, r_left = far, to_right
        else:
            r_near = shifted(far, "cuts", 1, False)
            r_left = shifted(to_right, "blk", 1, True)
        if which == 0:
            ct_own, ct_left, ct_right = pl.pallas_call(
                spread_kernel,
                out_shape=(
                    shape(count, 6 * size, 6 * height, kind=BF16),
                    shape(size, 6 * height, kind=BF16),
                    shape(size, 6 * height, kind=BF16),
                ),
                in_specs=[SMEM] + [VMEM] * 6,
                out_specs=(VMEM,) * 3,
                compiler_params=room(coupling, from_near, r_far, from_left, r_right, table, *[faces] * 6),
                name="spread",
            )(at, coupling, from_near, r_far, from_left, r_right, table)
        args = [all_offsets, side, mine, theirs, k_high, k_low, ct_own, ct_left, ct_right, near, far, sides,
                r_near, r_far, r_left, r_right, loads, *state]
        specs = [SMEM, SMEM] + [VMEM] * (len(args) - 2)
        if last:
            outs, scratch = (pair, pair), f_buffers
        else:
            args += [a_high, a_low, c_rows]
            specs += [VMEM] * 3
            outs = sends + (four, four) + ((pair, pair) if which > 0 else ()) + (shape(8, loads_n),)
            scratch = f_buffers + a_buffers
        result = pl.pallas_call(
            functools.partial(step_kernel, which, height, rr_rows),
            out_shape=outs,
            in_specs=specs,
            out_specs=(VMEM,) * len(outs),
            scratch_shapes=scratch,
            compiler_params=room(*args[2:], *outs, *scratch),
            cost_estimate=None if last else cost,
            name=f"step{which}",
        )(*args)
        if last:
            multipliers, residual = result
            break
        out = result[0:6]
        before, loads = loads, result[6]
        if which == 0:
            state = [result[7], before, before, result[8]]
        else:
            state = [result[7], result[8], result[9], result[10]]
    return multipliers[None], residual[None]


def solution(mesh):
    spec5, spec4, spec3 = (P("cuts", "blk", *[None] * k) for k in (3, 2, 1))
    return jax.shard_map(
        per_device,
        mesh=mesh,
        in_specs=(spec5, spec3, spec3, spec4, spec4, spec4),
        out_specs=(spec5, spec5),
        check_vma=False,
    )
```

```python
import functools

import jax
import jax.numpy as jnp
import numpy as np
from jax import lax
from jax.experimental import pallas as pl
from jax.experimental.pallas import tpu as pltpu
from jax.sharding import PartitionSpec as P

ITERS = 3
NEAR, FAR, LEFT, RIGHT = range(4)
VMEM = pl.BlockSpec(memory_space=pltpu.VMEM)
SMEM = pl.BlockSpec(memory_space=pltpu.SMEM)
ANY = pl.BlockSpec(memory_space=pl.ANY)
F32, BF16 = jnp.float32, jnp.bfloat16


def shifted(value, axis, steps, wrap):
    count = lax.axis_size(axis)
    if wrap:
        pairs = [(source, (source + steps) % count) for source in range(count)]
    else:
        pairs = [(source, source + steps) for source in range(count) if 0 <= source + steps < count]
    return lax.ppermute(value, axis, pairs)


def summed(value, axis):
    others = [shifted(value, axis, k, True) for k in range(1, lax.axis_size(axis))]
    return functools.reduce(jnp.add, others, value)


def chip_parts(value, axis):
    count, stride = lax.axis_size(axis) // 2, 1
    parts = [value]
    while stride < count:
        radix = next((r for r in range(8, 1, -1) if (count // stride) % r == 0), count // stride)
        value = parts[0] if len(parts) == 1 else jnp.concatenate(parts, axis=0)
        parts = [value] + [shifted(value, axis, 2 * k * stride, True) for k in range(1, radix)]
        stride *= radix
    return parts


def swapped(value, axis):
    return lax.ppermute(value, axis, [(source, source ^ 1) for source in range(lax.axis_size(axis))])


def halves(value):
    high = value.astype(BF16)
    return high, (value - high.astype(F32)).astype(BF16)


def kept_halves(value):
    high = lax.reduce_precision(value, 8, 7)
    return high.astype(BF16), (value - high).astype(BF16)


def dot(first, second):
    return lax.dot_general(first, second, (((1,), (0,)), ((), ())), preferred_element_type=F32)


def rotated(buffer, value, start):
    size = value.shape[0]
    buffer[0:size] = value
    buffer[size:] = value
    return buffer[pl.ds(start, size)]


def put_coupling(ref, size, face, amount):
    for i in range(size // 128):
        rows = size + 16 * i
        ref[rows:rows + 12] = face[:, i * 128:(i + 1) * 128]
        ref[rows + 12:rows + 16] = jnp.full((4, 128), amount, F32)


def got_coupling(ref, size):
    return jnp.concatenate([ref[size + 16 * i:size + 16 * i + 12] for i in range(size // 128)], axis=1)


def prepare_kernel(cuts, at, *refs):
    sources, outs, buffer = refs[0:6], refs[6:13], refs[13]
    held, sems = refs[14:20], refs[20]
    residual, to_far, to_right, inner, c_rows, c_keep, corner = outs
    offsets, corner_map, gap, coupling, corner_rows, rows_table = held
    copies = [pltpu.make_async_copy(source, to, sems.at[i]) for i, (source, to) in enumerate(zip(sources, held))]
    for copy in copies:
        copy.start()
    for copy in copies:
        copy.wait()
    count, _, size, _ = gap.shape
    for s in range(count):
        for f in range(4):
            c_keep[s, :, f * size:(f + 1) * size] = coupling[:, s, f * size:(f + 1) * size]
    for s in range(count):
        for face in range(2):
            shift = offsets[s, face]
            value = gap[s, face] * (shift >= 0).astype(F32)
            residual[s, face] = value
            turned = -rotated(buffer.at[s, face], value, jnp.maximum(shift, 0))
            amount = (shift + 1).astype(F32)
            if face == 0:
                to_far[s, 0:size] = turned
                put_coupling(to_far.at[s], size, c_keep[s, :, FAR * size:(FAR + 1) * size], amount)
            elif s == count - 1:
                to_right[0:size] = turned
                put_coupling(to_right, size, c_keep[s, :, RIGHT * size:(RIGHT + 1) * size], amount)
            else:
                inner[s] = turned
        c_rows[s] = dot(rows_table[at[0]], paired(c_keep[s])).astype(BF16)
    inner[count - 1] = jnp.zeros(inner.shape[1:], F32)
    corner[...] = jnp.zeros_like(corner)
    dofs, rows = corner_rows.shape[2], 3 * cuts
    lanes = -(-dofs // 128)
    lane = lax.broadcasted_iota(jnp.int32, (1, 128), 1)
    number = jnp.zeros((1, 128), F32)
    for s in range(count):
        number = number + jnp.where(lane == at[0] * count + s, (corner_map[s, 2] + 1).astype(F32), 0.0)
        for i in range(lanes):
            wide = min(128, dofs - 128 * i)
            for a in range(cuts):
                keep = (at[0] == a).astype(F32)
                first = (s * lanes + i) * rows + 3 * a
                corner[first:first + 3, 0:wide] = corner_rows[6:9, s, 128 * i:128 * i + wide] * keep
    corner[corner.shape[0] - 8:corner.shape[0] - 7] = number


def paired(face):
    high, low = halves(face)
    rest = jnp.zeros((4, face.shape[1]), F32)
    both = jnp.concatenate([high.astype(F32), rest, low.astype(F32), rest], axis=0)
    return both.astype(BF16)


def spread_kernel(at, coupling, from_near, from_far, from_left, from_right, table, ct_own, ct_left, ct_right):
    count, size = coupling.shape[0], coupling.shape[2] // 4

    def turned(face, cycle):
        product = lax.dot_general(
            paired(face), table[cycle + 1], (((0,), (0,)), ((), ())), preferred_element_type=F32
        )
        return product.astype(BF16)

    for s in range(count):
        ct_own[s, 0:4 * size] = turned(coupling[s], at[0])
        ct_own[s, 4 * size:5 * size] = turned(got_coupling(from_far.at[s], size), at[0] + 1)
        ct_own[s, 5 * size:6 * size] = turned(got_coupling(from_near.at[s], size), at[0] - 1)
    ct_left[...] = turned(got_coupling(from_left, size), at[0])
    ct_right[...] = turned(got_coupling(from_right, size), at[0])


def sum_kernel(parts, *refs):
    refs[parts + (len(refs) - parts - 1) // 2][...] = functools.reduce(jnp.add, [r[...] for r in refs[:parts]])


def stack_kernel(parts, *refs):
    out = refs[parts + (len(refs) - parts - 1) // 2]
    size = refs[0].shape[0]
    for i in range(parts):
        out[i * size:(i + 1) * size] = refs[i][...]


def room(*shapes):
    total = 0
    for x in shapes:
        dims = (1, 1, *x.shape)
        total += int(np.prod(dims[:-2])) * -(-dims[-2] // 16) * 16 * -(-dims[-1] // 128) * 128 * np.dtype(x.dtype).itemsize
    return pltpu.CompilerParams(vmem_limit_bytes=total + 2 * 1024 * 1024)


def relay(kernel, parts, shape, through, name):
    specs = [VMEM] * len(parts) + [ANY] * len(through)
    return pl.pallas_call(
        functools.partial(kernel, len(parts)),
        out_shape=(jax.ShapeDtypeStruct(shape.shape, shape.dtype), *[jax.ShapeDtypeStruct(x.shape, x.dtype) for x in through]),
        in_specs=specs,
        out_specs=(VMEM, *[ANY] * len(through)),
        compiler_params=room(*parts, shape),
        input_output_aliases={len(parts) + i: 1 + i for i in range(len(through))},
        name=name,
    )(*parts, *through)


def apply_flexibility(loads, flexibility, coupling, height, outs, scratch, rr_rows):
    near, far, sides, to_left, to_right, terms = outs
    split, a_high, a_low = scratch["split"]
    count, size = len(loads), loads[0][0].shape[0]
    for s in range(count):
        for face in range(4):
            high, low = halves(loads[s][face])
            split[s, face * size:(face + 1) * size, 0:128] = high
            split[s, face * size:(face + 1) * size, 128:256] = low
    terms[...] = jnp.zeros_like(terms)
    total = jnp.zeros((1, 128), F32)
    width = coupling.shape[1] // 2
    for s in range(count):
        both = dot(coupling[s], split[s])
        mine = both[0:width, 0:128] + both[0:width, 128:256] + both[width:, 0:128]
        terms[s * height:s * height + width] += mine
    for s in range(count):
        for i in range(0, a_high.shape[1], size):
            a_high[s, i:i + size], a_low[s, i:i + size] = halves(flexibility[s, i:i + size])
        whole = dot(a_high[s], split[s])
        whole = whole[:, 0:128] + whole[:, 128:256] + dot(a_low[s], split[s, :, 0:128])
        for face in range(4):
            product = whole[face * size:(face + 1) * size]
            total = total + jnp.sum(product * loads[s][face], axis=0, keepdims=True)
            if face == NEAR:
                near[s, 0:size] = product
            elif face == FAR:
                far[s] = product
            else:
                sides[s, face - 2] = product
                if face == LEFT and s == 0:
                    to_left[0:size] = product
                if face == RIGHT and s == count - 1:
                    to_right[...] = product
    squares = jnp.zeros((1, 128), F32)
    for s in range(count):
        for face in (FAR, RIGHT):
            squares = squares + jnp.sum(loads[s][face] * loads[s][face], axis=0, keepdims=True)
    terms[rr_rows:rr_rows + 1] = squares
    terms[rr_rows + 1:rr_rows + 2] = total


def finish_operator(offsets, terms, matrix, spread, product, received, height, rr_rows, scratch, faces):
    k_high, k_low = matrix
    ct_own, ct_left, ct_right = spread
    near, far, sides = product
    from_near, from_far, from_left, from_right = received
    count, size = far.shape[0], far.shape[1]
    side, mine, theirs = terms
    odd = side[0] == 1
    stacked, table = scratch["stack"], scratch["values"]
    span = count * height
    chips = scratch["chips"]
    stride = mine.shape[0] // chips
    terms = [x[k * stride:k * stride + span + height] for x in (mine, theirs) for k in range(chips)]
    norm = functools.reduce(jnp.add, [t[rr_rows:rr_rows + 1] for t in terms])
    energy = functools.reduce(jnp.add, [t[rr_rows + 1:rr_rows + 2] for t in terms])
    for k in range(2 * chips):
        chip, swap = k % chips, k // chips
        near_by = terms[chip + (1 - swap) * chips][span:span + height]
        farther = terms[(chip + 1) % chips + (1 - swap) * chips][span:span + height]
        stacked[k * span:(k + 1) * span] = terms[k][0:span]
        if swap == 0:
            extra = jnp.where(odd, near_by, farther)
        else:
            extra = jnp.where(odd, farther, near_by)
        stacked[k * span:k * span + height] = terms[k][0:height] + extra
    coarse = stacked[...]
    high, low = halves(coarse)
    both = dot(k_high[...], jnp.concatenate([high, low], axis=1))
    values = both[:, 0:128] + both[:, 128:256] + dot(k_low[...], high)
    energy = energy + jnp.sum(coarse * values, axis=0, keepdims=True)

    table[...] = values

    def column(q):
        along = side[0] + q // count
        block = (-(along // 2)) % chips + jnp.where(along % 2 == side[0], 0, chips)
        at = block * span + (q % count) * height
        return table[pl.ds(pl.multiple_of(at, 8), height)]

    def tripled(q):
        high, low = halves(jnp.concatenate([column(q), column(q + 1)], axis=0))
        return jnp.concatenate([high, high, low], axis=0)

    own = [[None] * 4 for _ in range(count)]
    other = [[None] * 4 for _ in range(count)]
    for s in range(count):
        added = dot(ct_own[s], tripled(s))
        parts = [added[i * size:(i + 1) * size] for i in range(6)]
        raw = [near[s, 0:size], far[s], sides[s, 0], sides[s, 1]]
        own[s] = [raw[i] + parts[i] for i in range(4)]
        other[s][FAR] = from_far[s, 0:size] + parts[4]
        if NEAR in faces:
            other[s][NEAR] = from_near[s] + parts[5]
    other[count - 1][RIGHT] = from_right[0:size] + dot(ct_right[...], tripled(count))
    if LEFT in faces:
        other[0][LEFT] = from_left[...] + dot(ct_left[...], tripled(-1))
    for s in range(count):
        if s + 1 < count:
            other[s][RIGHT] = own[s + 1][LEFT]
        if s > 0:
            other[s][LEFT] = own[s - 1][RIGHT]
    result = [[None] * 4 for _ in range(count)]
    for s in range(count):
        for face in faces:
            shift = offsets[s, face]
            safe = jnp.maximum(shift, 0)
            start = safe if face in (NEAR, LEFT) else size - safe
            turned = rotated(scratch["turn"].at[s, face], other[s][face], start)
            result[s][face] = (own[s][face] - turned) * (shift >= 0).astype(F32)
    return result, norm, energy


def first_kernel(height, rr_rows, residual, from_near, from_left, inner, coupling, corner, flexibility, c_rows, *rest):
    outs, loads_out, split = rest[0:6], rest[6], rest[7:10]
    near, to_left, terms = outs[0], outs[3], outs[5]
    count, size = residual.shape[0], residual.shape[2]
    loads = []
    for s in range(count):
        left = from_left[0:size] if s == 0 else inner[s - 1]
        loads.append([from_near[s, 0:size], residual[s, 0], left, residual[s, 1]])
        for face in range(4):
            loads_out[s, face] = loads[s][face]
        put_coupling(near.at[s], size, coupling[s, :, NEAR * size:(NEAR + 1) * size], 0.0)
    put_coupling(to_left, size, coupling[0, :, LEFT * size:(LEFT + 1) * size], 0.0)
    apply_flexibility(loads, flexibility, c_rows, height, outs, dict(split=split), rr_rows)
    rows = corner.shape[0] - 8
    terms[(count + 1) * height:] = corner[0:rows]
    terms[rr_rows + 2:rr_rows + 3] = corner[rows:rows + 1]


def step_kernel(which, chips, height, rr_rows, *refs):
    refs = list(refs)
    take = lambda number: [refs.pop(0) for _ in range(number)]
    last = which == ITERS - 1
    (offsets,) = take(1)
    terms = take(3)
    matrix, spread, product, received = take(2), take(3), take(3), take(4)
    (loads,) = take(1)
    map_before, ways, found, scalars = (take(4) if which > 0 else [None] * 4)
    if not last:
        flexibility, coupling = take(2)
        outs = take(6)
        loads_out, map_out = take(2)
        ways_out, found_out = take(2) if which > 0 else (None, None)
        (scalars_out,) = take(1)
        stack, values, turn, *split = take(6)
        faces = (NEAR, FAR, LEFT, RIGHT)
    else:
        found_out, residual_out = take(2)
        stack, values, turn = take(3)
        faces = (FAR, RIGHT)
    count, size = loads.shape[0], loads.shape[2]
    scratch = dict(stack=stack, values=values, turn=turn, chips=chips)
    if not last:
        scratch["split"] = split
    mapped, norm, energy = finish_operator(
        offsets, terms, matrix, spread, product, received, height, rr_rows, scratch, faces
    )
    if which > 0:
        ratio = norm / scalars[0:1]
        energy = energy - ratio * norm / scalars[1:2]
    step = norm / energy
    fresh = [[None] * 4 for _ in range(count)]
    for s in range(count):
        for face in faces:
            here = mapped[s][face]
            now = loads[s, face]
            if which > 0:
                here = here + ratio * map_before[s, face]
            fresh[s][face] = now - step * here
            if not last:
                map_out[s, face] = here
                loads_out[s, face] = fresh[s][face]
            if face in (FAR, RIGHT):
                i = 0 if face == FAR else 1
                if which == 0:
                    continue
                if which == 1:
                    before = ways[s, face]
                    start = scalars[1:2] * before
                else:
                    before = ways[s, i]
                    start = found[s, i]
                way = now + ratio * before
                found_out[s, i] = start + step * way
                if last:
                    residual_out[s, i] = fresh[s][face]
                else:
                    ways_out[s, i] = way
    if not last:
        scalars_out[...] = jnp.concatenate([norm, step, jnp.zeros((6, 128), F32)], axis=0)
        apply_flexibility(fresh, flexibility, coupling, height, outs, scratch, rr_rows)


def corner_tables(cuts, height):
    places = np.zeros((cuts + 2, 12, 2 * height), np.float32)
    for at in range(-1, cuts + 1):
        for k in range(4):
            cycle = at - 1 + k // 2
            if 0 <= cycle < cuts:
                for j in range(3):
                    places[at + 1, 3 * k + j, (k % 2) * height + 3 * cycle + j] = 1
    wide = 2 * height
    table = np.zeros((cuts + 2, 32, 3 * wide), np.float32)
    rows = np.zeros((cuts, 2 * wide, 32), np.float32)
    table[:, 0:12, 0:wide] = table[:, 16:28, wide:2 * wide] = table[:, 0:12, 2 * wide:] = places
    rows[:, 0:wide, 0:12] = rows[:, wide:, 16:28] = np.swapaxes(places[1:-1], 1, 2)
    return jnp.asarray(table, BF16), jnp.asarray(rows, BF16)


def corner_matrix(sources, count, dofs, cuts, height):
    rows, lanes = 3 * cuts, -(-dofs // 128)
    first = (count + 1) * height
    numbers = jnp.concatenate([x[:, rows + 2, :cuts * count] for x in sources], axis=0).astype(jnp.int32) - 1
    numbers = jnp.swapaxes(numbers.reshape(-1, cuts, count), 1, 2)
    chosen = (3 * numbers[..., None] + jnp.arange(3, dtype=jnp.int32)).reshape(-1, rows)
    chosen = jnp.pad(chosen, ((0, 0), (0, height - rows)), constant_values=-1).reshape(-1)
    pick = (jnp.arange(128 * lanes, dtype=jnp.int32)[:, None] == chosen[None, :]).astype(BF16)
    pick = pick.reshape(lanes, 128, -1)
    found = [[], []]
    for x in sources:
        matrix = x[:, first:first + count * lanes * rows].reshape(-1, lanes, rows, 128)
        for half, into in zip(kept_halves(matrix), found):
            product = jnp.einsum("nlrd,ldc->nrc", half, pick, preferred_element_type=F32).astype(BF16)
            into.append(jnp.pad(product, ((0, 0), (0, height - rows), (0, 0))).reshape(-1, product.shape[-1]))
    return [jnp.concatenate(into, axis=0) for into in found]


def per_device(gap_load, offsets, corner_map, flexibility, coupling, corner_rows):
    _, count, _, size, loads_n = gap_load.shape
    dofs = corner_rows.shape[-1]
    cuts, blocks = lax.axis_size("cuts"), lax.axis_size("blk")
    at = lax.axis_index("cuts").reshape(1)
    side = (lax.axis_index("blk") % 2).reshape(1)
    rr_rows = 3 * cuts
    height = -(-(rr_rows + 3) // 8) * 8
    gap, offsets, corner_map, flexibility, coupling, corner_rows = (
        x[0] for x in (gap_load, offsets, corner_map, flexibility, coupling, corner_rows)
    )
    total = flexibility.shape[1]
    below = 16 * (size // 128)
    shape = lambda *dims, kind=F32: jax.ShapeDtypeStruct(dims, kind)
    face = shape(size, loads_n)
    faces = shape(count, size, loads_n)
    pair = shape(count, 2, size, loads_n)
    four = shape(count, 4, size, loads_n)
    long_face = shape(size + below, loads_n)
    long_faces = shape(count, size + below, loads_n)
    table, rows_table = corner_tables(cuts, height)

    corner_size = -(-(count * -(-dofs // 128) * rr_rows) // 8) * 8
    corner_shape = shape(corner_size + 8, loads_n)
    wide = shape(count, rr_rows, total)
    held = [
        pltpu.SMEM(offsets.shape, jnp.int32),
        pltpu.SMEM(corner_map.shape, jnp.int32),
        pltpu.VMEM(gap.shape, F32),
        pltpu.VMEM((12, count, total), F32),
        pltpu.VMEM((12, count, dofs), F32),
        pltpu.VMEM(rows_table.shape, BF16),
    ]
    prepared = (pair, long_faces, long_face, faces, shape(count, 4 * height, total, kind=BF16), shape(count, 12, total),
                corner_shape)
    residual, to_far, to_right, inner, c_rows, c_keep, corner = pl.pallas_call(
        functools.partial(prepare_kernel, cuts),
        out_shape=prepared,
        in_specs=[SMEM] + [ANY] * 6,
        out_specs=(VMEM,) * 7,
        scratch_shapes=[pltpu.VMEM((count, 2, 2 * size, loads_n), F32), *held, pltpu.SemaphoreType.DMA((6,))],
        compiler_params=room(*prepared, pair, pair, *held[2:]),
        name="prepare",
    )(at, offsets, corner_map, gap, jnp.swapaxes(coupling, 0, 1), jnp.swapaxes(corner_rows, 0, 1), rows_table)
    from_near = shifted(to_far, "cuts", 1, False)
    from_left = shifted(to_right, "blk", 1, True)
    near_offsets = from_near[:, size + 12, 0]
    left_offsets = jnp.concatenate([from_left[size + 12:size + 13, 0], (offsets[:-1, 1] + 1).astype(F32)])
    all_offsets = jnp.stack([
        near_offsets.astype(jnp.int32) - 1, offsets[:, 0], left_offsets.astype(jnp.int32) - 1, offsets[:, 1]
    ], axis=1)

    flops = 2 * count * total * total * loads_n * 3
    cost = pl.CostEstimate(flops=flops, bytes_accessed=4 * flexibility.size, transcendentals=0)
    terms_shape = shape((count + 1) * height, loads_n)
    sends = (faces, faces, pair, face, face, terms_shape)
    first_terms = shape((count + 1) * height + corner_size, loads_n)
    first_sends = (long_faces, faces, pair, long_face, face, first_terms)
    a_buffers = [pltpu.VMEM((count, total, 2 * loads_n), BF16)] + [pltpu.VMEM(flexibility.shape, BF16)] * 2
    f_buffers = [
        pltpu.VMEM((blocks * count * height, loads_n), F32),
        pltpu.VMEM((blocks * count * height, loads_n), F32),
        pltpu.VMEM((count, 4, 2 * size, loads_n), F32),
    ]
    first_args = (residual, from_near, from_left, inner, c_keep, corner, flexibility, c_rows)
    *out, loads = pl.pallas_call(
        functools.partial(first_kernel, height, rr_rows),
        out_shape=first_sends + (four,),
        in_specs=[VMEM] * 8,
        out_specs=(VMEM,) * 7,
        scratch_shapes=a_buffers,
        compiler_params=room(*first_args, *first_sends, four, *a_buffers),
        cost_estimate=cost,
        name="first",
    )(*first_args)

    state = []
    for which in range(ITERS):
        last = which == ITERS - 1
        near, far, sides, to_left, to_right, terms = out
        pieces = [terms] + [shifted(terms, "cuts", k, True) for k in range(1, cuts)]
        r_right = shifted(to_left, "blk", -1, True)
        through = [near, r_right]
        if not last:
            through.append(shifted(to_right, "blk", 1, True))
        terms, near, r_right, *r_left = relay(sum_kernel, pieces, terms, through, f"sum{which}")
        r_left = to_right if last else r_left[0]
        r_far = shifted(near, "cuts", -1, False)
        pieces = chip_parts(terms, "blk")
        mine, far = relay(
            stack_kernel, pieces, shape(blocks // 2 * terms.shape[0], loads_n), [far], f"stack{which}"
        )
        r_near = far if last else shifted(far, "cuts", 1, False)
        theirs = swapped(mine, "blk")
        if which == 0:
            stride = terms.shape[0]
            k_high, k_low = corner_matrix(
                [x.reshape(-1, stride, loads_n) for x in (mine, theirs)], count, dofs, cuts, height
            )
        if which == 0:
            ct_own, ct_left, ct_right = pl.pallas_call(
                spread_kernel,
                out_shape=(
                    shape(count, 6 * size, 6 * height, kind=BF16),
                    shape(size, 6 * height, kind=BF16),
                    shape(size, 6 * height, kind=BF16),
                ),
                in_specs=[SMEM] + [VMEM] * 6,
                out_specs=(VMEM,) * 3,
                compiler_params=room(c_keep, from_near, r_far, from_left, r_right, table, *[faces] * 6),
                name="spread",
            )(at, c_keep, from_near, r_far, from_left, r_right, table)
        args = [all_offsets, side, mine, theirs, k_high, k_low, ct_own, ct_left, ct_right, near, far, sides,
                r_near, r_far, r_left, r_right, loads, *state]
        specs = [SMEM, SMEM] + [VMEM] * (len(args) - 2)
        if last:
            outs, scratch = (pair, pair), f_buffers
        else:
            args += [flexibility, c_rows]
            specs += [VMEM] * 2
            outs = sends + (four, four) + ((pair, pair) if which > 0 else ()) + (shape(8, loads_n),)
            scratch = f_buffers + a_buffers
        result = pl.pallas_call(
            functools.partial(step_kernel, which, blocks // 2, height, rr_rows),
            out_shape=outs,
            in_specs=specs,
            out_specs=(VMEM,) * len(outs),
            scratch_shapes=scratch,
            compiler_params=room(*args[2:], *outs, *scratch),
            cost_estimate=None if last else cost,
            name=f"step{which}",
        )(*args)
        if last:
            multipliers, residual = result
            break
        out = result[0:6]
        before, loads = loads, result[6]
        if which == 0:
            state = [result[7], before, before, result[8]]
        else:
            state = [result[7], result[8], result[9], result[10]]
    return multipliers[None], residual[None]


def solution(mesh):
    spec5, spec4, spec3 = (P("cuts", "blk", *[None] * k) for k in (3, 2, 1))
    return jax.shard_map(
        per_device,
        mesh=mesh,
        in_specs=(spec5, spec3, spec3, spec4, spec4, spec4),
        out_specs=(spec5, spec5),
        check_vma=False,
    )
```

```python
import functools

import jax
import jax.numpy as jnp
import numpy as np
from jax import lax
from jax.experimental import pallas as pl
from jax.experimental.pallas import tpu as pltpu
from jax.sharding import PartitionSpec as P

ITERS = 3
NEAR, FAR, LEFT, RIGHT = range(4)
VMEM = pl.BlockSpec(memory_space=pltpu.VMEM)
SMEM = pl.BlockSpec(memory_space=pltpu.SMEM)
ANY = pl.BlockSpec(memory_space=pl.ANY)
HBM = pl.BlockSpec(memory_space=pltpu.HBM)
F32, BF16 = jnp.float32, jnp.bfloat16


def shifted(value, axis, steps, wrap):
    count = lax.axis_size(axis)
    if wrap:
        pairs = [(source, (source + steps) % count) for source in range(count)]
    else:
        pairs = [(source, source + steps) for source in range(count) if 0 <= source + steps < count]
    return lax.ppermute(value, axis, pairs)


def summed(value, axis):
    others = [shifted(value, axis, k, True) for k in range(1, lax.axis_size(axis))]
    return functools.reduce(jnp.add, others, value)


def chip_parts(value, axis):
    count, stride = lax.axis_size(axis) // 2, 1
    parts = [value]
    while stride < count:
        radix = next((r for r in range(8, 1, -1) if (count // stride) % r == 0), count // stride)
        value = parts[0] if len(parts) == 1 else jnp.concatenate(parts, axis=0)
        parts = [value] + [shifted(value, axis, 2 * k * stride, True) for k in range(1, radix)]
        stride *= radix
    return parts


def swapped(value, axis):
    return lax.ppermute(value, axis, [(source, source ^ 1) for source in range(lax.axis_size(axis))])


def halves(value):
    high = value.astype(BF16)
    return high, (value - high.astype(F32)).astype(BF16)


def dot(first, second):
    return lax.dot_general(first, second, (((1,), (0,)), ((), ())), preferred_element_type=F32)


def rotated(buffer, value, start):
    size = value.shape[0]
    buffer[0:size] = value
    buffer[size:] = value
    return buffer[pl.ds(start, size)]


def put_coupling(ref, size, face, amount):
    for i in range(size // 128):
        rows = size + 16 * i
        ref[rows:rows + 12] = face[:, i * 128:(i + 1) * 128]
        ref[rows + 12:rows + 16] = jnp.full((4, 128), amount, F32)


def got_coupling(ref, size):
    return jnp.concatenate([ref[size + 16 * i:size + 16 * i + 12] for i in range(size // 128)], axis=1)


def prepare_kernel(cuts, at, *refs):
    sources, outs, buffer = refs[0:6], refs[6:14], refs[14]
    held, sems = refs[15:21], refs[21]
    residual, to_far, to_right, inner, c_rows, c_keep, corner, own_offsets = outs
    offsets, corner_map, gap, coupling, corner_rows, rows_table = held
    copies = [pltpu.make_async_copy(source, to, sems.at[i]) for i, (source, to) in enumerate(zip(sources, held))]
    for copy in copies:
        copy.start()
    for copy in copies:
        copy.wait()
    count, _, size, _ = gap.shape
    for s in range(count):
        for f in range(4):
            c_keep[s, :, f * size:(f + 1) * size] = coupling[:, s, f * size:(f + 1) * size]
    for s in range(count):
        for face in range(2):
            shift = offsets[s, face]
            value = gap[s, face] * (shift >= 0).astype(F32)
            residual[s, face] = value
            turned = -rotated(buffer.at[s, face], value, jnp.maximum(shift, 0))
            amount = (shift + 1).astype(F32)
            if face == 0:
                to_far[s, 0:size] = turned
                put_coupling(to_far.at[s], size, c_keep[s, :, FAR * size:(FAR + 1) * size], amount)
            elif s == count - 1:
                to_right[0:size] = turned
                put_coupling(to_right, size, c_keep[s, :, RIGHT * size:(RIGHT + 1) * size], amount)
            else:
                inner[s] = turned
        c_rows[s] = dot(rows_table[at[0]], paired(c_keep[s])).astype(BF16)
    inner[count - 1] = jnp.zeros(inner.shape[1:], F32)
    corner[...] = jnp.zeros_like(corner)
    dofs, rows = corner_rows.shape[2], 3 * cuts
    lanes = dofs // 128 + 1
    lane = lax.broadcasted_iota(jnp.int32, (3, 128), 1)
    row = lax.broadcasted_iota(jnp.int32, (3, 128), 0)
    for s in range(count):
        number = (3 * corner_map[s, 2] + 1 + row).astype(F32)
        for i in range(lanes):
            wide = min(128, dofs - 128 * i)
            for a in range(cuts):
                keep = (at[0] == a).astype(F32)
                first = (s * lanes + i) * rows + 3 * a
                if wide > 0:
                    corner[first:first + 3, 0:wide] = corner_rows[6:9, s, 128 * i:128 * i + wide] * keep
                if i == lanes - 1:
                    before = corner[first:first + 3]
                    corner[first:first + 3] = jnp.where(lane == dofs % 128, number * keep, before)
    for s in range(count):
        for face in range(2):
            own_offsets[s, face] = offsets[s, face]


def matrix_kernel(cuts, dofs, height, count, chips, mine, theirs, k_high, k_low, rows, pick):
    used, lanes, stride = 3 * cuts, dofs // 128 + 1, mine.shape[0] // chips
    rows[...] = jnp.zeros_like(rows)
    for i, source in enumerate((mine, theirs)):
        for k in range(chips):
            for s in range(count):
                to = ((i * chips + k) * count + s) * height
                for l in range(lanes):
                    first = k * stride + (count + 1) * height + (s * lanes + l) * used
                    rows[to:to + used, 128 * l:128 * (l + 1)] = source[first:first + used]
    lane = lax.broadcasted_iota(jnp.int32, pick.shape, 1)
    number = rows[:, dofs:dofs + 1].astype(jnp.int32)
    pick[...] = jnp.where(lane + 1 == number, 1.0, 0.0).astype(BF16)
    tile = 256 if rows.shape[0] % 256 == 0 else rows.shape[0]

    @pl.loop(0, rows.shape[0] // tile)
    def _(t):
        at = pl.ds(pl.multiple_of(t * tile, tile), tile)
        for half, out in zip(halves(rows[at]), (k_high, k_low)):
            product = lax.dot_general(half, pick[...], (((1,), (1,)), ((), ())), preferred_element_type=F32)
            out[at] = product.astype(BF16)


def paired(face):
    high, low = halves(face)
    rest = jnp.zeros((4, face.shape[1]), F32)
    both = jnp.concatenate([high.astype(F32), rest, low.astype(F32), rest], axis=0)
    return both.astype(BF16)


def spread_kernel(at, own_offsets, coupling, from_near, from_far, from_left, from_right, table, ct_own, ct_left, ct_right, offsets):
    count, size = coupling.shape[0], coupling.shape[2] // 4

    def turned(face, cycle):
        product = lax.dot_general(
            paired(face), table[cycle + 1], (((0,), (0,)), ((), ())), preferred_element_type=F32
        )
        return product.astype(BF16)

    for s in range(count):
        ct_own[s, 0:4 * size] = turned(coupling[s], at[0])
        ct_own[s, 4 * size:5 * size] = turned(got_coupling(from_far.at[s], size), at[0] + 1)
        ct_own[s, 5 * size:6 * size] = turned(got_coupling(from_near.at[s], size), at[0] - 1)
    ct_left[...] = turned(got_coupling(from_left, size), at[0])
    ct_right[...] = turned(got_coupling(from_right, size), at[0])
    noted = lambda ref: jnp.max(ref[size + 12:size + 16]).astype(jnp.int32) - 1
    for s in range(count):
        offsets[s, NEAR] = noted(from_near.at[s])
        offsets[s, FAR] = own_offsets[s, 0]
        offsets[s, LEFT] = noted(from_left) if s == 0 else own_offsets[s - 1, 1]
        offsets[s, RIGHT] = own_offsets[s, 1]


def sum_kernel(parts, *refs):
    refs[parts + (len(refs) - parts - 1) // 2][...] = functools.reduce(jnp.add, [r[...] for r in refs[:parts]])


def stack_kernel(parts, *refs):
    out = refs[parts + (len(refs) - parts - 1) // 2]
    size = refs[0].shape[0]
    for i in range(parts):
        out[i * size:(i + 1) * size] = refs[i][...]


def room(*shapes):
    total = 0
    for x in shapes:
        dims = (1, 1, *x.shape)
        total += int(np.prod(dims[:-2])) * -(-dims[-2] // 16) * 16 * -(-dims[-1] // 128) * 128 * np.dtype(x.dtype).itemsize
    return pltpu.CompilerParams(vmem_limit_bytes=total + 2 * 1024 * 1024)


def relay(kernel, parts, shape, through, name):
    specs = [VMEM] * len(parts) + [ANY] * len(through)
    return pl.pallas_call(
        functools.partial(kernel, len(parts)),
        out_shape=(jax.ShapeDtypeStruct(shape.shape, shape.dtype), *[jax.ShapeDtypeStruct(x.shape, x.dtype) for x in through]),
        in_specs=specs,
        out_specs=(VMEM, *[ANY] * len(through)),
        compiler_params=room(*parts, shape),
        input_output_aliases={len(parts) + i: 1 + i for i in range(len(through))},
        name=name,
    )(*parts, *through)


def apply_flexibility(loads, fetched, coupling, height, outs, scratch, rr_rows):
    near, far, sides, to_left, to_right, terms = outs
    split, a_high, a_low, flexibility = scratch["split"][0:4]
    count, size = len(loads), loads[0][0].shape[0]
    for s in range(count):
        for face in range(4):
            high, low = halves(loads[s][face])
            split[s, face * size:(face + 1) * size, 0:128] = high
            split[s, face * size:(face + 1) * size, 128:256] = low
    terms[0:(count + 1) * height] = jnp.zeros(((count + 1) * height, 128), F32)
    total = jnp.zeros((1, 128), F32)
    width = coupling.shape[1] // 2
    for s in range(count):
        both = dot(coupling[s], split[s])
        mine = both[0:width, 0:128] + both[0:width, 128:256] + both[width:, 0:128]
        terms[s * height:s * height + width] += mine
    for s in range(count):
        for i in range(0, a_high.shape[1], size):
            fetched(s, i // size)
            a_high[s, i:i + size], a_low[s, i:i + size] = halves(flexibility[s, i:i + size])
        whole = dot(a_high[s], split[s])
        whole = whole[:, 0:128] + whole[:, 128:256] + dot(a_low[s], split[s, :, 0:128])
        for face in range(4):
            product = whole[face * size:(face + 1) * size]
            total = total + jnp.sum(product * loads[s][face], axis=0, keepdims=True)
            if face == NEAR:
                near[s, 0:size] = product
            elif face == FAR:
                far[s] = product
            else:
                sides[s, face - 2] = product
                if face == LEFT and s == 0:
                    to_left[0:size] = product
                if face == RIGHT and s == count - 1:
                    to_right[...] = product
    squares = jnp.zeros((1, 128), F32)
    for s in range(count):
        for face in (FAR, RIGHT):
            squares = squares + jnp.sum(loads[s][face] * loads[s][face], axis=0, keepdims=True)
    terms[rr_rows:rr_rows + 1] = squares
    terms[rr_rows + 1:rr_rows + 2] = total


def finish_operator(offsets, terms, matrix, spread, product, received, height, rr_rows, scratch, faces):
    k_high, k_low = matrix
    ct_own, ct_left, ct_right = spread
    near, far, sides = product
    from_near, from_far, from_left, from_right = received
    count, size = far.shape[0], far.shape[1]
    side, mine, theirs = terms
    odd = side[0] == 1
    stacked, table = scratch["stack"], scratch["values"]
    span = count * height
    chips = scratch["chips"]
    stride = mine.shape[0] // chips
    terms = [x[k * stride:k * stride + span + height] for x in (mine, theirs) for k in range(chips)]
    norm = functools.reduce(jnp.add, [t[rr_rows:rr_rows + 1] for t in terms])
    energy = functools.reduce(jnp.add, [t[rr_rows + 1:rr_rows + 2] for t in terms])
    for k in range(2 * chips):
        chip, swap = k % chips, k // chips
        near_by = terms[chip + (1 - swap) * chips][span:span + height]
        farther = terms[(chip + 1) % chips + (1 - swap) * chips][span:span + height]
        stacked[k * span:(k + 1) * span] = terms[k][0:span]
        if swap == 0:
            extra = jnp.where(odd, near_by, farther)
        else:
            extra = jnp.where(odd, farther, near_by)
        stacked[k * span:k * span + height] = terms[k][0:height] + extra
    coarse = stacked[...]
    high, low = halves(coarse)
    both = dot(k_high[...], jnp.concatenate([high, low], axis=1))
    values = both[:, 0:128] + both[:, 128:256] + dot(k_low[...], high)
    energy = energy + jnp.sum(coarse * values, axis=0, keepdims=True)

    table[...] = values

    def column(q):
        along = side[0] + q // count
        block = (-(along // 2)) % chips + jnp.where(along % 2 == side[0], 0, chips)
        at = block * span + (q % count) * height
        return table[pl.ds(pl.multiple_of(at, 8), height)]

    def tripled(q):
        high, low = halves(jnp.concatenate([column(q), column(q + 1)], axis=0))
        return jnp.concatenate([high, high, low], axis=0)

    own = [[None] * 4 for _ in range(count)]
    other = [[None] * 4 for _ in range(count)]
    for s in range(count):
        added = dot(ct_own[s], tripled(s))
        parts = [added[i * size:(i + 1) * size] for i in range(6)]
        raw = [near[s, 0:size], far[s], sides[s, 0], sides[s, 1]]
        own[s] = [raw[i] + parts[i] for i in range(4)]
        other[s][FAR] = from_far[s, 0:size] + parts[4]
        if NEAR in faces:
            other[s][NEAR] = from_near[s] + parts[5]
    other[count - 1][RIGHT] = from_right[0:size] + dot(ct_right[...], tripled(count))
    if LEFT in faces:
        other[0][LEFT] = from_left[...] + dot(ct_left[...], tripled(-1))
    for s in range(count):
        if s + 1 < count:
            other[s][RIGHT] = own[s + 1][LEFT]
        if s > 0:
            other[s][LEFT] = own[s - 1][RIGHT]
    result = [[None] * 4 for _ in range(count)]
    for s in range(count):
        for face in faces:
            shift = offsets[s, face]
            safe = jnp.maximum(shift, 0)
            start = safe if face in (NEAR, LEFT) else size - safe
            turned = rotated(scratch["turn"].at[s, face], other[s][face], start)
            result[s][face] = (own[s][face] - turned) * (shift >= 0).astype(F32)
    return result, norm, energy


def fetch(source, to, sems, size):
    copies = {}
    for s in range(source.shape[0]):
        for i in range(source.shape[1] // size):
            rows = pl.ds(i * size, size)
            copies[s, i] = pltpu.make_async_copy(source.at[s, rows], to.at[s, rows], sems.at[s, i])
            copies[s, i].start()
    return lambda s, i: copies[s, i].wait()


def first_kernel(height, rr_rows, residual, from_near, from_left, inner, coupling, corner, flexibility, c_rows, *rest):
    outs, loads_out, split = rest[0:6], rest[6], rest[7:12]
    near, to_left, terms = outs[0], outs[3], outs[5]
    count, size = residual.shape[0], residual.shape[2]
    fetched = fetch(flexibility, split[3], split[4], size)
    loads = []
    for s in range(count):
        left = from_left[0:size] if s == 0 else inner[s - 1]
        loads.append([from_near[s, 0:size], residual[s, 0], left, residual[s, 1]])
        for face in range(4):
            loads_out[s, face] = loads[s][face]
        put_coupling(near.at[s], size, coupling[s, :, NEAR * size:(NEAR + 1) * size], 0.0)
    put_coupling(to_left, size, coupling[0, :, LEFT * size:(LEFT + 1) * size], 0.0)
    apply_flexibility(loads, fetched, c_rows, height, outs, dict(split=split), rr_rows)
    terms[(count + 1) * height:] = corner[...]


def step_kernel(which, chips, height, rr_rows, *refs):
    refs = list(refs)
    take = lambda number: [refs.pop(0) for _ in range(number)]
    last = which == ITERS - 1
    (offsets,) = take(1)
    terms = take(3)
    matrix, spread, product, received = take(2), take(3), take(3), take(4)
    (loads,) = take(1)
    map_before, ways, found, scalars = (take(4) if which > 0 else [None] * 4)
    if not last:
        coupling, flexibility = take(2)
        outs = take(6)
        loads_out, map_out = take(2)
        ways_out, found_out = take(2) if which > 0 else (None, None)
        (scalars_out,) = take(1)
        stack, values, turn, *split = take(8)
        faces = (NEAR, FAR, LEFT, RIGHT)
    else:
        found_out, residual_out = take(2)
        stack, values, turn = take(3)
        faces = (FAR, RIGHT)
    count, size = loads.shape[0], loads.shape[2]
    scratch = dict(stack=stack, values=values, turn=turn, chips=chips)
    if not last:
        scratch["split"] = split
        fetched = fetch(flexibility, split[3], split[4], size)
    mapped, norm, energy = finish_operator(
        offsets, terms, matrix, spread, product, received, height, rr_rows, scratch, faces
    )
    if which > 0:
        ratio = norm / scalars[0:1]
        energy = energy - ratio * norm / scalars[1:2]
    step = norm / energy
    fresh = [[None] * 4 for _ in range(count)]
    for s in range(count):
        for face in faces:
            here = mapped[s][face]
            now = loads[s, face]
            if which > 0:
                here = here + ratio * map_before[s, face]
            fresh[s][face] = now - step * here
            if not last:
                map_out[s, face] = here
                loads_out[s, face] = fresh[s][face]
            if face in (FAR, RIGHT):
                i = 0 if face == FAR else 1
                if which == 0:
                    continue
                if which == 1:
                    before = ways[s, face]
                    start = scalars[1:2] * before
                else:
                    before = ways[s, i]
                    start = found[s, i]
                way = now + ratio * before
                found_out[s, i] = start + step * way
                if last:
                    residual_out[s, i] = fresh[s][face]
                else:
                    ways_out[s, i] = way
    if not last:
        scalars_out[...] = jnp.concatenate([norm, step, jnp.zeros((6, 128), F32)], axis=0)
        apply_flexibility(fresh, fetched, coupling, height, outs, scratch, rr_rows)


def corner_tables(cuts, height):
    places = np.zeros((cuts + 2, 12, 2 * height), np.float32)
    for at in range(-1, cuts + 1):
        for k in range(4):
            cycle = at - 1 + k // 2
            if 0 <= cycle < cuts:
                for j in range(3):
                    places[at + 1, 3 * k + j, (k % 2) * height + 3 * cycle + j] = 1
    wide = 2 * height
    table = np.zeros((cuts + 2, 32, 3 * wide), np.float32)
    rows = np.zeros((cuts, 2 * wide, 32), np.float32)
    table[:, 0:12, 0:wide] = table[:, 16:28, wide:2 * wide] = table[:, 0:12, 2 * wide:] = places
    rows[:, 0:wide, 0:12] = rows[:, wide:, 16:28] = np.swapaxes(places[1:-1], 1, 2)
    return jnp.asarray(table, BF16), jnp.asarray(rows, BF16)


def per_device(gap_load, offsets, corner_map, flexibility, coupling, corner_rows):
    _, count, _, size, loads_n = gap_load.shape
    dofs = corner_rows.shape[-1]
    cuts, blocks = lax.axis_size("cuts"), lax.axis_size("blk")
    at = lax.axis_index("cuts").reshape(1)
    side = (lax.axis_index("blk") % 2).reshape(1)
    rr_rows = 3 * cuts
    height = -(-(rr_rows + 2) // 8) * 8
    gap, offsets, corner_map, flexibility, coupling, corner_rows = (
        x[0] for x in (gap_load, offsets, corner_map, flexibility, coupling, corner_rows)
    )
    total = flexibility.shape[1]
    below = 16 * (size // 128)
    shape = lambda *dims, kind=F32: jax.ShapeDtypeStruct(dims, kind)
    face = shape(size, loads_n)
    faces = shape(count, size, loads_n)
    pair = shape(count, 2, size, loads_n)
    four = shape(count, 4, size, loads_n)
    long_face = shape(size + below, loads_n)
    long_faces = shape(count, size + below, loads_n)
    table, rows_table = corner_tables(cuts, height)

    corner_size = -(-(count * (dofs // 128 + 1) * rr_rows) // 8) * 8
    corner_shape = shape(corner_size, loads_n)
    wide = shape(count, rr_rows, total)
    held = [
        pltpu.SMEM(offsets.shape, jnp.int32),
        pltpu.SMEM(corner_map.shape, jnp.int32),
        pltpu.VMEM(gap.shape, F32),
        pltpu.VMEM((12, count, total), F32),
        pltpu.VMEM((12, count, dofs), F32),
        pltpu.VMEM(rows_table.shape, BF16),
    ]
    prepared = (pair, long_faces, long_face, faces, shape(count, 4 * height, total, kind=BF16), shape(count, 12, total),
                corner_shape)
    residual, to_far, to_right, inner, c_rows, c_keep, corner, own_offsets = pl.pallas_call(
        functools.partial(prepare_kernel, cuts),
        out_shape=prepared + (shape(count, 2, kind=jnp.int32),),
        in_specs=[SMEM] + [HBM] * 6,
        out_specs=(VMEM,) * 7 + (SMEM,),
        scratch_shapes=[pltpu.VMEM((count, 2, 2 * size, loads_n), F32), *held, pltpu.SemaphoreType.DMA((6,))],
        compiler_params=room(*prepared, pair, pair, *held[2:]),
        name="prepare",
    )(at, offsets, corner_map, gap, jnp.swapaxes(coupling, 0, 1), jnp.swapaxes(corner_rows, 0, 1), rows_table)
    from_near = shifted(to_far, "cuts", 1, False)
    from_left = shifted(to_right, "blk", 1, True)
    flops = 2 * count * total * total * loads_n * 3
    cost = pl.CostEstimate(flops=flops, bytes_accessed=4 * flexibility.size, transcendentals=0)
    terms_shape = shape((count + 1) * height, loads_n)
    sends = (faces, faces, pair, face, face, terms_shape)
    first_terms = shape((count + 1) * height + corner_size, loads_n)
    first_sends = (long_faces, faces, pair, long_face, face, first_terms)
    a_buffers = [pltpu.VMEM((count, total, 2 * loads_n), BF16)] + [pltpu.VMEM(flexibility.shape, BF16)] * 2 + [
        pltpu.VMEM(flexibility.shape, F32), pltpu.SemaphoreType.DMA((count, total // size))
    ]
    f_buffers = [
        pltpu.VMEM((blocks * count * height, loads_n), F32),
        pltpu.VMEM((blocks * count * height, loads_n), F32),
        pltpu.VMEM((count, 4, 2 * size, loads_n), F32),
    ]
    first_args = (residual, from_near, from_left, inner, c_keep, corner, flexibility, c_rows)
    *out, loads = pl.pallas_call(
        functools.partial(first_kernel, height, rr_rows),
        out_shape=first_sends + (four,),
        in_specs=[VMEM] * 6 + [HBM, VMEM],
        out_specs=(VMEM,) * 7,
        scratch_shapes=a_buffers,
        compiler_params=room(*first_args[:6], c_rows, *first_sends, four, *a_buffers[:-1]),
        cost_estimate=cost,
        name="first",
    )(*first_args)

    state = []
    for which in range(ITERS):
        last = which == ITERS - 1
        near, far, sides, to_left, to_right, terms = out
        pieces = [terms] + [shifted(terms, "cuts", k, True) for k in range(1, cuts)]
        r_right = shifted(to_left, "blk", -1, True)
        through = [near, r_right]
        if not last:
            through.append(shifted(to_right, "blk", 1, True))
        terms, near, r_right, *r_left = relay(sum_kernel, pieces, terms, through, f"sum{which}")
        r_left = to_right if last else r_left[0]
        r_far = shifted(near, "cuts", -1, False)
        pieces = chip_parts(terms, "blk")
        mine, far = relay(
            stack_kernel, pieces, shape(blocks // 2 * terms.shape[0], loads_n), [far], f"stack{which}"
        )
        r_near = far if last else shifted(far, "cuts", 1, False)
        theirs = swapped(mine, "blk")
        if which == 0:
            k_shape = shape(blocks * count * height, blocks * count * height, kind=BF16)
            held = [pltpu.VMEM((k_shape.shape[0], 128 * (dofs // 128 + 1)), kind) for kind in (F32, BF16)]
            k_high, k_low = pl.pallas_call(
                functools.partial(matrix_kernel, cuts, dofs, height, count, blocks // 2),
                out_shape=(k_shape, k_shape),
                in_specs=[VMEM] * 2,
                out_specs=(VMEM,) * 2,
                scratch_shapes=held,
                compiler_params=room(mine, theirs, k_shape, k_shape, *held),
                name="matrix",
            )(mine, theirs)
            ct_own, ct_left, ct_right, all_offsets = pl.pallas_call(
                spread_kernel,
                out_shape=(
                    shape(count, 6 * size, 6 * height, kind=BF16),
                    shape(size, 6 * height, kind=BF16),
                    shape(size, 6 * height, kind=BF16),
                    shape(count, 4, kind=jnp.int32),
                ),
                in_specs=[SMEM] * 2 + [VMEM] * 6,
                out_specs=(VMEM,) * 3 + (SMEM,),
                compiler_params=room(c_keep, from_near, r_far, from_left, r_right, table, *[faces] * 6),
                name="spread",
            )(at, own_offsets, c_keep, from_near, r_far, from_left, r_right, table)
        args = [all_offsets, side, mine, theirs, k_high, k_low, ct_own, ct_left, ct_right, near, far, sides,
                r_near, r_far, r_left, r_right, loads, *state]
        specs = [SMEM, SMEM] + [VMEM] * (len(args) - 2)
        if last:
            outs, scratch = (pair, pair), f_buffers
        else:
            args += [c_rows, flexibility]
            specs += [VMEM, HBM]
            outs = sends + (four, four) + ((pair, pair) if which > 0 else ()) + (shape(8, loads_n),)
            scratch = f_buffers + a_buffers
        result = pl.pallas_call(
            functools.partial(step_kernel, which, blocks // 2, height, rr_rows),
            out_shape=outs,
            in_specs=specs,
            out_specs=(VMEM,) * len(outs),
            scratch_shapes=scratch,
            compiler_params=room(*args[2:] if last else args[2:-1], *outs, *(scratch if last else scratch[:-1])),
            cost_estimate=None if last else cost,
            name=f"step{which}",
        )(*args)
        if last:
            multipliers, residual = result
            break
        out = result[0:6]
        before, loads = loads, result[6]
        if which == 0:
            state = [result[7], before, before, result[8]]
        else:
            state = [result[7], result[8], result[9], result[10]]
    return multipliers[None], residual[None]


def solution(mesh):
    spec5, spec4, spec3 = (P("cuts", "blk", *[None] * k) for k in (3, 2, 1))
    return jax.shard_map(
        per_device,
        mesh=mesh,
        in_specs=(spec5, spec3, spec3, spec4, spec4, spec4),
        out_specs=(spec5, spec5),
        check_vma=False,
    )
```

```python
import functools

import jax
import jax.numpy as jnp
import numpy as np
from jax import lax
from jax.experimental import pallas as pl
from jax.experimental.pallas import tpu as pltpu
from jax.sharding import PartitionSpec as P

ITERS = 3
NEAR, FAR, LEFT, RIGHT = range(4)
VMEM = pl.BlockSpec(memory_space=pltpu.VMEM)
SMEM = pl.BlockSpec(memory_space=pltpu.SMEM)
ANY = pl.BlockSpec(memory_space=pl.ANY)
HBM = pl.BlockSpec(memory_space=pltpu.HBM)
F32, BF16 = jnp.float32, jnp.bfloat16


def shifted(value, axis, steps, wrap):
    count = lax.axis_size(axis)
    if wrap:
        pairs = [(source, (source + steps) % count) for source in range(count)]
    else:
        pairs = [(source, source + steps) for source in range(count) if 0 <= source + steps < count]
    return lax.ppermute(value, axis, pairs)


def summed(value, axis):
    others = [shifted(value, axis, k, True) for k in range(1, lax.axis_size(axis))]
    return functools.reduce(jnp.add, others, value)


def chip_parts(value, axis):
    count, stride = lax.axis_size(axis) // 2, 1
    parts = [value]
    while stride < count:
        radix = next((r for r in range(8, 1, -1) if (count // stride) % r == 0), count // stride)
        value = parts[0] if len(parts) == 1 else jnp.concatenate(parts, axis=0)
        parts = [value] + [shifted(value, axis, 2 * k * stride, True) for k in range(1, radix)]
        stride *= radix
    return parts


def chip_neighbour(value, axis):
    count = lax.axis_size(axis)
    pairs = [(source, (source + (1 if source % 2 else -1)) % count) for source in range(count)]
    return lax.ppermute(value, axis, pairs)


def swapped(value, axis):
    return lax.ppermute(value, axis, [(source, source ^ 1) for source in range(lax.axis_size(axis))])


def halves(value):
    high = value.astype(BF16)
    return high, (value - high.astype(F32)).astype(BF16)


def dot(first, second):
    return lax.dot_general(first, second, (((1,), (0,)), ((), ())), preferred_element_type=F32)


def rotated(buffer, value, start):
    size = value.shape[0]
    buffer[0:size] = value
    buffer[size:] = value
    return buffer[pl.ds(start, size)]


def put_coupling(ref, size, face, amount):
    for i in range(size // 128):
        rows = size + 16 * i
        ref[rows:rows + 12] = face[:, i * 128:(i + 1) * 128]
        ref[rows + 12:rows + 16] = jnp.full((4, 128), amount, F32)


def got_coupling(ref, size):
    return jnp.concatenate([ref[size + 16 * i:size + 16 * i + 12] for i in range(size // 128)], axis=1)


def prepare_kernel(cuts, at, *refs):
    sources, outs, buffer = refs[0:6], refs[6:14], refs[14]
    held, sems = refs[15:21], refs[21]
    residual, to_far, to_right, inner, c_rows, c_keep, corner, own_offsets = outs
    offsets, corner_map, gap, coupling, corner_rows, rows_table = held
    copies = [pltpu.make_async_copy(source, to, sems.at[i]) for i, (source, to) in enumerate(zip(sources, held))]
    for copy in copies:
        copy.start()
    for copy in copies:
        copy.wait()
    count, _, size, _ = gap.shape
    for s in range(count):
        for f in range(4):
            c_keep[s, :, f * size:(f + 1) * size] = coupling[:, s, f * size:(f + 1) * size]
    for s in range(count):
        for face in range(2):
            shift = offsets[s, face]
            value = gap[s, face] * (shift >= 0).astype(F32)
            residual[s, face] = value
            turned = -rotated(buffer.at[s, face], value, jnp.maximum(shift, 0))
            amount = (shift + 1).astype(F32)
            if face == 0:
                to_far[s, 0:size] = turned
                put_coupling(to_far.at[s], size, c_keep[s, :, FAR * size:(FAR + 1) * size], amount)
            elif s == count - 1:
                to_right[0:size] = turned
                put_coupling(to_right, size, c_keep[s, :, RIGHT * size:(RIGHT + 1) * size], amount)
            else:
                inner[s] = turned
        c_rows[s] = dot(rows_table[at[0]], paired(c_keep[s])).astype(BF16)
    inner[count - 1] = jnp.zeros(inner.shape[1:], F32)
    corner[...] = jnp.zeros_like(corner)
    dofs, rows = corner_rows.shape[2], 3 * cuts
    lanes = dofs // 128 + 1
    lane = lax.broadcasted_iota(jnp.int32, (3, 128), 1)
    row = lax.broadcasted_iota(jnp.int32, (3, 128), 0)
    for s in range(count):
        number = (3 * corner_map[s, 2] + 1 + row).astype(F32)
        for i in range(lanes):
            wide = min(128, dofs - 128 * i)
            for a in range(cuts):
                keep = (at[0] == a).astype(F32)
                first = (s * lanes + i) * rows + 3 * a
                if wide > 0:
                    corner[first:first + 3, 0:wide] = corner_rows[6:9, s, 128 * i:128 * i + wide] * keep
                if i == lanes - 1:
                    before = corner[first:first + 3]
                    corner[first:first + 3] = jnp.where(lane == dofs % 128, number * keep, before)
    for s in range(count):
        for face in range(2):
            own_offsets[s, face] = offsets[s, face]


def matrix_kernel(cuts, dofs, height, count, chips, stride, mine, theirs, k_high, k_low, rows, pick):
    used, lanes = 3 * cuts, dofs // 128 + 1
    rows[...] = jnp.zeros_like(rows)
    for i, source in enumerate((mine, theirs)):
        for k in range(chips):
            for s in range(count):
                to = ((i * chips + k) * count + s) * height
                for l in range(lanes):
                    first = k * stride + (count + 1) * height + (s * lanes + l) * used
                    rows[to:to + used, 128 * l:128 * (l + 1)] = source[first:first + used]
    lane = lax.broadcasted_iota(jnp.int32, pick.shape, 1)
    number = rows[:, dofs:dofs + 1].astype(jnp.int32)
    pick[...] = jnp.where(lane + 1 == number, 1.0, 0.0).astype(BF16)
    tile = 256 if rows.shape[0] % 256 == 0 else rows.shape[0]

    @pl.loop(0, rows.shape[0] // tile)
    def _(t):
        at = pl.ds(pl.multiple_of(t * tile, tile), tile)
        for half, out in zip(halves(rows[at]), (k_high, k_low)):
            product = lax.dot_general(half, pick[...], (((1,), (1,)), ((), ())), preferred_element_type=F32)
            out[at] = product.astype(BF16)


def paired(face):
    high, low = halves(face)
    rest = jnp.zeros((4, face.shape[1]), F32)
    both = jnp.concatenate([high.astype(F32), rest, low.astype(F32), rest], axis=0)
    return both.astype(BF16)


def spread_kernel(stacked, at, side, own_offsets, coupling, from_near, from_far, from_left, across, theirs, table, ct_own, ct_left, ct_right, offsets):
    count, size = coupling.shape[0], coupling.shape[2] // 4

    def turned(face, cycle):
        product = lax.dot_general(
            paired(face), table[cycle + 1], (((0,), (0,)), ((), ())), preferred_element_type=F32
        )
        return product.astype(BF16)

    for s in range(count):
        ct_own[s, 0:4 * size] = turned(coupling[s], at[0])
        ct_own[s, 4 * size:5 * size] = turned(got_coupling(from_far.at[s], size), at[0] + 1)
        ct_own[s, 5 * size:6 * size] = turned(got_coupling(from_near.at[s], size), at[0] - 1)
    ct_left[...] = turned(got_coupling(from_left, size), at[0])
    inside = got_coupling(theirs.at[stacked:], size)
    ct_right[...] = turned(jnp.where(side[0] == 1, got_coupling(across, size), inside), at[0])
    noted = lambda ref: jnp.max(ref[size + 12:size + 16]).astype(jnp.int32) - 1
    for s in range(count):
        offsets[s, NEAR] = noted(from_near.at[s])
        offsets[s, FAR] = own_offsets[s, 0]
        offsets[s, LEFT] = noted(from_left) if s == 0 else own_offsets[s - 1, 1]
        offsets[s, RIGHT] = own_offsets[s, 1]


def split_kernel(block, *outs):
    for s in range(block.shape[0]):
        for i in range(0, block.shape[1], 256):
            for half, pair in zip(halves(block[s, i:i + 256]), (outs[0::2], outs[1::2])):
                for out in pair:
                    out[s, i:i + 256] = half


def sum_kernel(parts, *refs):
    refs[parts + (len(refs) - parts - 1) // 2][...] = functools.reduce(jnp.add, [r[...] for r in refs[:parts]])


def stack_kernel(parts, *refs):
    out = refs[parts + (len(refs) - parts - 1) // 2]
    at = 0
    for ref in refs[:parts]:
        out[at:at + ref.shape[0]] = ref[...]
        at += ref.shape[0]


def room(*shapes):
    total = 0
    for x in shapes:
        dims = (1, 1, *x.shape)
        total += int(np.prod(dims[:-2])) * -(-dims[-2] // 16) * 16 * -(-dims[-1] // 128) * 128 * np.dtype(x.dtype).itemsize
    return pltpu.CompilerParams(vmem_limit_bytes=total + 2 * 1024 * 1024)


def relay(kernel, parts, shape, through, name):
    specs = [VMEM] * len(parts) + [ANY] * len(through)
    return pl.pallas_call(
        functools.partial(kernel, len(parts)),
        out_shape=(jax.ShapeDtypeStruct(shape.shape, shape.dtype), *[jax.ShapeDtypeStruct(x.shape, x.dtype) for x in through]),
        in_specs=specs,
        out_specs=(VMEM, *[ANY] * len(through)),
        compiler_params=room(*parts, shape),
        input_output_aliases={len(parts) + i: 1 + i for i in range(len(through))},
        name=name,
    )(*parts, *through)


def apply_flexibility(loads, side, a_high, a_low, coupling, height, outs, split, rr_rows):
    near, far, sides, inside, across, terms = outs
    odd = side[0] == 1
    count, size = len(loads), loads[0][0].shape[0]
    for s in range(count):
        for face in range(4):
            high, low = halves(loads[s][face])
            split[s, face * size:(face + 1) * size, 0:128] = high
            split[s, face * size:(face + 1) * size, 128:256] = low
    terms[0:(count + 1) * height] = jnp.zeros(((count + 1) * height, 128), F32)
    total = jnp.zeros((1, 128), F32)
    width = coupling.shape[1] // 2
    for s in range(count):
        both = dot(coupling[s], split[s])
        mine = both[0:width, 0:128] + both[0:width, 128:256] + both[width:, 0:128]
        terms[s * height:s * height + width] += mine
    for s in range(count):
        whole = dot(a_high[s], split[s])
        whole = whole[:, 0:128] + whole[:, 128:256] + dot(a_low[s], split[s, :, 0:128])
        for face in range(4):
            product = whole[face * size:(face + 1) * size]
            total = total + jnp.sum(product * loads[s][face], axis=0, keepdims=True)
            if face == NEAR:
                near[s, 0:size] = product
            elif face == FAR:
                far[s] = product
            else:
                sides[s, face - 2] = product
    left, right = sides[0, 0], sides[count - 1, 1]
    inside[0:size] = jnp.where(odd, left, right)
    across[0:size] = jnp.where(odd, right, left)
    squares = jnp.zeros((1, 128), F32)
    for s in range(count):
        for face in (FAR, RIGHT):
            squares = squares + jnp.sum(loads[s][face] * loads[s][face], axis=0, keepdims=True)
    terms[rr_rows:rr_rows + 1] = squares
    terms[rr_rows + 1:rr_rows + 2] = total


def finish_operator(offsets, terms, matrix, spread, product, received, height, rr_rows, scratch, faces):
    k_high, k_low = matrix
    ct_own, ct_left, ct_right = spread
    near, far, sides = product
    from_near, from_far, across = received
    count, size = far.shape[0], far.shape[1]
    side, mine, theirs = terms
    odd = side[0] == 1
    stacked, table = scratch["stack"], scratch["values"]
    span = count * height
    chips, stride = scratch["chips"], scratch["stride"]
    inside, across = theirs[chips * stride:chips * stride + size], across[0:size]
    from_left, from_right = jnp.where(odd, inside, across), jnp.where(odd, across, inside)
    terms = [x[k * stride:k * stride + span + height] for x in (mine, theirs) for k in range(chips)]
    norm = functools.reduce(jnp.add, [t[rr_rows:rr_rows + 1] for t in terms])
    energy = functools.reduce(jnp.add, [t[rr_rows + 1:rr_rows + 2] for t in terms])
    for k in range(2 * chips):
        chip, swap = k % chips, k // chips
        near_by = terms[chip + (1 - swap) * chips][span:span + height]
        farther = terms[(chip + 1) % chips + (1 - swap) * chips][span:span + height]
        stacked[k * span:(k + 1) * span] = terms[k][0:span]
        if swap == 0:
            extra = jnp.where(odd, near_by, farther)
        else:
            extra = jnp.where(odd, farther, near_by)
        stacked[k * span:k * span + height] = terms[k][0:height] + extra
    coarse = stacked[...]
    high, low = halves(coarse)
    both = dot(k_high[...], jnp.concatenate([high, low], axis=1))
    values = both[:, 0:128] + both[:, 128:256] + dot(k_low[...], high)
    energy = energy + jnp.sum(coarse * values, axis=0, keepdims=True)

    table[...] = values

    def column(q):
        along = side[0] + q // count
        block = (-(along // 2)) % chips + jnp.where(along % 2 == side[0], 0, chips)
        at = block * span + (q % count) * height
        return table[pl.ds(pl.multiple_of(at, 8), height)]

    def tripled(q):
        high, low = halves(jnp.concatenate([column(q), column(q + 1)], axis=0))
        return jnp.concatenate([high, high, low], axis=0)

    own = [[None] * 4 for _ in range(count)]
    other = [[None] * 4 for _ in range(count)]
    for s in range(count):
        added = dot(ct_own[s], tripled(s))
        parts = [added[i * size:(i + 1) * size] for i in range(6)]
        raw = [near[s, 0:size], far[s], sides[s, 0], sides[s, 1]]
        own[s] = [raw[i] + parts[i] for i in range(4)]
        other[s][FAR] = from_far[s, 0:size] + parts[4]
        if NEAR in faces:
            other[s][NEAR] = from_near[s] + parts[5]
    other[count - 1][RIGHT] = from_right + dot(ct_right[...], tripled(count))
    if LEFT in faces:
        other[0][LEFT] = from_left + dot(ct_left[...], tripled(-1))
    for s in range(count):
        if s + 1 < count:
            other[s][RIGHT] = own[s + 1][LEFT]
        if s > 0:
            other[s][LEFT] = own[s - 1][RIGHT]
    result = [[None] * 4 for _ in range(count)]
    for s in range(count):
        for face in faces:
            shift = offsets[s, face]
            safe = jnp.maximum(shift, 0)
            start = safe if face in (NEAR, LEFT) else size - safe
            turned = rotated(scratch["turn"].at[s, face], other[s][face], start)
            result[s][face] = (own[s][face] - turned) * (shift >= 0).astype(F32)
    return result, norm, energy


def first_kernel(
    height, rr_rows, side, residual, from_near, from_left, inner, coupling, corner, a_high, a_low, c_rows, *rest
):
    outs, loads_out, split = rest[0:6], rest[6], rest[7]
    near, inside, across, terms = outs[0], outs[3], outs[4], outs[5]
    count, size = residual.shape[0], residual.shape[2]
    loads = []
    for s in range(count):
        left = from_left[0:size] if s == 0 else inner[s - 1]
        loads.append([from_near[s, 0:size], residual[s, 0], left, residual[s, 1]])
        for face in range(4):
            loads_out[s, face] = loads[s][face]
        put_coupling(near.at[s], size, coupling[s, :, NEAR * size:(NEAR + 1) * size], 0.0)
    for ref in (inside, across):
        put_coupling(ref, size, coupling[0, :, LEFT * size:(LEFT + 1) * size], 0.0)
    apply_flexibility(loads, side, a_high, a_low, c_rows, height, outs, split, rr_rows)
    terms[(count + 1) * height:] = corner[...]


def step_kernel(which, chips, stride, height, rr_rows, *refs):
    refs = list(refs)
    take = lambda number: [refs.pop(0) for _ in range(number)]
    last = which == ITERS - 1
    (offsets,) = take(1)
    terms = take(3)
    matrix, spread, product, received = take(2), take(3), take(3), take(3)
    (loads,) = take(1)
    map_before, ways, found, scalars = (take(4) if which > 0 else [None] * 4)
    if not last:
        a_high, a_low, coupling = take(3)
        outs = take(6)
        loads_out, map_out = take(2)
        ways_out, found_out = take(2) if which > 0 else (None, None)
        (scalars_out,) = take(1)
        stack, values, turn, split = take(4)
        faces = (NEAR, FAR, LEFT, RIGHT)
    else:
        found_out, residual_out = take(2)
        stack, values, turn = take(3)
        faces = (FAR, RIGHT)
    count, size = loads.shape[0], loads.shape[2]
    scratch = dict(stack=stack, values=values, turn=turn, chips=chips, stride=stride)
    mapped, norm, energy = finish_operator(
        offsets, terms, matrix, spread, product, received, height, rr_rows, scratch, faces
    )
    if which > 0:
        ratio = norm / scalars[0:1]
        energy = energy - ratio * norm / scalars[1:2]
    step = norm / energy
    fresh = [[None] * 4 for _ in range(count)]
    for s in range(count):
        for face in faces:
            here = mapped[s][face]
            now = loads[s, face]
            if which > 0:
                here = here + ratio * map_before[s, face]
            fresh[s][face] = now - step * here
            if not last:
                map_out[s, face] = here
                loads_out[s, face] = fresh[s][face]
            if face in (FAR, RIGHT):
                i = 0 if face == FAR else 1
                if which == 0:
                    continue
                if which == 1:
                    before = ways[s, face]
                    start = scalars[1:2] * before
                else:
                    before = ways[s, i]
                    start = found[s, i]
                way = now + ratio * before
                found_out[s, i] = start + step * way
                if last:
                    residual_out[s, i] = fresh[s][face]
                else:
                    ways_out[s, i] = way
    if not last:
        scalars_out[...] = jnp.concatenate([norm, step, jnp.zeros((6, 128), F32)], axis=0)
        apply_flexibility(fresh, terms[0], a_high, a_low, coupling, height, outs, split, rr_rows)


def corner_tables(cuts, height):
    places = np.zeros((cuts + 2, 12, 2 * height), np.float32)
    for at in range(-1, cuts + 1):
        for k in range(4):
            cycle = at - 1 + k // 2
            if 0 <= cycle < cuts:
                for j in range(3):
                    places[at + 1, 3 * k + j, (k % 2) * height + 3 * cycle + j] = 1
    wide = 2 * height
    table = np.zeros((cuts + 2, 32, 3 * wide), np.float32)
    rows = np.zeros((cuts, 2 * wide, 32), np.float32)
    table[:, 0:12, 0:wide] = table[:, 16:28, wide:2 * wide] = table[:, 0:12, 2 * wide:] = places
    rows[:, 0:wide, 0:12] = rows[:, wide:, 16:28] = np.swapaxes(places[1:-1], 1, 2)
    return jnp.asarray(table, BF16), jnp.asarray(rows, BF16)


def per_device(gap_load, offsets, corner_map, flexibility, coupling, corner_rows):
    _, count, _, size, loads_n = gap_load.shape
    dofs = corner_rows.shape[-1]
    cuts, blocks = lax.axis_size("cuts"), lax.axis_size("blk")
    at = lax.axis_index("cuts").reshape(1)
    side = (lax.axis_index("blk") % 2).reshape(1)
    rr_rows = 3 * cuts
    height = -(-(rr_rows + 2) // 8) * 8
    gap, offsets, corner_map, flexibility, coupling, corner_rows = (
        x[0] for x in (gap_load, offsets, corner_map, flexibility, coupling, corner_rows)
    )
    total = flexibility.shape[1]
    below = 16 * (size // 128)
    shape = lambda *dims, kind=F32: jax.ShapeDtypeStruct(dims, kind)
    face = shape(size, loads_n)
    faces = shape(count, size, loads_n)
    pair = shape(count, 2, size, loads_n)
    four = shape(count, 4, size, loads_n)
    long_face = shape(size + below, loads_n)
    long_faces = shape(count, size + below, loads_n)
    table, rows_table = corner_tables(cuts, height)

    corner_size = -(-(count * (dofs // 128 + 1) * rr_rows) // 8) * 8
    corner_shape = shape(corner_size, loads_n)
    wide = shape(count, rr_rows, total)
    held = [
        pltpu.SMEM(offsets.shape, jnp.int32),
        pltpu.SMEM(corner_map.shape, jnp.int32),
        pltpu.VMEM(gap.shape, F32),
        pltpu.VMEM((12, count, total), F32),
        pltpu.VMEM((12, count, dofs), F32),
        pltpu.VMEM(rows_table.shape, BF16),
    ]
    prepared = (pair, long_faces, long_face, faces, shape(count, 4 * height, total, kind=BF16), shape(count, 12, total),
                corner_shape)
    residual, to_far, to_right, inner, c_rows, c_keep, corner, own_offsets = pl.pallas_call(
        functools.partial(prepare_kernel, cuts),
        out_shape=prepared + (shape(count, 2, kind=jnp.int32),),
        in_specs=[SMEM] + [HBM] * 6,
        out_specs=(VMEM,) * 7 + (SMEM,),
        scratch_shapes=[pltpu.VMEM((count, 2, 2 * size, loads_n), F32), *held, pltpu.SemaphoreType.DMA((6,))],
        compiler_params=room(*prepared, pair, pair, *held[2:]),
        name="prepare",
    )(at, offsets, corner_map, gap, jnp.swapaxes(coupling, 0, 1), jnp.swapaxes(corner_rows, 0, 1), rows_table)
    from_near = shifted(to_far, "cuts", 1, False)
    from_left = shifted(to_right, "blk", 1, True)
    a_shape = jax.ShapeDtypeStruct(flexibility.shape, BF16)
    first_high, first_low, a_high, a_low = pl.pallas_call(
        split_kernel,
        out_shape=(a_shape,) * 4,
        in_specs=[VMEM],
        out_specs=(VMEM,) * 4,
        compiler_params=room(flexibility, *[a_shape] * 4),
        cost_estimate=pl.CostEstimate(flops=0, bytes_accessed=12 * flexibility.size, transcendentals=0),
        name="split",
    )(flexibility)

    flops = 2 * count * total * total * loads_n * 3
    cost = pl.CostEstimate(flops=flops, bytes_accessed=4 * flexibility.size, transcendentals=0)
    terms_shape = shape((count + 1) * height, loads_n)
    sends = (faces, faces, pair, face, face, terms_shape)
    first_terms = shape((count + 1) * height + corner_size, loads_n)
    first_sends = (long_faces, faces, pair, long_face, long_face, first_terms)
    a_buffers = [pltpu.VMEM((count, total, 2 * loads_n), BF16)]
    f_buffers = [
        pltpu.VMEM((blocks * count * height, loads_n), F32),
        pltpu.VMEM((blocks * count * height, loads_n), F32),
        pltpu.VMEM((count, 4, 2 * size, loads_n), F32),
    ]
    first_args = (side, residual, from_near, from_left, inner, c_keep, corner, first_high, first_low, c_rows)
    *out, loads = pl.pallas_call(
        functools.partial(first_kernel, height, rr_rows),
        out_shape=first_sends + (four,),
        in_specs=[SMEM] + [VMEM] * 9,
        out_specs=(VMEM,) * 7,
        scratch_shapes=a_buffers,
        compiler_params=room(*first_args[1:], *first_sends, four, *a_buffers),
        cost_estimate=cost,
        name="first",
    )(*first_args)

    state = []
    for which in range(ITERS):
        last = which == ITERS - 1
        near, far, sides, inside, across, terms = out
        pieces = [terms] + [shifted(terms, "cuts", k, True) for k in range(1, cuts)]
        across = chip_neighbour(across, "blk")
        terms, near, across = relay(sum_kernel, pieces, terms, [near, across], f"sum{which}")
        r_far = shifted(near, "cuts", -1, False)
        pieces = chip_parts(terms, "blk")
        stacked = blocks // 2 * terms.shape[0]
        mine, far = relay(
            stack_kernel, [*pieces, inside], shape(stacked + inside.shape[0], loads_n), [far], f"stack{which}"
        )
        r_near = far if last else shifted(far, "cuts", 1, False)
        theirs = swapped(mine, "blk")
        if which == 0:
            k_shape = shape(blocks * count * height, blocks * count * height, kind=BF16)
            held = [pltpu.VMEM((k_shape.shape[0], 128 * (dofs // 128 + 1)), kind) for kind in (F32, BF16)]
            k_high, k_low = pl.pallas_call(
                functools.partial(matrix_kernel, cuts, dofs, height, count, blocks // 2, terms.shape[0]),
                out_shape=(k_shape, k_shape),
                in_specs=[VMEM] * 2,
                out_specs=(VMEM,) * 2,
                scratch_shapes=held,
                compiler_params=room(mine, theirs, k_shape, k_shape, *held),
                name="matrix",
            )(mine, theirs)
            ct_own, ct_left, ct_right, all_offsets = pl.pallas_call(
                functools.partial(spread_kernel, stacked),
                out_shape=(
                    shape(count, 6 * size, 6 * height, kind=BF16),
                    shape(size, 6 * height, kind=BF16),
                    shape(size, 6 * height, kind=BF16),
                    shape(count, 4, kind=jnp.int32),
                ),
                in_specs=[SMEM] * 3 + [VMEM] * 7,
                out_specs=(VMEM,) * 3 + (SMEM,),
                compiler_params=room(c_keep, from_near, r_far, from_left, across, theirs, table, *[faces] * 6),
                name="spread",
            )(at, side, own_offsets, c_keep, from_near, r_far, from_left, across, theirs, table)
        args = [all_offsets, side, mine, theirs, k_high, k_low, ct_own, ct_left, ct_right, near, far, sides,
                r_near, r_far, across, loads, *state]
        specs = [SMEM, SMEM] + [VMEM] * (len(args) - 2)
        if last:
            outs, scratch = (pair, pair), f_buffers
        else:
            args += [a_high, a_low, c_rows]
            specs += [VMEM] * 3
            outs = sends + (four, four) + ((pair, pair) if which > 0 else ()) + (shape(8, loads_n),)
            scratch = f_buffers + a_buffers
        result = pl.pallas_call(
            functools.partial(step_kernel, which, blocks // 2, terms.shape[0], height, rr_rows),
            out_shape=outs,
            in_specs=specs,
            out_specs=(VMEM,) * len(outs),
            scratch_shapes=scratch,
            compiler_params=room(*args[2:], *outs, *scratch),
            cost_estimate=None if last else cost,
            name=f"step{which}",
        )(*args)
        if last:
            multipliers, residual = result
            break
        out = result[0:6]
        before, loads = loads, result[6]
        if which == 0:
            state = [result[7], before, before, result[8]]
        else:
            state = [result[7], result[8], result[9], result[10]]
    return multipliers[None], residual[None]


def solution(mesh):
    spec5, spec4, spec3 = (P("cuts", "blk", *[None] * k) for k in (3, 2, 1))
    return jax.shard_map(
        per_device,
        mesh=mesh,
        in_specs=(spec5, spec3, spec3, spec4, spec4, spec4),
        out_specs=(spec5, spec5),
        check_vma=False,
    )
```

```python
import functools

import jax
import jax.numpy as jnp
import numpy as np
from jax import lax
from jax.experimental import pallas as pl
from jax.experimental.pallas import tpu as pltpu
from jax.sharding import PartitionSpec as P

ITERS = 3
NEAR, FAR, LEFT, RIGHT = range(4)
VMEM = pl.BlockSpec(memory_space=pltpu.VMEM)
SMEM = pl.BlockSpec(memory_space=pltpu.SMEM)
ANY = pl.BlockSpec(memory_space=pl.ANY)
HBM = pl.BlockSpec(memory_space=pltpu.HBM)
F32, BF16 = jnp.float32, jnp.bfloat16


def shifted(value, axis, steps, wrap):
    count = lax.axis_size(axis)
    if wrap:
        pairs = [(source, (source + steps) % count) for source in range(count)]
    else:
        pairs = [(source, source + steps) for source in range(count) if 0 <= source + steps < count]
    return lax.ppermute(value, axis, pairs)


def summed(value, axis):
    others = [shifted(value, axis, k, True) for k in range(1, lax.axis_size(axis))]
    return functools.reduce(jnp.add, others, value)


def chip_parts(value, axis):
    count, stride = lax.axis_size(axis) // 2, 1
    parts = [value]
    while stride < count:
        radix = next((r for r in range(8, 1, -1) if (count // stride) % r == 0), count // stride)
        value = parts[0] if len(parts) == 1 else jnp.concatenate(parts, axis=0)
        parts = [value] + [shifted(value, axis, 2 * k * stride, True) for k in range(1, radix)]
        stride *= radix
    return parts


def chip_neighbour(value, axis):
    count = lax.axis_size(axis)
    pairs = [(source, (source + (1 if source % 2 else -1)) % count) for source in range(count)]
    return lax.ppermute(value, axis, pairs)


def swapped(value, axis):
    return lax.ppermute(value, axis, [(source, source ^ 1) for source in range(lax.axis_size(axis))])


def halves(value):
    high = value.astype(BF16)
    return high, (value - high.astype(F32)).astype(BF16)


def dot(first, second):
    return lax.dot_general(first, second, (((1,), (0,)), ((), ())), preferred_element_type=F32)


def rotated(buffer, value, start):
    size = value.shape[0]
    buffer[0:size] = value
    buffer[size:] = value
    return buffer[pl.ds(start, size)]


def put_coupling(ref, size, face, amount):
    for i in range(size // 128):
        rows = size + 16 * i
        ref[rows:rows + 12] = face[:, i * 128:(i + 1) * 128]
        ref[rows + 12:rows + 16] = jnp.full((4, 128), amount, F32)


def got_coupling(ref, size):
    return jnp.concatenate([ref[size + 16 * i:size + 16 * i + 12] for i in range(size // 128)], axis=1)


def prepare_kernel(cuts, at, *refs):
    sources, outs, buffer = refs[0:5], refs[5:13], refs[13]
    held, sems, wide = refs[14:19], refs[19], refs[20]
    residual, to_far, to_right, inner, c_rows, c_keep, corner, own_offsets = outs
    offsets, corner_map, gap, coupling, corner_rows = held
    copies = [pltpu.make_async_copy(source, to, sems.at[i]) for i, (source, to) in enumerate(zip(sources, held))]
    for copy in copies:
        copy.start()
    for copy in copies:
        copy.wait()
    count, _, size, _ = gap.shape
    for s in range(count):
        for f in range(4):
            c_keep[s, :, f * size:(f + 1) * size] = coupling[:, s, f * size:(f + 1) * size]
    for s in range(count):
        for face in range(2):
            shift = offsets[s, face]
            value = gap[s, face] * (shift >= 0).astype(F32)
            residual[s, face] = value
            turned = -rotated(buffer.at[s, face], value, jnp.maximum(shift, 0))
            amount = (shift + 1).astype(F32)
            if face == 0:
                to_far[s, 0:size] = turned
                put_coupling(to_far.at[s], size, c_keep[s, :, FAR * size:(FAR + 1) * size], amount)
            elif s == count - 1:
                to_right[0:size] = turned
                put_coupling(to_right, size, c_keep[s, :, RIGHT * size:(RIGHT + 1) * size], amount)
            else:
                inner[s] = turned
    width = wide.shape[1] // 2
    wide[...] = jnp.zeros_like(wide)
    for a in range(cuts):

        @pl.when(at[0] == a)
        def _():
            for s in range(count):
                for k in range(4):
                    to = (k % 2) * width + 3 * (a - 1 + k // 2)
                    if a - 1 + k // 2 >= 0:
                        wide[s, to:to + 3] = c_keep[s, 3 * k:3 * k + 3]

    for s in range(count):
        c_rows[s, 0:2 * width], c_rows[s, 2 * width:] = halves(wide[s])
    inner[count - 1] = jnp.zeros(inner.shape[1:], F32)
    corner[...] = jnp.zeros_like(corner)
    dofs, rows = corner_rows.shape[2], 3 * cuts
    lanes = dofs // 128 + 1
    lane = lax.broadcasted_iota(jnp.int32, (3, 128), 1)
    row = lax.broadcasted_iota(jnp.int32, (3, 128), 0)
    for s in range(count):
        number = (3 * corner_map[s, 2] + 1 + row).astype(F32)
        for i in range(lanes):
            wide = min(128, dofs - 128 * i)
            for a in range(cuts):
                keep = (at[0] == a).astype(F32)
                first = (s * lanes + i) * rows + 3 * a
                if wide > 0:
                    corner[first:first + 3, 0:wide] = corner_rows[6:9, s, 128 * i:128 * i + wide] * keep
                if i == lanes - 1:
                    before = corner[first:first + 3]
                    corner[first:first + 3] = jnp.where(lane == dofs % 128, number * keep, before)
    for s in range(count):
        for face in range(2):
            own_offsets[s, face] = offsets[s, face]


def matrix_kernel(cuts, dofs, height, count, chips, stride, mine, theirs, k_high, k_low, rows, pick):
    used, lanes = 3 * cuts, dofs // 128 + 1
    rows[...] = jnp.zeros_like(rows)
    for i, source in enumerate((mine, theirs)):
        for k in range(chips):
            for s in range(count):
                to = ((i * chips + k) * count + s) * height
                for l in range(lanes):
                    first = k * stride + (count + 1) * height + (s * lanes + l) * used
                    rows[to:to + used, 128 * l:128 * (l + 1)] = source[first:first + used]
    lane = lax.broadcasted_iota(jnp.int32, pick.shape, 1)
    number = rows[:, dofs:dofs + 1].astype(jnp.int32)
    pick[...] = jnp.where(lane + 1 == number, 1.0, 0.0).astype(BF16)
    tile = 256 if rows.shape[0] % 256 == 0 else rows.shape[0]

    @pl.loop(0, rows.shape[0] // tile)
    def _(t):
        at = pl.ds(pl.multiple_of(t * tile, tile), tile)
        for half, out in zip(halves(rows[at]), (k_high, k_low)):
            product = lax.dot_general(half, pick[...], (((1,), (1,)), ((), ())), preferred_element_type=F32)
            out[at] = product.astype(BF16)


def paired(face):
    high, low = halves(face)
    rest = jnp.zeros((4, face.shape[1]), F32)
    both = jnp.concatenate([high.astype(F32), rest, low.astype(F32), rest], axis=0)
    return both.astype(BF16)


def spread_kernel(stacked, at, side, own_offsets, coupling, from_near, from_far, from_left, across, theirs, table, ct_own, ct_left, ct_right, offsets):
    count, size = coupling.shape[0], coupling.shape[2] // 4

    def turned(face, cycle):
        product = lax.dot_general(
            paired(face), table[cycle + 1], (((0,), (0,)), ((), ())), preferred_element_type=F32
        )
        return product.astype(BF16)

    for s in range(count):
        ct_own[s, 0:4 * size] = turned(coupling[s], at[0])
        ct_own[s, 4 * size:5 * size] = turned(got_coupling(from_far.at[s], size), at[0] + 1)
        ct_own[s, 5 * size:6 * size] = turned(got_coupling(from_near.at[s], size), at[0] - 1)
    ct_left[...] = turned(got_coupling(from_left, size), at[0])
    inside = got_coupling(theirs.at[stacked:], size)
    ct_right[...] = turned(jnp.where(side[0] == 1, got_coupling(across, size), inside), at[0])
    noted = lambda ref: jnp.max(ref[size + 12:size + 16]).astype(jnp.int32) - 1
    for s in range(count):
        offsets[s, NEAR] = noted(from_near.at[s])
        offsets[s, FAR] = own_offsets[s, 0]
        offsets[s, LEFT] = noted(from_left) if s == 0 else own_offsets[s - 1, 1]
        offsets[s, RIGHT] = own_offsets[s, 1]


def beside(value):
    return jnp.concatenate(halves(value), axis=1)


def three_passes(first, second):
    high, low = halves(first)
    both = dot(high, second)
    return both[:, 0:128] + both[:, 128:256] + dot(low, second[:, 0:128])


def own_kernel(residual, flexibility, product):
    count, size = residual.shape[0], residual.shape[2]
    for s in range(count):
        total = None
        for i, face in enumerate((FAR, RIGHT)):
            part = three_passes(flexibility[s, :, face * size:(face + 1) * size], beside(residual[s, i]))
            total = part if total is None else total + part
        product[s] = total


def sum_kernel(parts, *refs):
    refs[parts + (len(refs) - parts - 1) // 2][...] = functools.reduce(jnp.add, [r[...] for r in refs[:parts]])


def stack_kernel(parts, *refs):
    out = refs[parts + (len(refs) - parts - 1) // 2]
    at = 0
    for ref in refs[:parts]:
        out[at:at + ref.shape[0]] = ref[...]
        at += ref.shape[0]


def room(*shapes):
    total = 0
    for x in shapes:
        dims = (1, 1, *x.shape)
        total += int(np.prod(dims[:-2])) * -(-dims[-2] // 16) * 16 * -(-dims[-1] // 128) * 128 * np.dtype(x.dtype).itemsize
    return pltpu.CompilerParams(vmem_limit_bytes=total + 2 * 1024 * 1024)


def relay(kernel, parts, shape, through, name):
    specs = [VMEM] * len(parts) + [ANY] * len(through)
    return pl.pallas_call(
        functools.partial(kernel, len(parts)),
        out_shape=(jax.ShapeDtypeStruct(shape.shape, shape.dtype), *[jax.ShapeDtypeStruct(x.shape, x.dtype) for x in through]),
        in_specs=specs,
        out_specs=(VMEM, *[ANY] * len(through)),
        compiler_params=room(*parts, shape),
        input_output_aliases={len(parts) + i: 1 + i for i in range(len(through))},
        name=name,
    )(*parts, *through)


def apply_flexibility(loads, side, flexibility, known, coupling, height, outs, split, rr_rows):
    near, far, sides, inside, across, terms = outs
    odd = side[0] == 1
    count, size = len(loads), loads[0][0].shape[0]
    for s in range(count):
        for face in range(4):
            high, low = halves(loads[s][face])
            split[s, face * size:(face + 1) * size, 0:128] = high
            split[s, face * size:(face + 1) * size, 128:256] = low
    terms[0:(count + 1) * height] = jnp.zeros(((count + 1) * height, 128), F32)
    total = jnp.zeros((1, 128), F32)
    width = coupling.shape[1] // 2
    for s in range(count):
        both = dot(coupling[s], split[s])
        mine = both[0:width, 0:128] + both[0:width, 128:256] + both[width:, 0:128]
        terms[s * height:s * height + width] += mine
    for s in range(count):
        if known is None:
            whole = three_passes(flexibility[s], split[s])
        else:
            whole = known[s]
            for face in (NEAR, LEFT):
                part = slice(face * size, (face + 1) * size)
                whole = whole + three_passes(flexibility[s, :, part], split[s, part])
        for face in range(4):
            product = whole[face * size:(face + 1) * size]
            total = total + jnp.sum(product * loads[s][face], axis=0, keepdims=True)
            if face == NEAR:
                near[s, 0:size] = product
            elif face == FAR:
                far[s] = product
            else:
                sides[s, face - 2] = product
    left, right = sides[0, 0], sides[count - 1, 1]
    inside[0:size] = jnp.where(odd, left, right)
    across[0:size] = jnp.where(odd, right, left)
    squares = jnp.zeros((1, 128), F32)
    for s in range(count):
        for face in (FAR, RIGHT):
            squares = squares + jnp.sum(loads[s][face] * loads[s][face], axis=0, keepdims=True)
    terms[rr_rows:rr_rows + 1] = squares
    terms[rr_rows + 1:rr_rows + 2] = total


def finish_operator(offsets, terms, matrix, spread, product, received, height, rr_rows, scratch, faces):
    k_high, k_low = matrix
    ct_own, ct_left, ct_right = spread
    near, far, sides = product
    from_near, from_far, across = received
    count, size = far.shape[0], far.shape[1]
    side, mine, theirs = terms
    odd = side[0] == 1
    stacked, table = scratch["stack"], scratch["values"]
    span = count * height
    chips, stride = scratch["chips"], scratch["stride"]
    inside, across = theirs[chips * stride:chips * stride + size], across[0:size]
    from_left, from_right = jnp.where(odd, inside, across), jnp.where(odd, across, inside)
    terms = [x[k * stride:k * stride + span + height] for x in (mine, theirs) for k in range(chips)]
    norm = functools.reduce(jnp.add, [t[rr_rows:rr_rows + 1] for t in terms])
    energy = functools.reduce(jnp.add, [t[rr_rows + 1:rr_rows + 2] for t in terms])
    for k in range(2 * chips):
        chip, swap = k % chips, k // chips
        near_by = terms[chip + (1 - swap) * chips][span:span + height]
        farther = terms[(chip + 1) % chips + (1 - swap) * chips][span:span + height]
        stacked[k * span:(k + 1) * span] = terms[k][0:span]
        if swap == 0:
            extra = jnp.where(odd, near_by, farther)
        else:
            extra = jnp.where(odd, farther, near_by)
        stacked[k * span:k * span + height] = terms[k][0:height] + extra
    coarse = stacked[...]
    high, low = halves(coarse)
    both = dot(k_high[...], jnp.concatenate([high, low], axis=1))
    values = both[:, 0:128] + both[:, 128:256] + dot(k_low[...], high)
    energy = energy + jnp.sum(coarse * values, axis=0, keepdims=True)

    table[...] = values

    def column(q):
        along = side[0] + q // count
        block = (-(along // 2)) % chips + jnp.where(along % 2 == side[0], 0, chips)
        at = block * span + (q % count) * height
        return table[pl.ds(pl.multiple_of(at, 8), height)]

    def tripled(q):
        high, low = halves(jnp.concatenate([column(q), column(q + 1)], axis=0))
        return jnp.concatenate([high, high, low], axis=0)

    own = [[None] * 4 for _ in range(count)]
    other = [[None] * 4 for _ in range(count)]
    for s in range(count):
        added = dot(ct_own[s], tripled(s))
        parts = [added[i * size:(i + 1) * size] for i in range(6)]
        raw = [near[s, 0:size], far[s], sides[s, 0], sides[s, 1]]
        own[s] = [raw[i] + parts[i] for i in range(4)]
        other[s][FAR] = from_far[s, 0:size] + parts[4]
        if NEAR in faces:
            other[s][NEAR] = from_near[s] + parts[5]
    other[count - 1][RIGHT] = from_right + dot(ct_right[...], tripled(count))
    if LEFT in faces:
        other[0][LEFT] = from_left + dot(ct_left[...], tripled(-1))
    for s in range(count):
        if s + 1 < count:
            other[s][RIGHT] = own[s + 1][LEFT]
        if s > 0:
            other[s][LEFT] = own[s - 1][RIGHT]
    result = [[None] * 4 for _ in range(count)]
    for s in range(count):
        for face in faces:
            shift = offsets[s, face]
            safe = jnp.maximum(shift, 0)
            start = safe if face in (NEAR, LEFT) else size - safe
            turned = rotated(scratch["turn"].at[s, face], other[s][face], start)
            result[s][face] = (own[s][face] - turned) * (shift >= 0).astype(F32)
    return result, norm, energy


def first_kernel(
    height, rr_rows, side, residual, from_near, from_left, inner, coupling, corner, known, flexibility, c_rows, *rest
):
    outs, loads_out, split = rest[0:6], rest[6], rest[7]
    near, inside, across, terms = outs[0], outs[3], outs[4], outs[5]
    count, size = residual.shape[0], residual.shape[2]
    loads = []
    for s in range(count):
        left = from_left[0:size] if s == 0 else inner[s - 1]
        loads.append([from_near[s, 0:size], residual[s, 0], left, residual[s, 1]])
        for face in range(4):
            loads_out[s, face] = loads[s][face]
        put_coupling(near.at[s], size, coupling[s, :, NEAR * size:(NEAR + 1) * size], 0.0)
    for ref in (inside, across):
        put_coupling(ref, size, coupling[0, :, LEFT * size:(LEFT + 1) * size], 0.0)
    apply_flexibility(loads, side, flexibility, known, c_rows, height, outs, split, rr_rows)
    terms[(count + 1) * height:] = corner[...]


def step_kernel(which, chips, stride, height, rr_rows, *refs):
    refs = list(refs)
    take = lambda number: [refs.pop(0) for _ in range(number)]
    last = which == ITERS - 1
    (offsets,) = take(1)
    terms = take(3)
    matrix, spread, product, received = take(2), take(3), take(3), take(3)
    (loads,) = take(1)
    map_before, ways, found, scalars = (take(4) if which > 0 else [None] * 4)
    if not last:
        flexibility, coupling = take(2)
        outs = take(6)
        loads_out, map_out = take(2)
        ways_out, found_out = take(2) if which > 0 else (None, None)
        (scalars_out,) = take(1)
        stack, values, turn, split = take(4)
        faces = (NEAR, FAR, LEFT, RIGHT)
    else:
        found_out, residual_out = take(2)
        stack, values, turn = take(3)
        faces = (FAR, RIGHT)
    count, size = loads.shape[0], loads.shape[2]
    scratch = dict(stack=stack, values=values, turn=turn, chips=chips, stride=stride)
    mapped, norm, energy = finish_operator(
        offsets, terms, matrix, spread, product, received, height, rr_rows, scratch, faces
    )
    if which > 0:
        ratio = norm / scalars[0:1]
        energy = energy - ratio * norm / scalars[1:2]
    step = norm / energy
    fresh = [[None] * 4 for _ in range(count)]
    for s in range(count):
        for face in faces:
            here = mapped[s][face]
            now = loads[s, face]
            if which > 0:
                here = here + ratio * map_before[s, face]
            fresh[s][face] = now - step * here
            if not last:
                map_out[s, face] = here
                loads_out[s, face] = fresh[s][face]
            if face in (FAR, RIGHT):
                i = 0 if face == FAR else 1
                if which == 0:
                    continue
                if which == 1:
                    before = ways[s, face]
                    start = scalars[1:2] * before
                else:
                    before = ways[s, i]
                    start = found[s, i]
                way = now + ratio * before
                found_out[s, i] = start + step * way
                if last:
                    residual_out[s, i] = fresh[s][face]
                else:
                    ways_out[s, i] = way
    if not last:
        scalars_out[...] = jnp.concatenate([norm, step, jnp.zeros((6, 128), F32)], axis=0)
        apply_flexibility(fresh, terms[0], flexibility, None, coupling, height, outs, split, rr_rows)


def corner_tables(cuts, height):
    places = np.zeros((cuts + 2, 12, 2 * height), np.float32)
    for at in range(-1, cuts + 1):
        for k in range(4):
            cycle = at - 1 + k // 2
            if 0 <= cycle < cuts:
                for j in range(3):
                    places[at + 1, 3 * k + j, (k % 2) * height + 3 * cycle + j] = 1
    wide = 2 * height
    table = np.zeros((cuts + 2, 32, 3 * wide), np.float32)
    table[:, 0:12, 0:wide] = table[:, 16:28, wide:2 * wide] = table[:, 0:12, 2 * wide:] = places
    return jnp.asarray(table, BF16)


def per_device(gap_load, offsets, corner_map, flexibility, coupling, corner_rows):
    _, count, _, size, loads_n = gap_load.shape
    dofs = corner_rows.shape[-1]
    cuts, blocks = lax.axis_size("cuts"), lax.axis_size("blk")
    at = lax.axis_index("cuts").reshape(1)
    side = (lax.axis_index("blk") % 2).reshape(1)
    rr_rows = 3 * cuts
    height = -(-(rr_rows + 2) // 8) * 8
    gap, offsets, corner_map, flexibility, coupling, corner_rows = (
        x[0] for x in (gap_load, offsets, corner_map, flexibility, coupling, corner_rows)
    )
    total = flexibility.shape[1]
    below = 16 * (size // 128)
    shape = lambda *dims, kind=F32: jax.ShapeDtypeStruct(dims, kind)
    face = shape(size, loads_n)
    faces = shape(count, size, loads_n)
    pair = shape(count, 2, size, loads_n)
    four = shape(count, 4, size, loads_n)
    long_face = shape(size + below, loads_n)
    long_faces = shape(count, size + below, loads_n)
    table = corner_tables(cuts, height)

    corner_size = -(-(count * (dofs // 128 + 1) * rr_rows) // 8) * 8
    corner_shape = shape(corner_size, loads_n)
    wide = shape(count, rr_rows, total)
    held = [
        pltpu.SMEM(offsets.shape, jnp.int32),
        pltpu.SMEM(corner_map.shape, jnp.int32),
        pltpu.VMEM(gap.shape, F32),
        pltpu.VMEM((12, count, total), F32),
        pltpu.VMEM((12, count, dofs), F32),
    ]
    prepared = (pair, long_faces, long_face, faces, shape(count, 4 * height, total, kind=BF16), shape(count, 12, total),
                corner_shape)
    residual, to_far, to_right, inner, c_rows, c_keep, corner, own_offsets = pl.pallas_call(
        functools.partial(prepare_kernel, cuts),
        out_shape=prepared + (shape(count, 2, kind=jnp.int32),),
        in_specs=[SMEM] + [HBM] * 5,
        out_specs=(VMEM,) * 7 + (SMEM,),
        scratch_shapes=[pltpu.VMEM((count, 2, 2 * size, loads_n), F32), *held, pltpu.SemaphoreType.DMA((5,)),
                        pltpu.VMEM((count, 2 * height, total), F32)],
        compiler_params=room(*prepared, pair, pair, *held[2:], shape(count, 2 * height, total)),
        name="prepare",
    )(at, offsets, corner_map, gap, jnp.swapaxes(coupling, 0, 1), jnp.swapaxes(corner_rows, 0, 1))
    from_near = shifted(to_far, "cuts", 1, False)
    from_left = shifted(to_right, "blk", 1, True)
    own_shape = shape(count, total, loads_n)
    own_part = pl.pallas_call(
        own_kernel,
        out_shape=own_shape,
        in_specs=[VMEM] * 2,
        out_specs=VMEM,
        compiler_params=room(residual, flexibility, flexibility, own_shape),
        cost_estimate=pl.CostEstimate(
            flops=3 * count * total * total * loads_n, bytes_accessed=4 * flexibility.size, transcendentals=0
        ),
        name="own",
    )(residual, flexibility)

    flops = 2 * count * total * total * loads_n * 3
    cost = pl.CostEstimate(flops=flops, bytes_accessed=4 * flexibility.size, transcendentals=0)
    terms_shape = shape((count + 1) * height, loads_n)
    sends = (faces, faces, pair, face, face, terms_shape)
    first_terms = shape((count + 1) * height + corner_size, loads_n)
    first_sends = (long_faces, faces, pair, long_face, long_face, first_terms)
    a_buffers = [pltpu.VMEM((count, total, 2 * loads_n), BF16)]
    f_buffers = [
        pltpu.VMEM((blocks * count * height, loads_n), F32),
        pltpu.VMEM((blocks * count * height, loads_n), F32),
        pltpu.VMEM((count, 4, 2 * size, loads_n), F32),
    ]
    first_args = (side, residual, from_near, from_left, inner, c_keep, corner, own_part, flexibility, c_rows)
    *out, loads = pl.pallas_call(
        functools.partial(first_kernel, height, rr_rows),
        out_shape=first_sends + (four,),
        in_specs=[SMEM] + [VMEM] * 9,
        out_specs=(VMEM,) * 7,
        scratch_shapes=a_buffers,
        compiler_params=room(*first_args[1:], *first_sends, four, flexibility, *a_buffers),
        cost_estimate=cost,
        name="first",
    )(*first_args)

    state = []
    for which in range(ITERS):
        last = which == ITERS - 1
        near, far, sides, inside, across, terms = out
        pieces = [terms] + [shifted(terms, "cuts", k, True) for k in range(1, cuts)]
        terms, near = relay(sum_kernel, pieces, terms, [near], f"sum{which}")
        r_far = shifted(near, "cuts", -1, False)
        pieces = chip_parts(terms, "blk")
        stacked = blocks // 2 * terms.shape[0]
        mine, far, across = relay(
            stack_kernel, [*pieces, inside], shape(stacked + inside.shape[0], loads_n), [far, across], f"stack{which}"
        )
        across = chip_neighbour(across, "blk")
        r_near = far if last else shifted(far, "cuts", 1, False)
        theirs = swapped(mine, "blk")
        if which == 0:
            k_shape = shape(blocks * count * height, blocks * count * height, kind=BF16)
            held = [pltpu.VMEM((k_shape.shape[0], 128 * (dofs // 128 + 1)), kind) for kind in (F32, BF16)]
            k_high, k_low = pl.pallas_call(
                functools.partial(matrix_kernel, cuts, dofs, height, count, blocks // 2, terms.shape[0]),
                out_shape=(k_shape, k_shape),
                in_specs=[VMEM] * 2,
                out_specs=(VMEM,) * 2,
                scratch_shapes=held,
                compiler_params=room(mine, theirs, k_shape, k_shape, *held),
                name="matrix",
            )(mine, theirs)
            ct_own, ct_left, ct_right, all_offsets = pl.pallas_call(
                functools.partial(spread_kernel, stacked),
                out_shape=(
                    shape(count, 6 * size, 6 * height, kind=BF16),
                    shape(size, 6 * height, kind=BF16),
                    shape(size, 6 * height, kind=BF16),
                    shape(count, 4, kind=jnp.int32),
                ),
                in_specs=[SMEM] * 3 + [VMEM] * 7,
                out_specs=(VMEM,) * 3 + (SMEM,),
                compiler_params=room(c_keep, from_near, r_far, from_left, across, theirs, table, *[faces] * 6),
                name="spread",
            )(at, side, own_offsets, c_keep, from_near, r_far, from_left, across, theirs, table)
        args = [all_offsets, side, mine, theirs, k_high, k_low, ct_own, ct_left, ct_right, near, far, sides,
                r_near, r_far, across, loads, *state]
        specs = [SMEM, SMEM] + [VMEM] * (len(args) - 2)
        if last:
            outs, scratch = (pair, pair), f_buffers
        else:
            args += [flexibility, c_rows]
            specs += [VMEM] * 2
            outs = sends + (four, four) + ((pair, pair) if which > 0 else ()) + (shape(8, loads_n),)
            scratch = f_buffers + a_buffers
        result = pl.pallas_call(
            functools.partial(step_kernel, which, blocks // 2, terms.shape[0], height, rr_rows),
            out_shape=outs,
            in_specs=specs,
            out_specs=(VMEM,) * len(outs),
            scratch_shapes=scratch,
            compiler_params=room(*args[2:], *outs, *scratch, *([] if last else [flexibility])),
            cost_estimate=None if last else cost,
            name=f"step{which}",
        )(*args)
        if last:
            multipliers, residual = result
            break
        out = result[0:6]
        before, loads = loads, result[6]
        if which == 0:
            state = [result[7], before, before, result[8]]
        else:
            state = [result[7], result[8], result[9], result[10]]
    return multipliers[None], residual[None]


def solution(mesh):
    spec5, spec4, spec3 = (P("cuts", "blk", *[None] * k) for k in (3, 2, 1))
    return jax.shard_map(
        per_device,
        mesh=mesh,
        in_specs=(spec5, spec3, spec3, spec4, spec4, spec4),
        out_specs=(spec5, spec5),
        check_vma=False,
    )
```

```python
import functools

import jax
import jax.numpy as jnp
import numpy as np
from jax import lax
from jax.experimental import pallas as pl
from jax.experimental.pallas import tpu as pltpu
from jax.sharding import PartitionSpec as P

ITERS = 3
NEAR, FAR, LEFT, RIGHT = range(4)
VMEM = pl.BlockSpec(memory_space=pltpu.VMEM)
SMEM = pl.BlockSpec(memory_space=pltpu.SMEM)
ANY = pl.BlockSpec(memory_space=pl.ANY)
HBM = pl.BlockSpec(memory_space=pltpu.HBM)
F32, BF16 = jnp.float32, jnp.bfloat16


def shifted(value, axis, steps, wrap):
    count = lax.axis_size(axis)
    if wrap:
        pairs = [(source, (source + steps) % count) for source in range(count)]
    else:
        pairs = [(source, source + steps) for source in range(count) if 0 <= source + steps < count]
    return lax.ppermute(value, axis, pairs)


def summed(value, axis):
    others = [shifted(value, axis, k, True) for k in range(1, lax.axis_size(axis))]
    return functools.reduce(jnp.add, others, value)


def chip_parts(value, axis):
    count, stride = lax.axis_size(axis) // 2, 1
    parts = [value]
    while stride < count:
        radix = next((r for r in range(8, 1, -1) if (count // stride) % r == 0), count // stride)
        value = parts[0] if len(parts) == 1 else jnp.concatenate(parts, axis=0)
        parts = [value] + [shifted(value, axis, 2 * k * stride, True) for k in range(1, radix)]
        stride *= radix
    return parts


def chip_neighbour(value, axis, back_only):
    count = lax.axis_size(axis)
    sources = range(0, count, 2 if back_only else 1)
    pairs = [(source, (source + (1 if source % 2 else -1)) % count) for source in sources]
    return lax.ppermute(value, axis, pairs)


def swapped(value, axis):
    return lax.ppermute(value, axis, [(source, source ^ 1) for source in range(lax.axis_size(axis))])


def halves(value):
    high = value.astype(BF16)
    return high, (value - high.astype(F32)).astype(BF16)


def dot(first, second):
    return lax.dot_general(first, second, (((1,), (0,)), ((), ())), preferred_element_type=F32)


def rotated(buffer, value, start):
    size = value.shape[0]
    buffer[0:size] = value
    buffer[size:] = value
    return buffer[pl.ds(start, size)]


def put_coupling(ref, size, face, amount):
    for i in range(size // 128):
        rows = size + 16 * i
        ref[rows:rows + 12] = face[:, i * 128:(i + 1) * 128]
        ref[rows + 12:rows + 16] = jnp.full((4, 128), amount, F32)


def got_coupling(ref, size):
    return jnp.concatenate([ref[size + 16 * i:size + 16 * i + 12] for i in range(size // 128)], axis=1)


def prepare_kernel(cuts, at, *refs):
    sources, outs, buffer = refs[0:5], refs[5:13], refs[13]
    held, sems, wide = refs[14:19], refs[19], refs[20]
    residual, to_far, to_right, inner, c_rows, c_keep, corner, own_offsets = outs
    offsets, corner_map, gap, coupling, corner_rows = held
    copies = [pltpu.make_async_copy(source, to, sems.at[i]) for i, (source, to) in enumerate(zip(sources, held))]
    for copy in copies:
        copy.start()
    for copy in copies:
        copy.wait()
    count, _, size, _ = gap.shape
    for s in range(count):
        for f in range(4):
            c_keep[s, :, f * size:(f + 1) * size] = coupling[:, s, f * size:(f + 1) * size]
    for s in range(count):
        for face in range(2):
            shift = offsets[s, face]
            value = gap[s, face] * (shift >= 0).astype(F32)
            residual[s, face] = value
            turned = -rotated(buffer.at[s, face], value, jnp.maximum(shift, 0))
            amount = (shift + 1).astype(F32)
            if face == 0:
                to_far[s, 0:size] = turned
                put_coupling(to_far.at[s], size, c_keep[s, :, FAR * size:(FAR + 1) * size], amount)
            elif s == count - 1:
                to_right[0:size] = turned
                put_coupling(to_right, size, c_keep[s, :, RIGHT * size:(RIGHT + 1) * size], amount)
            else:
                inner[s] = turned
    width = wide.shape[1] // 2
    wide[...] = jnp.zeros_like(wide)
    for a in range(cuts):

        @pl.when(at[0] == a)
        def _():
            for s in range(count):
                for k in range(4):
                    to = (k % 2) * width + 3 * (a - 1 + k // 2)
                    if a - 1 + k // 2 >= 0:
                        wide[s, to:to + 3] = c_keep[s, 3 * k:3 * k + 3]

    for s in range(count):
        c_rows[s, 0:2 * width], c_rows[s, 2 * width:] = halves(wide[s])
    inner[count - 1] = jnp.zeros(inner.shape[1:], F32)
    corner[...] = jnp.zeros_like(corner)
    dofs, rows = corner_rows.shape[2], 3 * cuts
    lanes = dofs // 128 + 1
    lane = lax.broadcasted_iota(jnp.int32, (3, 128), 1)
    row = lax.broadcasted_iota(jnp.int32, (3, 128), 0)
    for s in range(count):
        number = (3 * corner_map[s, 2] + 1 + row).astype(F32)
        for i in range(lanes):
            wide = min(128, dofs - 128 * i)
            for a in range(cuts):
                keep = (at[0] == a).astype(F32)
                first = (s * lanes + i) * rows + 3 * a
                if wide > 0:
                    corner[first:first + 3, 0:wide] = corner_rows[6:9, s, 128 * i:128 * i + wide] * keep
                if i == lanes - 1:
                    before = corner[first:first + 3]
                    corner[first:first + 3] = jnp.where(lane == dofs % 128, number * keep, before)
    for s in range(count):
        for face in range(2):
            own_offsets[s, face] = offsets[s, face]


def matrix_kernel(cuts, dofs, height, count, chips, stride, mine, theirs, k_high, k_low, rows, pick):
    used, lanes = 3 * cuts, dofs // 128 + 1
    rows[...] = jnp.zeros_like(rows)
    for i, source in enumerate((mine, theirs)):
        for k in range(chips):
            for s in range(count):
                to = ((i * chips + k) * count + s) * height
                for l in range(lanes):
                    first = k * stride + (count + 1) * height + (s * lanes + l) * used
                    rows[to:to + used, 128 * l:128 * (l + 1)] = source[first:first + used]
    lane = lax.broadcasted_iota(jnp.int32, pick.shape, 1)
    number = rows[:, dofs:dofs + 1].astype(jnp.int32)
    pick[...] = jnp.where(lane + 1 == number, 1.0, 0.0).astype(BF16)
    tile = 256 if rows.shape[0] % 256 == 0 else rows.shape[0]

    @pl.loop(0, rows.shape[0] // tile)
    def _(t):
        at = pl.ds(pl.multiple_of(t * tile, tile), tile)
        for half, out in zip(halves(rows[at]), (k_high, k_low)):
            product = lax.dot_general(half, pick[...], (((1,), (1,)), ((), ())), preferred_element_type=F32)
            out[at] = product.astype(BF16)


def paired(face):
    high, low = halves(face)
    rest = jnp.zeros((4, face.shape[1]), F32)
    both = jnp.concatenate([high.astype(F32), rest, low.astype(F32), rest], axis=0)
    return both.astype(BF16)


def turned(face, table):
    product = lax.dot_general(paired(face), table, (((0,), (0,)), ((), ())), preferred_element_type=F32)
    return product.astype(BF16)


def spread_kernel(at, own_offsets, coupling, from_near, from_left, table, ct_own, ct_left, offsets):
    count, size = coupling.shape[0], coupling.shape[2] // 4
    for s in range(count):
        ct_own[s, 0:4 * size] = turned(coupling[s], table[at[0] + 1])
        ct_own[s, 4 * size:5 * size] = turned(got_coupling(from_near.at[s], size), table[at[0]])
    ct_left[...] = turned(got_coupling(from_left, size), table[at[0] + 1])
    noted = lambda ref: jnp.max(ref[size + 12:size + 16]).astype(jnp.int32) - 1
    for s in range(count):
        offsets[s, NEAR] = noted(from_near.at[s])
        offsets[s, FAR] = own_offsets[s, 0]
        offsets[s, LEFT] = noted(from_left) if s == 0 else own_offsets[s - 1, 1]
        offsets[s, RIGHT] = own_offsets[s, 1]


def spread_back_kernel(stacked, at, side, from_far, across, theirs, table, ct_far, ct_right):
    count, size = ct_far.shape[0], ct_far.shape[1]
    for s in range(count):
        ct_far[s] = turned(got_coupling(from_far.at[s], size), table[at[0] + 2])
    inside = got_coupling(theirs.at[stacked:], size)
    ct_right[...] = turned(jnp.where(side[0] == 1, got_coupling(across, size), inside), table[at[0] + 1])


def beside(value):
    return jnp.concatenate(halves(value), axis=1)


def three_passes(first, second):
    high, low = halves(first)
    both = dot(high, second)
    return both[:, 0:128] + both[:, 128:256] + dot(low, second[:, 0:128])


def own_kernel(residual, flexibility, product):
    count, size = residual.shape[0], residual.shape[2]
    for s in range(count):
        total = None
        for i, face in enumerate((FAR, RIGHT)):
            part = three_passes(flexibility[s, :, face * size:(face + 1) * size], beside(residual[s, i]))
            total = part if total is None else total + part
        product[s] = total


def sum_kernel(parts, *refs):
    refs[parts + (len(refs) - parts - 1) // 2][...] = functools.reduce(jnp.add, [r[...] for r in refs[:parts]])


def stack_kernel(parts, *refs):
    out = refs[parts + (len(refs) - parts - 1) // 2]
    at = 0
    for ref in refs[:parts]:
        out[at:at + ref.shape[0]] = ref[...]
        at += ref.shape[0]


def room(*shapes):
    total = 0
    for x in shapes:
        dims = (1, 1, *x.shape)
        total += int(np.prod(dims[:-2])) * -(-dims[-2] // 16) * 16 * -(-dims[-1] // 128) * 128 * np.dtype(x.dtype).itemsize
    return pltpu.CompilerParams(vmem_limit_bytes=total + 2 * 1024 * 1024)


def relay(kernel, parts, shape, through, name):
    specs = [VMEM] * len(parts) + [ANY] * len(through)
    return pl.pallas_call(
        functools.partial(kernel, len(parts)),
        out_shape=(jax.ShapeDtypeStruct(shape.shape, shape.dtype), *[jax.ShapeDtypeStruct(x.shape, x.dtype) for x in through]),
        in_specs=specs,
        out_specs=(VMEM, *[ANY] * len(through)),
        compiler_params=room(*parts, shape),
        input_output_aliases={len(parts) + i: 1 + i for i in range(len(through))},
        name=name,
    )(*parts, *through)


def apply_flexibility(loads, side, flexibility, known, coupling, height, outs, split, rr_rows):
    near, far, sides, inside, across, terms = outs
    odd = side[0] == 1
    count, size = len(loads), loads[0][0].shape[0]
    for s in range(count):
        for face in range(4):
            high, low = halves(loads[s][face])
            split[s, face * size:(face + 1) * size, 0:128] = high
            split[s, face * size:(face + 1) * size, 128:256] = low
    terms[0:(count + 1) * height] = jnp.zeros(((count + 1) * height, 128), F32)
    total = jnp.zeros((1, 128), F32)
    width = coupling.shape[1] // 2
    for s in range(count):
        both = dot(coupling[s], split[s])
        mine = both[0:width, 0:128] + both[0:width, 128:256] + both[width:, 0:128]
        terms[s * height:s * height + width] += mine
    for s in range(count):
        if known is None:
            whole = three_passes(flexibility[s], split[s])
        else:
            whole = known[s]
            for face in (NEAR, LEFT):
                part = slice(face * size, (face + 1) * size)
                whole = whole + three_passes(flexibility[s, :, part], split[s, part])
        for face in range(4):
            product = whole[face * size:(face + 1) * size]
            total = total + jnp.sum(product * loads[s][face], axis=0, keepdims=True)
            if face == NEAR:
                near[s, 0:size] = product
            elif face == FAR:
                far[s] = product
            else:
                sides[s, face - 2] = product
    left, right = sides[0, 0], sides[count - 1, 1]
    inside[0:size] = jnp.where(odd, left, right)
    across[0:size] = jnp.where(odd, right, left)
    squares = jnp.zeros((1, 128), F32)
    for s in range(count):
        for face in (FAR, RIGHT):
            squares = squares + jnp.sum(loads[s][face] * loads[s][face], axis=0, keepdims=True)
    terms[rr_rows:rr_rows + 1] = squares
    terms[rr_rows + 1:rr_rows + 2] = total


def finish_operator(offsets, terms, matrix, spread, product, received, height, rr_rows, scratch, faces):
    k_high, k_low = matrix
    ct_own, ct_far, ct_left, ct_right = spread
    near, far, sides = product
    from_near, from_far, across = received
    count, size = far.shape[0], far.shape[1]
    side, mine, theirs = terms
    odd = side[0] == 1
    stacked, table = scratch["stack"], scratch["values"]
    span = count * height
    chips, stride = scratch["chips"], scratch["stride"]
    inside, across = theirs[chips * stride:chips * stride + size], across[0:size]
    from_left, from_right = jnp.where(odd, inside, across), jnp.where(odd, across, inside)
    terms = [x[k * stride:k * stride + span + height] for x in (mine, theirs) for k in range(chips)]
    norm = functools.reduce(jnp.add, [t[rr_rows:rr_rows + 1] for t in terms])
    energy = functools.reduce(jnp.add, [t[rr_rows + 1:rr_rows + 2] for t in terms])
    for k in range(2 * chips):
        chip, swap = k % chips, k // chips
        near_by = terms[chip + (1 - swap) * chips][span:span + height]
        farther = terms[(chip + 1) % chips + (1 - swap) * chips][span:span + height]
        stacked[k * span:(k + 1) * span] = terms[k][0:span]
        if swap == 0:
            extra = jnp.where(odd, near_by, farther)
        else:
            extra = jnp.where(odd, farther, near_by)
        stacked[k * span:k * span + height] = terms[k][0:height] + extra
    coarse = stacked[...]
    high, low = halves(coarse)
    both = dot(k_high[...], jnp.concatenate([high, low], axis=1))
    values = both[:, 0:128] + both[:, 128:256] + dot(k_low[...], high)
    energy = energy + jnp.sum(coarse * values, axis=0, keepdims=True)

    table[...] = values

    def column(q):
        along = side[0] + q // count
        block = (-(along // 2)) % chips + jnp.where(along % 2 == side[0], 0, chips)
        at = block * span + (q % count) * height
        return table[pl.ds(pl.multiple_of(at, 8), height)]

    def tripled(q):
        high, low = halves(jnp.concatenate([column(q), column(q + 1)], axis=0))
        return jnp.concatenate([high, high, low], axis=0)

    own = [[None] * 4 for _ in range(count)]
    other = [[None] * 4 for _ in range(count)]
    for s in range(count):
        columns = tripled(s)
        added = dot(ct_own[s], columns)
        parts = [added[i * size:(i + 1) * size] for i in range(5)]
        raw = [near[s, 0:size], far[s], sides[s, 0], sides[s, 1]]
        own[s] = [raw[i] + parts[i] for i in range(4)]
        other[s][FAR] = from_far[s, 0:size] + dot(ct_far[s], columns)
        if NEAR in faces:
            other[s][NEAR] = from_near[s] + parts[4]
    other[count - 1][RIGHT] = from_right + dot(ct_right[...], tripled(count))
    if LEFT in faces:
        other[0][LEFT] = from_left + dot(ct_left[...], tripled(-1))
    for s in range(count):
        if s + 1 < count:
            other[s][RIGHT] = own[s + 1][LEFT]
        if s > 0:
            other[s][LEFT] = own[s - 1][RIGHT]
    result = [[None] * 4 for _ in range(count)]
    for s in range(count):
        for face in faces:
            shift = offsets[s, face]
            safe = jnp.maximum(shift, 0)
            start = safe if face in (NEAR, LEFT) else size - safe
            turned = rotated(scratch["turn"].at[s, face], other[s][face], start)
            result[s][face] = (own[s][face] - turned) * (shift >= 0).astype(F32)
    return result, norm, energy


def first_kernel(
    height, rr_rows, side, residual, from_near, from_left, inner, coupling, corner, known, flexibility, c_rows, *rest
):
    outs, loads_out, split = rest[0:6], rest[6], rest[7]
    near, inside, across, terms = outs[0], outs[3], outs[4], outs[5]
    count, size = residual.shape[0], residual.shape[2]
    loads = []
    for s in range(count):
        left = from_left[0:size] if s == 0 else inner[s - 1]
        loads.append([from_near[s, 0:size], residual[s, 0], left, residual[s, 1]])
        for face in range(4):
            loads_out[s, face] = loads[s][face]
        put_coupling(near.at[s], size, coupling[s, :, NEAR * size:(NEAR + 1) * size], 0.0)
    for ref in (inside, across):
        put_coupling(ref, size, coupling[0, :, LEFT * size:(LEFT + 1) * size], 0.0)
    apply_flexibility(loads, side, flexibility, known, c_rows, height, outs, split, rr_rows)
    terms[(count + 1) * height:] = corner[...]


def step_kernel(which, chips, stride, height, rr_rows, *refs):
    refs = list(refs)
    take = lambda number: [refs.pop(0) for _ in range(number)]
    last = which == ITERS - 1
    (offsets,) = take(1)
    terms = take(3)
    matrix, spread, product, received = take(2), take(4), take(3), take(3)
    (loads,) = take(1)
    map_before, ways, found, scalars = (take(4) if which > 0 else [None] * 4)
    if not last:
        flexibility, coupling = take(2)
        outs = take(6)
        loads_out, map_out = take(2)
        ways_out, found_out = take(2) if which > 0 else (None, None)
        (scalars_out,) = take(1)
        stack, values, turn, split = take(4)
        faces = (NEAR, FAR, LEFT, RIGHT)
    else:
        found_out, residual_out = take(2)
        stack, values, turn = take(3)
        faces = (FAR, RIGHT)
    count, size = loads.shape[0], loads.shape[2]
    scratch = dict(stack=stack, values=values, turn=turn, chips=chips, stride=stride)
    mapped, norm, energy = finish_operator(
        offsets, terms, matrix, spread, product, received, height, rr_rows, scratch, faces
    )
    if which > 0:
        ratio = norm / scalars[0:1]
        energy = energy - ratio * norm / scalars[1:2]
    step = norm / energy
    fresh = [[None] * 4 for _ in range(count)]
    for s in range(count):
        for face in faces:
            here = mapped[s][face]
            now = loads[s, face]
            if which > 0:
                here = here + ratio * map_before[s, face]
            fresh[s][face] = now - step * here
            if not last:
                map_out[s, face] = here
                loads_out[s, face] = fresh[s][face]
            if face in (FAR, RIGHT):
                i = 0 if face == FAR else 1
                if which == 0:
                    continue
                if which == 1:
                    before = ways[s, face]
                    start = scalars[1:2] * before
                else:
                    before = ways[s, i]
                    start = found[s, i]
                way = now + ratio * before
                found_out[s, i] = start + step * way
                if last:
                    residual_out[s, i] = fresh[s][face]
                else:
                    ways_out[s, i] = way
    if not last:
        scalars_out[...] = jnp.concatenate([norm, step, jnp.zeros((6, 128), F32)], axis=0)
        apply_flexibility(fresh, terms[0], flexibility, None, coupling, height, outs, split, rr_rows)


def corner_tables(cuts, height):
    places = np.zeros((cuts + 2, 12, 2 * height), np.float32)
    for at in range(-1, cuts + 1):
        for k in range(4):
            cycle = at - 1 + k // 2
            if 0 <= cycle < cuts:
                for j in range(3):
                    places[at + 1, 3 * k + j, (k % 2) * height + 3 * cycle + j] = 1
    wide = 2 * height
    table = np.zeros((cuts + 2, 32, 3 * wide), np.float32)
    table[:, 0:12, 0:wide] = table[:, 16:28, wide:2 * wide] = table[:, 0:12, 2 * wide:] = places
    return jnp.asarray(table, BF16)


def per_device(gap_load, offsets, corner_map, flexibility, coupling, corner_rows):
    _, count, _, size, loads_n = gap_load.shape
    dofs = corner_rows.shape[-1]
    cuts, blocks = lax.axis_size("cuts"), lax.axis_size("blk")
    at = lax.axis_index("cuts").reshape(1)
    side = (lax.axis_index("blk") % 2).reshape(1)
    rr_rows = 3 * cuts
    height = -(-(rr_rows + 2) // 8) * 8
    gap, offsets, corner_map, flexibility, coupling, corner_rows = (
        x[0] for x in (gap_load, offsets, corner_map, flexibility, coupling, corner_rows)
    )
    total = flexibility.shape[1]
    below = 16 * (size // 128)
    shape = lambda *dims, kind=F32: jax.ShapeDtypeStruct(dims, kind)
    face = shape(size, loads_n)
    faces = shape(count, size, loads_n)
    pair = shape(count, 2, size, loads_n)
    four = shape(count, 4, size, loads_n)
    long_face = shape(size + below, loads_n)
    long_faces = shape(count, size + below, loads_n)
    table = corner_tables(cuts, height)

    corner_size = -(-(count * (dofs // 128 + 1) * rr_rows) // 8) * 8
    corner_shape = shape(corner_size, loads_n)
    wide = shape(count, rr_rows, total)
    held = [
        pltpu.SMEM(offsets.shape, jnp.int32),
        pltpu.SMEM(corner_map.shape, jnp.int32),
        pltpu.VMEM(gap.shape, F32),
        pltpu.VMEM((12, count, total), F32),
        pltpu.VMEM((12, count, dofs), F32),
    ]
    prepared = (pair, long_faces, long_face, faces, shape(count, 4 * height, total, kind=BF16), shape(count, 12, total),
                corner_shape)
    residual, to_far, to_right, inner, c_rows, c_keep, corner, own_offsets = pl.pallas_call(
        functools.partial(prepare_kernel, cuts),
        out_shape=prepared + (shape(count, 2, kind=jnp.int32),),
        in_specs=[SMEM] + [HBM] * 5,
        out_specs=(VMEM,) * 7 + (SMEM,),
        scratch_shapes=[pltpu.VMEM((count, 2, 2 * size, loads_n), F32), *held, pltpu.SemaphoreType.DMA((5,)),
                        pltpu.VMEM((count, 2 * height, total), F32)],
        compiler_params=room(*prepared, pair, pair, *held[2:], shape(count, 2 * height, total)),
        name="prepare",
    )(at, offsets, corner_map, gap, jnp.swapaxes(coupling, 0, 1), jnp.swapaxes(corner_rows, 0, 1))
    from_near = shifted(to_far, "cuts", 1, False)
    from_left = shifted(to_right, "blk", 1, True)
    ct_own, ct_left, all_offsets = pl.pallas_call(
        spread_kernel,
        out_shape=(
            shape(count, 5 * size, 6 * height, kind=BF16),
            shape(size, 6 * height, kind=BF16),
            shape(count, 4, kind=jnp.int32),
        ),
        in_specs=[SMEM] * 2 + [VMEM] * 4,
        out_specs=(VMEM, VMEM, SMEM),
        compiler_params=room(c_keep, from_near, from_left, table, *[faces] * 4),
        name="spread",
    )(at, own_offsets, c_keep, from_near, from_left, table)
    own_shape = shape(count, total, loads_n)
    own_part = pl.pallas_call(
        own_kernel,
        out_shape=own_shape,
        in_specs=[VMEM] * 2,
        out_specs=VMEM,
        compiler_params=room(residual, flexibility, flexibility, own_shape),
        cost_estimate=pl.CostEstimate(
            flops=3 * count * total * total * loads_n, bytes_accessed=4 * flexibility.size, transcendentals=0
        ),
        name="own",
    )(residual, flexibility)

    flops = 2 * count * total * total * loads_n * 3
    cost = pl.CostEstimate(flops=flops, bytes_accessed=4 * flexibility.size, transcendentals=0)
    terms_shape = shape((count + 1) * height, loads_n)
    sends = (faces, faces, pair, face, face, terms_shape)
    first_terms = shape((count + 1) * height + corner_size, loads_n)
    first_sends = (long_faces, faces, pair, long_face, long_face, first_terms)
    a_buffers = [pltpu.VMEM((count, total, 2 * loads_n), BF16)]
    f_buffers = [
        pltpu.VMEM((blocks * count * height, loads_n), F32),
        pltpu.VMEM((blocks * count * height, loads_n), F32),
        pltpu.VMEM((count, 4, 2 * size, loads_n), F32),
    ]
    first_args = (side, residual, from_near, from_left, inner, c_keep, corner, own_part, flexibility, c_rows)
    *out, loads = pl.pallas_call(
        functools.partial(first_kernel, height, rr_rows),
        out_shape=first_sends + (four,),
        in_specs=[SMEM] + [VMEM] * 9,
        out_specs=(VMEM,) * 7,
        scratch_shapes=a_buffers,
        compiler_params=room(*first_args[1:], *first_sends, four, flexibility, *a_buffers),
        cost_estimate=cost,
        name="first",
    )(*first_args)

    state = []
    for which in range(ITERS):
        last = which == ITERS - 1
        near, far, sides, inside, across, terms = out
        pieces = [terms] + [shifted(terms, "cuts", k, True) for k in range(1, cuts)]
        terms, near, across = relay(sum_kernel, pieces, terms, [near, across], f"sum{which}")
        across = chip_neighbour(across, "blk", last)
        r_far = shifted(near, "cuts", -1, False)
        pieces = chip_parts(terms, "blk")
        stacked = blocks // 2 * terms.shape[0]
        mine, far, across, r_far = relay(
            stack_kernel, [*pieces, inside], shape(stacked + inside.shape[0], loads_n), [far, across, r_far],
            f"stack{which}",
        )
        r_near = far if last else shifted(far, "cuts", 1, False)
        theirs = swapped(mine, "blk")
        if which == 0:
            k_shape = shape(blocks * count * height, blocks * count * height, kind=BF16)
            held = [pltpu.VMEM((k_shape.shape[0], 128 * (dofs // 128 + 1)), kind) for kind in (F32, BF16)]
            k_high, k_low = pl.pallas_call(
                functools.partial(matrix_kernel, cuts, dofs, height, count, blocks // 2, terms.shape[0]),
                out_shape=(k_shape, k_shape),
                in_specs=[VMEM] * 2,
                out_specs=(VMEM,) * 2,
                scratch_shapes=held,
                compiler_params=room(mine, theirs, k_shape, k_shape, *held),
                name="matrix",
            )(mine, theirs)
            ct_far, ct_right = pl.pallas_call(
                functools.partial(spread_back_kernel, stacked),
                out_shape=(shape(count, size, 6 * height, kind=BF16), shape(size, 6 * height, kind=BF16)),
                in_specs=[SMEM] * 2 + [VMEM] * 4,
                out_specs=(VMEM,) * 2,
                compiler_params=room(r_far, across, theirs, table, *[faces] * 3),
                name="spread_back",
            )(at, side, r_far, across, theirs, table)
        args = [all_offsets, side, mine, theirs, k_high, k_low, ct_own, ct_far, ct_left, ct_right, near, far, sides,
                r_near, r_far, across, loads, *state]
        specs = [SMEM, SMEM] + [VMEM] * (len(args) - 2)
        if last:
            outs, scratch = (pair, pair), f_buffers
        else:
            args += [flexibility, c_rows]
            specs += [VMEM] * 2
            outs = sends + (four, four) + ((pair, pair) if which > 0 else ()) + (shape(8, loads_n),)
            scratch = f_buffers + a_buffers
        result = pl.pallas_call(
            functools.partial(step_kernel, which, blocks // 2, terms.shape[0], height, rr_rows),
            out_shape=outs,
            in_specs=specs,
            out_specs=(VMEM,) * len(outs),
            scratch_shapes=scratch,
            compiler_params=room(*args[2:], *outs, *scratch, *([] if last else [flexibility])),
            cost_estimate=None if last else cost,
            name=f"step{which}",
        )(*args)
        if last:
            multipliers, residual = result
            break
        out = result[0:6]
        before, loads = loads, result[6]
        if which == 0:
            state = [result[7], before, before, result[8]]
        else:
            state = [result[7], result[8], result[9], result[10]]
    return multipliers[None], residual[None]


def solution(mesh):
    spec5, spec4, spec3 = (P("cuts", "blk", *[None] * k) for k in (3, 2, 1))
    return jax.shard_map(
        per_device,
        mesh=mesh,
        in_specs=(spec5, spec3, spec3, spec4, spec4, spec4),
        out_specs=(spec5, spec5),
        check_vma=False,
    )
```
